32 devices in a mesh: expert: 8 (over y, x, core), tensor: 4 (over z).
Axes of the slice: x: 2, y: 2, z: 4, core: 2. Of those that a mesh axis runs over, the one named last changes fastest.
Arguments:
- tokens: bfloat16 [4096, 1024], P('expert'), may hold values from -6 to 6
- norm1_gain: float32 [1024], replicated, may hold values from 0.5 to 1.5
- w_query: bfloat16 [1024, 1024], P(None, 'tensor'), may hold values from -0.1875 to 0.1875
- key_projection_weight: bfloat16 [1024, 512], P(None, 'tensor'), may hold values from -0.1875 to 0.1875
- value_projection_weight: bfloat16 [1024, 512], P(None, 'tensor'), may hold values from -0.1875 to 0.1875
- w_output: bfloat16 [1024, 1024], P('tensor'), may hold values from -1.5 to 1.5
- norm2_gain: float32 [1024], replicated, may hold values from 0.5 to 1.5
- w_router: bfloat16 [1024, 32], replicated, may hold values from -0.09375 to 0.09375
- expert_gate_weight: bfloat16 [32, 1024, 512], P('expert', None, 'tensor'), may hold values from -0.1875 to 0.1875
- expert_up_weight: bfloat16 [32, 1024, 512], P('expert', None, 'tensor'), may hold values from -0.1875 to 0.1875
- expert_down_weight: bfloat16 [32, 512, 1024], P('expert', 'tensor'), may hold values from -0.75 to 0.75
- expert_ids: int32 [4096, 8], P('expert'), may hold values from 0 to 31, all different within a row; in each aligned block of 512 rows (0 to 511, 512 to 1023, ...) at most 160 rows name the same one
- cotangent: bfloat16 [4096, 1024], P('expert'), may hold values from -6 to 6
Outputs:
- mixed: bfloat16 [4096, 1024], P('expert', 'tensor')
- grad_input: float32 [4096, 1024], P('expert')
- grad_norm1: float32 [1024], replicated
- grad_query: float32 [1024, 1024], P(None, 'tensor')
- grad_key: float32 [1024, 512], P(None, 'tensor')
- grad_value: float32 [1024, 512], P(None, 'tensor')
- grad_output: float32 [1024, 1024], P('tensor')
- grad_norm2: float32 [1024], replicated
- grad_router: float32 [1024, 32], replicated
- grad_gate: float32 [32, 1024, 512], P('expert', None, 'tensor')
- up_weight_gradient: float32 [32, 1024, 512], P('expert', None, 'tensor')
- grad_down: float32 [32, 512, 1024], P('expert', 'tensor')
The draws below stay inside these ranges and needn't reach their ends.
Inputs may be any that keep to these rules, and one draw needn't show every extreme that they name: `expert_ids`: within the rows of one index of expert (512 tokens), no expert is named more than 160 times, a bound that some block reaches.
All inputs are finite; a program needn't handle non-finite values.
Results may differ from the reference program's by a relative error of at most 0.023.
Values may be sent and summed in bfloat16 or wider, within the bound.
No kernel may reach another device: no remote copies, remote signals or barrier semaphores. Data moves between devices by JAX's collectives and lax.ppermute only.
A program may use at most 192 MiB of HBM per device.

```python
import math
from functools import partial
import jax
import jax.numpy as jnp
import numpy as np
from jax import lax

MODEL_DIMENSION = 1024
QUERY_HEADS = 16
KEY_VALUE_HEADS = 8
HEAD_DIMENSION = 64
FF = 512
EXPERTS = 32
TOP = 8
SEQ_LEN = 512
TOK_DEV = 512
TOKENS = 4096
CAP = 160
N_EXPERT = 8


def levels(own_key, extent, cuts, smallest, largest):
    def one(axis_at, blocks):
        heights = jax.random.uniform(jax.random.fold_in(jax.random.fold_in(own_key, 6), axis_at), (blocks,), jnp.float32, smallest / len(cuts), largest / len(cuts))
        return jnp.repeat(jnp.exp(heights), extent[axis_at] // blocks).reshape((-1,) + (1,) * (len(extent) - axis_at - 1))

    factor_of = one(*cuts[0])
    for cut in cuts[1:]:
        factor_of = factor_of * one(*cut)
    return factor_of


def assign_block(key, own, number, rows, count, top, bound, slope):
    sequence = jax.random.permutation(key, count)
    heavy_load, ordinary = portions_of(count, rows * top, bound, slope, True), portions_of(count, rows * top, bound, slope, False)
    places = jnp.arange(count)

    def named(sizes, rotation):
        used = int((sizes > 0).sum())
        fixed = max(1, used // 4)
        moved = fixed + (places - fixed + rotation * (used - fixed)) % max(1, count - fixed)
        return jnp.zeros((count,), jnp.int32).at[sequence[jnp.where(places < fixed, places, moved)]].set(jnp.asarray(sizes, jnp.int32))

    sizes = jnp.where(number % 4 == 0, named(heavy_load, number // 4), named(ordinary, number - number // 4 - 1))
    mixed = jax.random.permutation(jax.random.fold_in(own, 3), count)
    source_of, sink = mixed[0:count // 2 * 2:2], mixed[1:count // 2 * 2:2]
    slack = jnp.minimum(sizes[source_of] - 1, bound - sizes[sink]) // 2
    slack = jnp.where((source_of == sequence[0]) | (sink == sequence[0]) | (sizes[sink] == 0), 0, jnp.maximum(slack, 0))
    moved = jax.random.randint(jax.random.fold_in(own, 4), (count // 2,), 0, 1 << 20) % (slack + 1)
    sizes = sizes.at[source_of].add(-moved).at[sink].add(moved)
    members = jnp.searchsorted(jnp.cumsum(sizes), jnp.arange(rows * top), side="right").astype(jnp.int32)
    grid = members.reshape(top, rows).T
    grid = grid[jax.random.permutation(jax.random.fold_in(own, 1), rows)]
    rotation = jax.random.randint(jax.random.fold_in(own, 2), (rows, 1), 0, top)
    return jnp.take_along_axis(grid, (jnp.arange(top)[None, :] + rotation) % top, axis=1)


def portions_of(number_of, total, most, slope, full):
    portions = [(1 << 20) // math.isqrt(standing ** slope) + 1 for standing in range(1, number_of + 1)]
    largest = most if full else min(most, max(-(-total // number_of), total * portions[0] // sum(portions)))
    least = 1 if total - largest >= number_of - 1 else 0
    holding, rest = [largest] + [least] * (number_of - 1), total - largest - least * (number_of - 1)
    while rest > 0:
        free = [i for i in range(1, number_of) if holding[i] < largest] or [i for i in range(1, number_of) if holding[i] < most]
        whole, budget = sum([portions[i] for i in free]), rest
        for i in free:
            more = min(most - holding[i], max(1, budget * portions[i] // whole), rest)
            holding[i] = holding[i] + more
            rest = rest - more
    return np.array(holding)


def scatter_about(stream_key, dims, deviation, bound, split=(), kind=jnp.bfloat16):
    entries = jax.random.normal(stream_key, dims, jnp.float32) * deviation
    if len(split) > 0:
        entries = levels(stream_key, dims, split, -0.22, 0.18) * entries
    return jnp.clip(entries, min=-bound, max=bound).astype(kind)


def setup_inputs(seed: int = 0) -> dict:
    arg_keys = jax.random.split(jax.random.key(seed), 14)
    tokens = scatter_about(arg_keys[0], (TOKENS, MODEL_DIMENSION), 1.0, 6.0, ((0, 8),))
    norm1_gain = jnp.clip(1.0 + 0.1 * jax.random.normal(arg_keys[1], (MODEL_DIMENSION,), jnp.float32), 0.5, 1.5)
    w_query = scatter_about(arg_keys[2], (MODEL_DIMENSION, QUERY_HEADS * HEAD_DIMENSION), MODEL_DIMENSION ** -0.5, 0.1875, ((1, 4),))
    key_projection_weight = scatter_about(arg_keys[3], (MODEL_DIMENSION, KEY_VALUE_HEADS * HEAD_DIMENSION), MODEL_DIMENSION ** -0.5, 0.1875, ((1, 4),))
    value_projection_weight = scatter_about(arg_keys[4], (MODEL_DIMENSION, KEY_VALUE_HEADS * HEAD_DIMENSION), MODEL_DIMENSION ** -0.5, 0.1875, ((1, 4),))
    w_output = scatter_about(arg_keys[5], (QUERY_HEADS * HEAD_DIMENSION, MODEL_DIMENSION), (QUERY_HEADS * HEAD_DIMENSION // 64) ** -0.5, 1.5, ((0, 4),))
    norm2_gain = jnp.clip(1.0 + 0.1 * jax.random.normal(arg_keys[6], (MODEL_DIMENSION,), jnp.float32), 0.5, 1.5)
    w_router = scatter_about(arg_keys[7], (MODEL_DIMENSION, EXPERTS), (4 * MODEL_DIMENSION) ** -0.5, 0.09375)
    expert_gate_weight = scatter_about(arg_keys[8], (EXPERTS, MODEL_DIMENSION, FF), MODEL_DIMENSION ** -0.5, 0.1875, ((0, 8), (2, 4)))
    expert_up_weight = scatter_about(arg_keys[9], (EXPERTS, MODEL_DIMENSION, FF), MODEL_DIMENSION ** -0.5, 0.1875, ((0, 8), (2, 4)))
    expert_down_weight = scatter_about(arg_keys[10], (EXPERTS, FF, MODEL_DIMENSION), (FF // 8) ** -0.5, 0.75, ((0, 8), (1, 4)))
    expert_ids_keys = jax.random.split(jax.random.fold_in(arg_keys[11], 1), TOKENS // TOK_DEV)
    expert_ids_turns = jax.random.permutation(jax.random.fold_in(arg_keys[11], 3), TOKENS // TOK_DEV)
    expert_ids = jax.vmap(lambda own, number: assign_block(jax.random.fold_in(arg_keys[11], 2), own, number, TOK_DEV, EXPERTS, TOP, CAP, 1))(expert_ids_keys, expert_ids_turns).reshape((TOKENS, TOP))
    cotangent = scatter_about(arg_keys[12], (TOKENS, MODEL_DIMENSION), 1.0, 6.0, ((0, 8),))
    return dict(tokens=tokens, norm1_gain=norm1_gain, w_query=w_query, key_projection_weight=key_projection_weight, value_projection_weight=value_projection_weight, w_output=w_output, norm2_gain=norm2_gain, w_router=w_router, expert_gate_weight=expert_gate_weight, expert_up_weight=expert_up_weight, expert_down_weight=expert_down_weight, expert_ids=expert_ids, cotangent=cotangent)


EPS = 1e-06
SCALE = 0.125
NEGATIVE = -1e+30
THETA = 10000.0

@jax.custom_vjp
def low(v):
    return lax.optimization_barrier(v.astype(jnp.bfloat16)).astype(jnp.float32)

@jax.custom_vjp
def low_back(v):
    return v

def low_keep(v):
    return (low(v), None)

def low_pass(kept, grad):
    return (grad,)

def back_keep(v):
    return (v, None)

def back_low(kept, grad):
    return (low(grad),)
low.defvjp(low_keep, low_pass)
low_back.defvjp(back_keep, back_low)

def matrix_multiply(left, right):
    return jnp.dot(left, right, precision=lax.Precision.HIGHEST)

def normed(field, gain):
    return field * lax.rsqrt(lax.optimization_barrier(jnp.mean(field * field, axis=-1, keepdims=True)) + EPS) * gain

def rotated_pairs(field, sequence_length):
    half = HEAD_DIMENSION // 2
    freq = jnp.exp(-math.log(THETA) * jnp.arange(half, dtype=jnp.float32) / half)
    angle = jnp.arange(sequence_length, dtype=jnp.float32)[:, None] * freq[None, :]
    cosine = jnp.cos(angle)[:, None, :]
    sine_table = jnp.sin(angle)[:, None, :]
    first = field[..., :half]
    second = field[..., half:]
    return jnp.concatenate([first * cosine - second * sine_table, second * cosine + first * sine_table], axis=-1)

def attend_sequence(normalized_input, query_w, key_matrix, value_matrix):
    sequence_length = normalized_input.shape[0]
    query_rows = low(rotated_pairs(low_back(matrix_multiply(normalized_input, query_w)).reshape(sequence_length, QUERY_HEADS, HEAD_DIMENSION), sequence_length))
    rotated_keys = low(rotated_pairs(low_back(matrix_multiply(normalized_input, key_matrix)).reshape(sequence_length, KEY_VALUE_HEADS, HEAD_DIMENSION), sequence_length))
    value_rows = low(low_back(matrix_multiply(normalized_input, value_matrix))).reshape(sequence_length, KEY_VALUE_HEADS, HEAD_DIMENSION)
    query_rows = query_rows.reshape(sequence_length, KEY_VALUE_HEADS, QUERY_HEADS // KEY_VALUE_HEADS, HEAD_DIMENSION)
    scores = low_back(jnp.einsum('lkgd,mkd->kglm', query_rows, rotated_keys, precision=lax.Precision.HIGHEST) * SCALE)
    places = jnp.arange(sequence_length)
    causal = places[:, None] >= places[None, :]
    probability = low(jax.nn.softmax(jnp.where(causal, scores, NEGATIVE), axis=-1))
    heads_out = jnp.einsum('kglm,mkd->lkgd', probability, value_rows, precision=lax.Precision.HIGHEST)
    return low_back(low(heads_out.reshape(sequence_length, QUERY_HEADS * HEAD_DIMENSION)))

def expert_rows(parts, source):
    gate_e, up_e, down_e, index_rows = parts
    rows_in = low_back(source[index_rows])
    gate_activation = low_back(matrix_multiply(rows_in, gate_e))
    up_activation = low_back(matrix_multiply(rows_in, up_e))
    inner_activation = low(jax.nn.silu(gate_activation) * up_activation)
    return low_back(low(matrix_multiply(inner_activation, down_e)))

def reference(tokens, norm1_gain, w_query, key_projection_weight, value_projection_weight, w_output, norm2_gain, w_router, expert_gate_weight, expert_up_weight, expert_down_weight, expert_ids, cotangent):
    blocks = expert_ids.reshape(N_EXPERT, TOK_DEV * TOP)
    one_hot = (blocks[:, :, None] == jnp.arange(EXPERTS, dtype=jnp.int32)[None, None, :]).astype(jnp.int32)
    before = jnp.cumsum(one_hot, axis=1) - one_hot
    slot_index = lax.optimization_barrier(jnp.sum(before * one_hot, axis=-1))
    row_place = (jnp.arange(N_EXPERT, dtype=jnp.int32)[:, None] * CAP + slot_index).reshape(-1).astype(jnp.int32)
    flat_ids = expert_ids.reshape(-1).astype(jnp.int32)
    pair_token = (jnp.arange(TOKENS * TOP, dtype=jnp.int32) // TOP).astype(jnp.int32)
    table = jnp.full((EXPERTS, N_EXPERT * CAP), TOKENS, jnp.int32).at[flat_ids, row_place].set(pair_token)
    slot_place = (flat_ids * (N_EXPERT * CAP) + row_place).astype(jnp.int32)

    def forward(resid_in, gain_one, query_w, key_matrix, value_matrix, output_w, gain_two, router_w, gate_w, up_w, down_w):
        first_norm = low(normed(resid_in, gain_one))
        sequences = first_norm.reshape(TOKENS // SEQ_LEN, SEQ_LEN, MODEL_DIMENSION)
        attend = jax.checkpoint(partial(attend_sequence, query_w=query_w, key_matrix=key_matrix, value_matrix=value_matrix))
        attended = lax.map(attend, sequences).reshape(TOKENS, QUERY_HEADS * HEAD_DIMENSION)
        hidden = resid_in + low_back(matrix_multiply(attended, output_w))
        second_norm = low(normed(hidden, gain_two))
        logits = matrix_multiply(second_norm, router_w)
        chosen = jnp.take_along_axis(logits, expert_ids, axis=1)
        routing = jax.nn.softmax(chosen, axis=-1)
        source = jnp.concatenate([second_norm, jnp.zeros((1, MODEL_DIMENSION), jnp.float32)], axis=0)
        outputs = lax.map(jax.checkpoint(partial(expert_rows, source=source)), (gate_w, up_w, down_w, table))
        picked = outputs.reshape(-1, MODEL_DIMENSION)[slot_place].reshape(TOKENS, TOP, MODEL_DIMENSION)
        routed = lax.optimization_barrier(jnp.sum(routing[:, :, None] * picked, axis=1))
        return hidden + routed
    floats = (tokens.astype(jnp.float32), norm1_gain.astype(jnp.float32), w_query.astype(jnp.float32), key_projection_weight.astype(jnp.float32), value_projection_weight.astype(jnp.float32), w_output.astype(jnp.float32), norm2_gain.astype(jnp.float32), w_router.astype(jnp.float32), expert_gate_weight.astype(jnp.float32), expert_up_weight.astype(jnp.float32), expert_down_weight.astype(jnp.float32))
    result, pull = jax.vjp(forward, *floats)
    grads = pull(cotangent.astype(jnp.float32))
    return (result.astype(jnp.bfloat16), grads[0], grads[1], grads[2], grads[3], grads[4], grads[5], grads[6], grads[7], grads[8], grads[9], grads[10])
```

```python
import math

import jax
import jax.numpy as jnp
from jax import lax
from jax.sharding import PartitionSpec as P

HEAD_DIMENSION = 64
SEQ_LEN = 512

EPS = 1e-06
SCALE = 0.125
NEGATIVE = -1e30
THETA = 10000.0
F32 = jnp.float32
BF16 = jnp.bfloat16
EXACT = lax.Precision.HIGHEST


def tables(tok_count):
    half = HEAD_DIMENSION // 2
    freq = jnp.exp(-math.log(THETA) * jnp.arange(half, dtype=F32) / half)
    places = (jnp.arange(tok_count) % SEQ_LEN).astype(F32)
    angle = places[:, None] * freq[None, :]
    return (jnp.cos(angle)[:, None, :], jnp.sin(angle)[:, None, :])


def rotate(field, cosine, sine_table, factor):
    half = HEAD_DIMENSION // 2
    first = field[..., :half]
    second = field[..., half:]
    return jnp.concatenate(
        [
            first * cosine - factor * second * sine_table,
            second * cosine + factor * first * sine_table,
        ],
        axis=-1,
    )


def causal_mask():
    places = jnp.arange(SEQ_LEN)
    return places[:, None] >= places[None, :]


def attend_forward(query_rows, rotated_keys, value_rows):
    scores = (
        jnp.einsum("lkgd,mkd->kglm", query_rows, rotated_keys, preferred_element_type=F32) * SCALE
    )
    scores = jnp.where(causal_mask(), scores, NEGATIVE)
    highest = jnp.max(scores, axis=-1, keepdims=True)
    expanded = jnp.exp(scores - highest)
    summed = jnp.sum(expanded, axis=-1, keepdims=True)
    probability = (expanded / summed).astype(BF16)
    heads_out = jnp.einsum("kglm,mkd->lkgd", probability, value_rows, preferred_element_type=F32)
    return (heads_out.astype(BF16), (highest + jnp.log(summed))[..., 0])


def attend_backward(query_rows, rotated_keys, value_rows, grad_heads, log_total):
    scores = (
        jnp.einsum("lkgd,mkd->kglm", query_rows, rotated_keys, preferred_element_type=F32) * SCALE
    )
    probability = jnp.where(causal_mask(), jnp.exp(scores - log_total[..., None]), 0.0)
    prob_low = probability.astype(BF16)
    grad_values = jnp.einsum("kglm,lkgd->mkd", prob_low, grad_heads, preferred_element_type=F32)
    grad_prob = jnp.einsum("lkgd,mkd->kglm", grad_heads, value_rows, preferred_element_type=F32)
    row_delta = jnp.sum(probability * grad_prob, axis=-1, keepdims=True)
    grad_scores = (probability * (grad_prob - row_delta)).astype(BF16)
    grad_queries = (
        jnp.einsum("kglm,mkd->lkgd", grad_scores, rotated_keys, preferred_element_type=F32) * SCALE
    )
    grad_keys = (
        jnp.einsum("kglm,lkgd->mkd", grad_scores, query_rows, preferred_element_type=F32) * SCALE
    )
    return (grad_queries, grad_keys, grad_values)


def mm(left, right):
    return jnp.dot(left, right, preferred_element_type=F32)


def mm_rows(left, right):
    return lax.dot_general(left, right, (((0,), (0,)), ((), ())), preferred_element_type=F32)


def mm_cols(left, right):
    return lax.dot_general(left, right, (((1,), (1,)), ((), ())), preferred_element_type=F32)


def piece(array, index, size, axis=0):
    return lax.dynamic_slice_in_dim(array, index * size, size, axis)


def swap(array, mask):
    size = lax.axis_size("expert")
    return lax.ppermute(array, "expert", [(i, i ^ mask) for i in range(size)])


def z_shift(array, step):
    size = lax.axis_size("tensor")
    return lax.ppermute(array, "tensor", [(i, (i + step) % size) for i in range(size)])


def z_received(array):
    return [array] + [z_shift(array, step) for step in range(1, lax.axis_size("tensor"))]


def z_gather(array):
    size, mine = lax.axis_size("tensor"), lax.axis_index("tensor")
    rows = array.shape[0]
    whole = jnp.zeros((rows * size,) + array.shape[1:], array.dtype)
    for step, part in enumerate(z_received(array)):
        whole = lax.dynamic_update_slice_in_dim(whole, part, (mine + size - step) % size * rows, 0)
    return whole


def z_scatter(array, axis=0):
    size, mine = lax.axis_size("tensor"), lax.axis_index("tensor")
    width = array.shape[axis] // size
    total = piece(array, mine, width, axis).astype(F32)
    for step in range(1, size):
        sent = piece(array, (mine + step) % size, width, axis).astype(BF16)
        total = total + z_shift(sent, step).astype(F32)
    return total


def same_core_groups():
    size = lax.axis_size("expert")
    return [list(range(0, size, 2)), list(range(1, size, 2))]


def plane_gather(array):
    if lax.axis_size("expert") != 8:
        return [
            lax.all_gather(
                array, "expert", axis=0, tiled=True, axis_index_groups=same_core_groups()
            )
        ]
    half = array.shape[0] // 2
    from_x = swap(array, 2)
    from_y = swap(array, 4)
    diagonal = jnp.concatenate([swap(from_x[:half], 4), swap(from_y[half:], 2)])
    return [array, from_x, from_y, diagonal]


def plane_scatter(blocks):
    if lax.axis_size("expert") != 8:
        return lax.psum_scatter(
            blocks[0].astype(BF16),
            "expert",
            scatter_dimension=0,
            tiled=True,
            axis_index_groups=same_core_groups(),
        ).astype(F32)
    own, for_x, for_y, diagonal = blocks
    half = own.shape[0] // 2
    diagonal = diagonal.astype(BF16)
    via_x = swap(diagonal[:half], 2).astype(F32)
    via_y = swap(diagonal[half:], 4).astype(F32)
    for_y = jnp.concatenate([for_y[:half] + via_x, for_y[half:]]).astype(BF16)
    for_x = jnp.concatenate([for_x[:half], for_x[half:] + via_y]).astype(BF16)
    return own + swap(for_x, 2).astype(F32) + swap(for_y, 4).astype(F32)


def expert_sum(array):
    if lax.axis_size("expert") != 8:
        return lax.psum(array.astype(BF16), "expert").astype(F32)
    place = lax.axis_index("expert")
    core, chip = place % 2, place // 2
    half = array.shape[0] // 2
    rows = half // 4
    mine = piece(array, core, half) + swap(
        piece(array, 1 - core, half).astype(BF16), 1
    ).astype(F32)
    total = piece(mine, chip, rows)
    for mask in (1, 2, 3):
        total = total + swap(piece(mine, chip ^ mask, rows).astype(BF16), 2 * mask).astype(F32)
    total = total.astype(BF16)
    gathered = jnp.zeros((half,) + array.shape[1:], BF16)
    for mask in (0, 1, 2, 3):
        part = swap(total, 2 * mask) if mask else total
        gathered = lax.dynamic_update_slice_in_dim(gathered, part, (chip ^ mask) * rows, 0)
    both = jnp.concatenate([gathered, gathered])
    both = lax.dynamic_update_slice_in_dim(both, swap(gathered, 1), (1 - core) * half, 0)
    return both.astype(F32)


def small_sum(array, over_tensor):
    size = lax.axis_size("expert")
    if size & (size - 1):
        array = lax.psum(array, "expert")
    else:
        mask = 1
        while mask < size:
            array = array + swap(array, mask)
            mask *= 2
    if over_tensor:
        parts = z_received(array)
        array = parts[0]
        for part in parts[1:]:
            array = array + part
    return array


def norm_scale(field):
    return lax.rsqrt(jnp.mean(field * field, axis=-1, keepdims=True) + EPS)


def route(normed, router, chosen):
    logits = mm(normed, router)
    masked = jnp.where(chosen, logits, NEGATIVE)
    highest = jnp.max(masked, axis=-1, keepdims=True)
    expanded = jnp.where(chosen, jnp.exp(masked - highest), 0.0)
    return expanded / jnp.sum(expanded, axis=-1, keepdims=True)


def local(
    tokens,
    norm1_gain,
    w_query,
    key_projection_weight,
    value_projection_weight,
    w_output,
    norm2_gain,
    w_router,
    expert_gate_weight,
    expert_up_weight,
    expert_down_weight,
    expert_ids,
    cotangent,
):
    tok_count = tokens.shape[0]
    model_width = tokens.shape[1]
    experts = w_router.shape[1]
    here, units = expert_gate_weight.shape[0], expert_gate_weight.shape[2]
    heads_query = w_query.shape[1] // HEAD_DIMENSION
    heads_kv = key_projection_weight.shape[1] // HEAD_DIMENSION
    group_size = heads_query // heads_kv
    cosine, sine_table = tables(tok_count)
    expert_count = lax.axis_size("expert")
    tensor_count = lax.axis_size("tensor")
    expert_place = lax.axis_index("expert")
    tensor_place = lax.axis_index("tensor")
    core = expert_place % 2
    own_rows = tok_count // tensor_count
    col_width = model_width // tensor_count

    ids_blocks = plane_gather(expert_ids.T) if expert_count == 8 else [
        lax.all_gather(
            expert_ids, "expert", axis=0, tiled=True, axis_index_groups=same_core_groups()
        ).T
    ]
    grad_blocks = plane_gather(cotangent)

    def chip_weights(weight):
        other = swap(weight, 1)
        return jnp.concatenate([weight, other])

    def as_columns(weight):
        return weight.transpose(1, 0, 2).reshape(model_width, -1)

    gate_w = as_columns(chip_weights(expert_gate_weight))
    up_w = as_columns(chip_weights(expert_up_weight))
    down_w = chip_weights(expert_down_weight).reshape(-1, model_width)

    share = w_output.shape[0] // expert_count
    w_piece = piece(w_output, expert_place, share)
    w_pieces = jnp.stack([z_shift(w_piece, step) for step in range(1, tensor_count)])
    if expert_count == 8:
        w_other = swap(w_pieces, 1)
        w_pair = jnp.where(
            core == 0,
            jnp.concatenate([w_pieces, w_other], axis=1),
            jnp.concatenate([w_other, w_pieces], axis=1),
        )
        chip = expert_place // 2
        w_parts = jnp.zeros((tensor_count - 1,) + w_output.shape, BF16)
        w_x = swap(w_pair, 2)
        w_y = swap(w_pair, 4)
        w_d = jnp.concatenate([swap(w_x[:, :share], 4), swap(w_y[:, share:], 2)], axis=1)
        for mask, part in enumerate((w_pair, w_x, w_y, w_d)):
            w_parts = lax.dynamic_update_slice_in_dim(w_parts, part, (chip ^ mask) * 2 * share, 1)
    else:
        w_parts = lax.all_gather(w_pieces, "expert", axis=1, tiled=True)

    resid_in = tokens.astype(F32)
    first_scale = norm_scale(resid_in)
    first_norm = (resid_in * first_scale * norm1_gain).astype(BF16)
    query_raw = mm(first_norm, w_query).reshape(tok_count, heads_query, HEAD_DIMENSION)
    key_raw = mm(first_norm, key_projection_weight).reshape(tok_count, heads_kv, HEAD_DIMENSION)
    query_rows = (
        rotate(query_raw, cosine, sine_table, 1.0)
        .astype(BF16)
        .reshape(tok_count, heads_kv, group_size, HEAD_DIMENSION)
    )
    rotated_keys = rotate(key_raw, cosine, sine_table, 1.0).astype(BF16)
    value_rows = (
        mm(first_norm, value_projection_weight)
        .astype(BF16)
        .reshape(tok_count, heads_kv, HEAD_DIMENSION)
    )
    attended, log_total = attend_forward(query_rows, rotated_keys, value_rows)
    attended = attended.reshape(tok_count, heads_query * HEAD_DIMENSION)

    attended_parts = z_received(attended)
    hidden = resid_in + mm(attended, w_output)
    for step in range(1, tensor_count):
        hidden = hidden + mm(attended_parts[step], w_parts[step - 1])
    second_scale = norm_scale(hidden)
    second_norm = (hidden * second_scale * norm2_gain).astype(BF16)

    names = jnp.arange(experts, dtype=jnp.int32)
    first_here = expert_place * here
    first_other = (expert_place ^ 1) * here
    out_blocks, row_blocks, routing_blocks = [], [], []
    gate_total = up_total = down_total = 0.0
    for normed, grad, ids in zip(plane_gather(second_norm), grad_blocks, ids_blocks):
        rows = normed.shape[0]
        chosen = jnp.any(ids.T[:, :, None] == names[None, None, :], axis=1)
        routing = route(normed, w_router, chosen)
        weight = jnp.concatenate(
            [
                lax.dynamic_slice_in_dim(routing, first_here, here, 1),
                lax.dynamic_slice_in_dim(routing, first_other, here, 1),
            ],
            axis=1,
        )
        wide = jnp.repeat(weight, units, axis=1)
        gate_act = mm(normed, gate_w)
        up_act = mm(normed, up_w)
        grad_plain = mm_cols(grad, down_w)
        sigmoid_gate = jax.nn.sigmoid(gate_act)
        swish = gate_act * sigmoid_gate
        inner = swish * up_act
        grad_inner = grad_plain * wide
        routing_blocks.append(
            jnp.sum((inner * grad_plain).reshape(rows, 2 * here, units), axis=-1)
        )
        inner_low = (inner * wide).astype(BF16)
        gate_grad = (
            grad_inner * up_act * sigmoid_gate * (1.0 + gate_act * (1.0 - sigmoid_gate))
        ).astype(BF16)
        up_grad = (grad_inner * swish).astype(BF16)
        out_blocks.append(mm(inner_low, down_w))
        row_blocks.append(mm_cols(gate_grad, gate_w) + mm_cols(up_grad, up_w))
        gate_total = gate_total + mm_rows(normed, gate_grad)
        up_total = up_total + mm_rows(normed, up_grad)
        down_total = down_total + mm_rows(inner_low, grad)

    row_sum = z_scatter(plane_scatter(row_blocks))

    if expert_count == 8:
        grad_routing = jnp.zeros((experts, tok_count), F32)
        for mask, block in enumerate(routing_blocks):
            part = block.T
            part = swap(part, 2 * mask) if mask else part
            source = (expert_place ^ (2 * mask)) * here
            source_other = (expert_place ^ (2 * mask) ^ 1) * here
            grad_routing = lax.dynamic_update_slice_in_dim(grad_routing, part[:here], source, 0)
            grad_routing = lax.dynamic_update_slice_in_dim(
                grad_routing, part[here:], source_other, 0
            )
    else:
        block = routing_blocks[0]
        spread = jnp.zeros((block.shape[0], experts), F32)
        spread = lax.dynamic_update_slice_in_dim(spread, block[:, :here], first_here, 1)
        spread = lax.dynamic_update_slice_in_dim(spread, block[:, here:], first_other, 1)
        grad_routing = lax.psum_scatter(
            spread,
            "expert",
            scatter_dimension=0,
            tiled=True,
            axis_index_groups=same_core_groups(),
        ).T
    routing_parts = z_received(grad_routing)
    grad_routing = routing_parts[0]
    for part in routing_parts[1:]:
        grad_routing = grad_routing + part
    grad_routing = grad_routing.T
    own_chosen = jnp.any(expert_ids[:, :, None] == names[None, None, :], axis=1)
    own_routing = route(second_norm, w_router, own_chosen)
    grad_logits = own_routing * (
        grad_routing - jnp.sum(own_routing * grad_routing, axis=-1, keepdims=True)
    )

    def mine(array):
        return piece(array, tensor_place, own_rows)

    my_logits, my_hidden, my_scale = mine(grad_logits), mine(hidden), mine(second_scale)
    my_normed = mine(second_norm).astype(F32)
    router_float = w_router.astype(F32)
    grad_second = row_sum + jnp.dot(my_logits, router_float.T, precision=EXACT)
    grad_router = lax.dot_general(
        my_logits, my_normed, (((0,), (0,)), ((), ())), precision=EXACT
    )
    grad_norm2 = jnp.sum(grad_second * my_hidden * my_scale, axis=0)
    gained_two = grad_second * norm2_gain
    my_grad_hidden = (
        mine(cotangent).astype(F32)
        + my_scale * gained_two
        - my_hidden * my_scale**3 * jnp.mean(gained_two * my_hidden, axis=-1, keepdims=True)
    )
    grad_branch = z_gather(my_grad_hidden.astype(BF16))
    early = small_sum(jnp.concatenate([grad_router, grad_norm2[None]]), True)
    grad_output = expert_sum(mm_rows(attended, grad_branch))

    grad_heads = mm_cols(grad_branch, w_output).astype(BF16)
    grad_heads = grad_heads.reshape(tok_count, heads_kv, group_size, HEAD_DIMENSION)
    grad_queries, grad_keys, grad_values = attend_backward(
        query_rows, rotated_keys, value_rows, grad_heads, log_total
    )
    grad_query_raw = rotate(
        grad_queries.reshape(tok_count, heads_query, HEAD_DIMENSION), cosine, sine_table, -1.0
    )
    grad_query_raw = grad_query_raw.reshape(tok_count, -1).astype(BF16)
    grad_key_raw = rotate(grad_keys, cosine, sine_table, -1.0)
    grad_key_raw = grad_key_raw.reshape(tok_count, -1).astype(BF16)
    grad_value_raw = grad_values.reshape(tok_count, -1).astype(BF16)
    grad_raw = jnp.concatenate([grad_query_raw, grad_key_raw, grad_value_raw], axis=1)
    grad_weights = expert_sum(mm_rows(first_norm, grad_raw))
    q_width, k_width = w_query.shape[1], key_projection_weight.shape[1]
    grad_first = (
        mm_cols(grad_query_raw, w_query)
        + mm_cols(grad_key_raw, key_projection_weight)
        + mm_cols(grad_value_raw, value_projection_weight)
    )
    grad_first = z_scatter(grad_first)
    gained_one = grad_first * norm1_gain
    my_resid, my_first_scale = mine(resid_in), mine(first_scale)
    grad_norm1 = jnp.sum(grad_first * my_resid * my_first_scale, axis=0)
    my_grad_input = (
        my_grad_hidden
        + my_first_scale * gained_one
        - my_resid * my_first_scale**3 * jnp.mean(gained_one * my_resid, axis=-1, keepdims=True)
    )
    grad_input = z_gather(my_grad_input.astype(BF16)).astype(F32)
    grad_norm1 = small_sum(grad_norm1[None], True)[0]

    routed = z_scatter(plane_scatter(out_blocks), axis=1)
    mixed = (piece(hidden, tensor_place, col_width, 1) + routed).astype(BF16)

    width = here * units

    def from_chip(total):
        return total[:, :width] + swap(total[:, width:].astype(BF16), 1).astype(F32)

    def as_experts(total):
        return total.reshape(model_width, here, units).transpose(1, 0, 2)

    grad_gate = as_experts(from_chip(gate_total))
    up_weight_gradient = as_experts(from_chip(up_total))
    grad_down = down_total[:width] + swap(down_total[width:].astype(BF16), 1).astype(F32)
    grad_down = grad_down.reshape(here, units, model_width)
    return (
        mixed,
        grad_input,
        grad_norm1,
        grad_weights[:, :q_width],
        grad_weights[:, q_width : q_width + k_width],
        grad_weights[:, q_width + k_width :],
        grad_output,
        early[experts],
        early[:experts].T,
        grad_gate,
        up_weight_gradient,
        grad_down,
    )


def solution(mesh):
    placed = (
        P("expert", None),
        P(),
        P(None, "tensor"),
        P(None, "tensor"),
        P(None, "tensor"),
        P("tensor", None),
        P(),
        P(),
        P("expert", None, "tensor"),
        P("expert", None, "tensor"),
        P("expert", "tensor", None),
        P("expert", None),
        P("expert", None),
    )
    return jax.shard_map(
        local,
        mesh=mesh,
        in_specs=placed,
        out_specs=(
            P("expert", "tensor"),
            P("expert", None),
            P(),
            P(None, "tensor"),
            P(None, "tensor"),
            P(None, "tensor"),
            P("tensor", None),
            P(),
            P(),
            P("expert", None, "tensor"),
            P("expert", None, "tensor"),
            P("expert", "tensor", None),
        ),
        check_vma=False,
    )
```

```python
import functools
import math

import jax
import jax.numpy as jnp
from jax import lax
from jax.experimental import pallas as pl
from jax.experimental.pallas import tpu as pltpu
from jax.sharding import PartitionSpec as P

HEAD_DIMENSION = 64
SEQ_LEN = 512

EPS = 1e-06
SCALE = 0.125
NEGATIVE = -1e30
THETA = 10000.0
F32 = jnp.float32
BF16 = jnp.bfloat16
EXACT = lax.Precision.HIGHEST
LANES = 128
TILE = 256


def tables(tok_count):
    half = HEAD_DIMENSION // 2
    freq = jnp.exp(-math.log(THETA) * jnp.arange(half, dtype=F32) / half)
    places = (jnp.arange(tok_count) % SEQ_LEN).astype(F32)
    angle = places[:, None] * freq[None, :]
    return (jnp.cos(angle)[:, None, :], jnp.sin(angle)[:, None, :])


def rotate(field, cosine, sine_table, factor):
    half = HEAD_DIMENSION // 2
    first = field[..., :half]
    second = field[..., half:]
    return jnp.concatenate(
        [
            first * cosine - factor * second * sine_table,
            second * cosine + factor * first * sine_table,
        ],
        axis=-1,
    )


def causal_mask():
    places = jnp.arange(SEQ_LEN)
    return places[:, None] >= places[None, :]


def attend_forward(query_rows, rotated_keys, value_rows):
    scores = (
        jnp.einsum("lkgd,mkd->kglm", query_rows, rotated_keys, preferred_element_type=F32) * SCALE
    )
    scores = jnp.where(causal_mask(), scores, NEGATIVE)
    highest = jnp.max(scores, axis=-1, keepdims=True)
    expanded = jnp.exp(scores - highest)
    summed = jnp.sum(expanded, axis=-1, keepdims=True)
    probability = (expanded / summed).astype(BF16)
    heads_out = jnp.einsum("kglm,mkd->lkgd", probability, value_rows, preferred_element_type=F32)
    return (heads_out.astype(BF16), (highest + jnp.log(summed))[..., 0])


def attend_backward(query_rows, rotated_keys, value_rows, grad_heads, log_total):
    scores = (
        jnp.einsum("lkgd,mkd->kglm", query_rows, rotated_keys, preferred_element_type=F32) * SCALE
    )
    probability = jnp.where(causal_mask(), jnp.exp(scores - log_total[..., None]), 0.0)
    prob_low = probability.astype(BF16)
    grad_values = jnp.einsum("kglm,lkgd->mkd", prob_low, grad_heads, preferred_element_type=F32)
    grad_prob = jnp.einsum("lkgd,mkd->kglm", grad_heads, value_rows, preferred_element_type=F32)
    row_delta = jnp.sum(probability * grad_prob, axis=-1, keepdims=True)
    grad_scores = (probability * (grad_prob - row_delta)).astype(BF16)
    grad_queries = (
        jnp.einsum("kglm,mkd->lkgd", grad_scores, rotated_keys, preferred_element_type=F32) * SCALE
    )
    grad_keys = (
        jnp.einsum("kglm,lkgd->mkd", grad_scores, query_rows, preferred_element_type=F32) * SCALE
    )
    return (grad_queries, grad_keys, grad_values)


def mm(left, right):
    return jnp.dot(left, right, preferred_element_type=F32)


def mm_rows(left, right):
    return lax.dot_general(left, right, (((0,), (0,)), ((), ())), preferred_element_type=F32)


def mm_cols(left, right):
    return lax.dot_general(left, right, (((1,), (1,)), ((), ())), preferred_element_type=F32)


def piece(array, index, size, axis=0):
    return lax.dynamic_slice_in_dim(array, index * size, size, axis)


def swap(array, mask):
    size = lax.axis_size("expert")
    return lax.ppermute(array, "expert", [(i, i ^ mask) for i in range(size)])


def z_shift(array, step):
    size = lax.axis_size("tensor")
    return lax.ppermute(array, "tensor", [(i, (i + step) % size) for i in range(size)])


def z_received(array):
    return [array] + [z_shift(array, step) for step in range(1, lax.axis_size("tensor"))]


def z_gather(array):
    size, mine = lax.axis_size("tensor"), lax.axis_index("tensor")
    rows = array.shape[0]
    whole = jnp.zeros((rows * size,) + array.shape[1:], array.dtype)
    for step, part in enumerate(z_received(array)):
        whole = lax.dynamic_update_slice_in_dim(whole, part, (mine + size - step) % size * rows, 0)
    return whole


def z_scatter(array, axis=0):
    size, mine = lax.axis_size("tensor"), lax.axis_index("tensor")
    width = array.shape[axis] // size
    total = piece(array, mine, width, axis).astype(F32)
    for step in range(1, size):
        sent = piece(array, (mine + step) % size, width, axis).astype(BF16)
        total = total + z_shift(sent, step).astype(F32)
    return total


def same_core_groups():
    size = lax.axis_size("expert")
    return [list(range(0, size, 2)), list(range(1, size, 2))]


def plane_gather(array):
    if lax.axis_size("expert") != 8:
        return [
            lax.all_gather(
                array, "expert", axis=0, tiled=True, axis_index_groups=same_core_groups()
            )
        ]
    half = array.shape[0] // 2
    from_x = swap(array, 2)
    from_y = swap(array, 4)
    diagonal = jnp.concatenate([swap(from_x[:half], 4), swap(from_y[half:], 2)])
    return [array, from_x, from_y, diagonal]


def plane_scatter(blocks):
    if lax.axis_size("expert") != 8:
        return lax.psum_scatter(
            blocks[0].astype(BF16),
            "expert",
            scatter_dimension=0,
            tiled=True,
            axis_index_groups=same_core_groups(),
        ).astype(F32)
    own, for_x, for_y, diagonal = blocks
    half = own.shape[0] // 2
    diagonal = diagonal.astype(BF16)
    via_x = swap(diagonal[:half], 2).astype(F32)
    via_y = swap(diagonal[half:], 4).astype(F32)
    for_y = jnp.concatenate([for_y[:half] + via_x, for_y[half:]]).astype(BF16)
    for_x = jnp.concatenate([for_x[:half], for_x[half:] + via_y]).astype(BF16)
    return own + swap(for_x, 2).astype(F32) + swap(for_y, 4).astype(F32)


def expert_sum(array):
    if lax.axis_size("expert") != 8:
        return lax.psum(array.astype(BF16), "expert").astype(F32)
    place = lax.axis_index("expert")
    core, chip = place % 2, place // 2
    half = array.shape[0] // 2
    rows = half // 4
    mine = piece(array, core, half) + swap(
        piece(array, 1 - core, half).astype(BF16), 1
    ).astype(F32)
    total = piece(mine, chip, rows)
    for mask in (1, 2, 3):
        total = total + swap(piece(mine, chip ^ mask, rows).astype(BF16), 2 * mask).astype(F32)
    total = total.astype(BF16)
    gathered = jnp.zeros((half,) + array.shape[1:], BF16)
    for mask in (0, 1, 2, 3):
        part = swap(total, 2 * mask) if mask else total
        gathered = lax.dynamic_update_slice_in_dim(gathered, part, (chip ^ mask) * rows, 0)
    both = jnp.concatenate([gathered, gathered])
    both = lax.dynamic_update_slice_in_dim(both, swap(gathered, 1), (1 - core) * half, 0)
    return both.astype(F32)


def small_sum(array, over_tensor):
    size = lax.axis_size("expert")
    if size & (size - 1):
        array = lax.psum(array, "expert")
    else:
        mask = 1
        while mask < size:
            array = array + swap(array, mask)
            mask *= 2
    if over_tensor:
        parts = z_received(array)
        array = parts[0]
        for part in parts[1:]:
            array = array + part
    return array


def expert_kernel(
    experts,
    top_count,
    units,
    names_ref,
    normed_ref,
    grad_ref,
    router_ref,
    gate_ref,
    up_ref,
    down_ref,
    out_ref,
    rows_ref,
    gate_grad_ref,
    up_grad_ref,
    inner_ref,
):
    tile, model_width = normed_ref.shape
    width = gate_ref.shape[1]
    normed = normed_ref[...]
    grad = grad_ref[:, :model_width]
    chosen_names = grad_ref[:, model_width:].astype(F32)
    lane = lax.broadcasted_iota(jnp.int32, (tile, LANES), 1)
    lane_float = lane.astype(F32)
    chosen = lane_float == chosen_names[:, 0:1]
    for k in range(1, top_count):
        chosen = chosen | (lane_float == chosen_names[:, k : k + 1])
    logits = jnp.where(chosen, mm(normed, router_ref[...]), NEGATIVE)
    expanded = jnp.exp(logits - jnp.max(logits, axis=-1, keepdims=True))
    expanded = jnp.where(chosen, expanded, 0.0)
    routing = expanded / jnp.sum(expanded, axis=-1, keepdims=True)
    grad_routing = jnp.zeros((tile, LANES), F32)
    columns = min(TILE, width)
    for start in range(0, width, columns):
        part = slice(start, start + columns)
        gate_act = mm(normed, gate_ref[:, part])
        up_act = mm(normed, up_ref[:, part])
        grad_plain = mm_cols(grad, down_ref[part, :])
        weights = []
        for e in range(start // units, (start + columns) // units):
            weight = jnp.sum(
                jnp.where(lane == names_ref[e], routing, 0.0), axis=-1, keepdims=True
            )
            weights.append(jnp.broadcast_to(weight, (tile, units)))
        wide = jnp.concatenate(weights, axis=1) if len(weights) > 1 else weights[0]
        sigmoid_gate = jax.nn.sigmoid(gate_act)
        swish = gate_act * sigmoid_gate
        inner = swish * up_act
        inner_grad = inner * grad_plain
        for i, e in enumerate(range(start // units, (start + columns) // units)):
            total = jnp.sum(inner_grad[:, i * units : (i + 1) * units], axis=-1, keepdims=True)
            grad_routing = jnp.where(lane == names_ref[e], total, grad_routing)
        grad_inner = grad_plain * wide
        inner_ref[:, part] = (inner * wide).astype(BF16)
        up_grad_ref[:, part] = (grad_inner * swish).astype(BF16)
        gate_grad_ref[:, part] = (
            grad_inner * up_act * (sigmoid_gate + swish * (1.0 - sigmoid_gate))
        ).astype(BF16)
    rounded = grad_routing.astype(BF16).astype(F32)
    left = pltpu.roll(grad_routing - rounded, experts, 1)
    rows_ref[:, model_width:] = (rounded + left).astype(BF16)
    rows_ref[:, :model_width] = (
        mm_cols(gate_grad_ref[...], gate_ref[...]) + mm_cols(up_grad_ref[...], up_ref[...])
    ).astype(BF16)
    out_ref[...] = mm(inner_ref[...], down_ref[...]).astype(BF16)


def expert_block(names, normed, grad, router, gate_w, up_w, down_w, experts, top_count, units):
    rows, model_width = normed.shape
    width = gate_w.shape[1]
    tile = min(TILE, rows)

    def tiled(columns):
        return pl.BlockSpec((tile, columns), lambda i, names: (i, 0))

    def fixed(array):
        return pl.BlockSpec(array.shape, lambda i, names: (0, 0))

    def shaped(columns):
        return jax.ShapeDtypeStruct((rows, columns), BF16)

    return pl.pallas_call(
        functools.partial(expert_kernel, experts, top_count, units),
        grid_spec=pltpu.PrefetchScalarGridSpec(
            num_scalar_prefetch=1,
            grid=(rows // tile,),
            in_specs=[
                tiled(model_width),
                tiled(model_width + LANES),
                fixed(router),
                fixed(gate_w),
                fixed(up_w),
                fixed(down_w),
            ],
            out_specs=[
                tiled(model_width),
                tiled(model_width + LANES),
                tiled(width),
                tiled(width),
                tiled(width),
            ],
        ),
        out_shape=[
            shaped(model_width),
            shaped(model_width + LANES),
            shaped(width),
            shaped(width),
            shaped(width),
        ],
        compiler_params=pltpu.CompilerParams(vmem_limit_bytes=44 * 1024 * 1024),
        cost_estimate=pl.CostEstimate(
            flops=12 * rows * model_width * width,
            bytes_accessed=6 * model_width * width + 14 * rows * model_width,
            transcendentals=rows * width,
        ),
        name="experts",
    )(names, normed, grad, router, gate_w, up_w, down_w)


def tied(*arrays):
    return lax.optimization_barrier(arrays)


def norm_scale(field):
    return lax.rsqrt(jnp.mean(field * field, axis=-1, keepdims=True) + EPS)


def route(normed, router, chosen):
    logits = mm(normed, router)
    masked = jnp.where(chosen, logits, NEGATIVE)
    highest = jnp.max(masked, axis=-1, keepdims=True)
    expanded = jnp.where(chosen, jnp.exp(masked - highest), 0.0)
    return expanded / jnp.sum(expanded, axis=-1, keepdims=True)


def local(
    tokens,
    norm1_gain,
    w_query,
    key_projection_weight,
    value_projection_weight,
    w_output,
    norm2_gain,
    w_router,
    expert_gate_weight,
    expert_up_weight,
    expert_down_weight,
    expert_ids,
    cotangent,
):
    tok_count = tokens.shape[0]
    model_width = tokens.shape[1]
    experts, top_count = w_router.shape[1], expert_ids.shape[1]
    here, units = expert_gate_weight.shape[0], expert_gate_weight.shape[2]
    heads_query = w_query.shape[1] // HEAD_DIMENSION
    heads_kv = key_projection_weight.shape[1] // HEAD_DIMENSION
    group_size = heads_query // heads_kv
    cosine, sine_table = tables(tok_count)
    expert_count = lax.axis_size("expert")
    tensor_count = lax.axis_size("tensor")
    expert_place = lax.axis_index("expert")
    tensor_place = lax.axis_index("tensor")
    core = expert_place % 2
    own_rows = tok_count // tensor_count
    col_width = model_width // tensor_count

    names_wide = jnp.pad(expert_ids.astype(BF16), ((0, 0), (0, LANES - top_count)))
    grad_blocks = plane_gather(jnp.concatenate([cotangent, names_wide], axis=1))

    def chip_weights(weight):
        other = swap(weight, 1)
        return jnp.concatenate([weight, other])

    def as_columns(weight):
        return weight.transpose(1, 0, 2).reshape(model_width, -1)

    gate_w = as_columns(chip_weights(expert_gate_weight))
    up_w = as_columns(chip_weights(expert_up_weight))
    down_w = chip_weights(expert_down_weight).reshape(-1, model_width)

    share = w_output.shape[0] // expert_count
    w_piece = piece(w_output, expert_place, share)
    w_pieces = jnp.stack([z_shift(w_piece, step) for step in range(1, tensor_count)])
    if expert_count == 8:
        w_other = swap(w_pieces, 1)
        w_pair = jnp.where(
            core == 0,
            jnp.concatenate([w_pieces, w_other], axis=1),
            jnp.concatenate([w_other, w_pieces], axis=1),
        )
        chip = expert_place // 2
        w_parts = jnp.zeros((tensor_count - 1,) + w_output.shape, BF16)
        w_x = swap(w_pair, 2)
        w_y = swap(w_pair, 4)
        w_d = jnp.concatenate([swap(w_x[:, :share], 4), swap(w_y[:, share:], 2)], axis=1)
        for mask, part in enumerate((w_pair, w_x, w_y, w_d)):
            w_parts = lax.dynamic_update_slice_in_dim(w_parts, part, (chip ^ mask) * 2 * share, 1)
    else:
        w_parts = lax.all_gather(w_pieces, "expert", axis=1, tiled=True)

    resid_in = tokens.astype(F32)
    first_scale = norm_scale(resid_in)
    first_norm = (resid_in * first_scale * norm1_gain).astype(BF16)
    query_raw = mm(first_norm, w_query).reshape(tok_count, heads_query, HEAD_DIMENSION)
    key_raw = mm(first_norm, key_projection_weight).reshape(tok_count, heads_kv, HEAD_DIMENSION)
    query_rows = (
        rotate(query_raw, cosine, sine_table, 1.0)
        .astype(BF16)
        .reshape(tok_count, heads_kv, group_size, HEAD_DIMENSION)
    )
    rotated_keys = rotate(key_raw, cosine, sine_table, 1.0).astype(BF16)
    value_rows = (
        mm(first_norm, value_projection_weight)
        .astype(BF16)
        .reshape(tok_count, heads_kv, HEAD_DIMENSION)
    )
    attended, log_total = attend_forward(query_rows, rotated_keys, value_rows)
    attended = attended.reshape(tok_count, heads_query * HEAD_DIMENSION)

    attended_parts = z_received(attended)
    if expert_count == 8:
        grad_x, grad_y, *attended_parts = tied(grad_blocks[1], grad_blocks[2], *attended_parts)
        grad_blocks[1], grad_blocks[2] = grad_x, grad_y
    hidden = resid_in + mm(attended, w_output)
    for step in range(1, tensor_count):
        hidden = hidden + mm(attended_parts[step], w_parts[step - 1])
    second_scale = norm_scale(hidden)
    second_norm = (hidden * second_scale * norm2_gain).astype(BF16)

    local_names = jnp.concatenate(
        [
            expert_place * here + jnp.arange(here, dtype=jnp.int32),
            (expert_place ^ 1) * here + jnp.arange(here, dtype=jnp.int32),
        ]
    )
    router_wide = jnp.pad(w_router, ((0, 0), (0, LANES - experts)))
    if expert_count == 8:
        second_norm, grad_blocks[3] = tied(second_norm, grad_blocks[3])
    normed_blocks = plane_gather(second_norm)
    done = [
        expert_block(
            local_names,
            normed,
            grad,
            router_wide,
            gate_w,
            up_w,
            down_w,
            experts,
            top_count,
            units,
        )
        for normed, grad in zip(normed_blocks, grad_blocks)
    ]
    plane_rows = plane_scatter([block[1].astype(F32) for block in done])
    plane_rows, *out_blocks = tied(plane_rows, *[block[0] for block in done])
    out_blocks = [block.astype(F32) for block in out_blocks]
    held = tied(*[array for block in done for array in block[2:]])
    done = [held[3 * i : 3 * i + 3] for i in range(len(done))]
    gate_total = up_total = down_total = 0.0
    for normed, grad, block in zip(normed_blocks, grad_blocks, done):
        gate_total = gate_total + mm_rows(normed, block[0])
        up_total = up_total + mm_rows(normed, block[1])
        down_total = down_total + mm_rows(block[2], grad[:, :model_width])

    row_sum = z_scatter(plane_rows)
    my_routing_grad = (
        row_sum[:, model_width : model_width + experts]
        + row_sum[:, model_width + experts : model_width + 2 * experts]
    )
    row_sum = row_sum[:, :model_width]

    def mine(array):
        return piece(array, tensor_place, own_rows)

    my_hidden, my_scale = mine(hidden), mine(second_scale)
    my_normed = mine(second_norm)
    names = jnp.arange(experts, dtype=jnp.int32)
    my_chosen = jnp.any(mine(expert_ids)[:, :, None] == names[None, None, :], axis=1)
    my_routing = route(my_normed, w_router, my_chosen)
    my_normed = my_normed.astype(F32)
    my_logits = my_routing * (
        my_routing_grad - jnp.sum(my_routing * my_routing_grad, axis=-1, keepdims=True)
    )
    router_float = w_router.astype(F32)
    grad_second = row_sum + jnp.dot(my_logits, router_float.T, precision=EXACT)
    grad_router = lax.dot_general(
        my_logits, my_normed, (((0,), (0,)), ((), ())), precision=EXACT
    )
    grad_norm2 = jnp.sum(grad_second * my_hidden * my_scale, axis=0)
    gained_two = grad_second * norm2_gain
    my_grad_hidden = (
        mine(cotangent).astype(F32)
        + my_scale * gained_two
        - my_hidden * my_scale**3 * jnp.mean(gained_two * my_hidden, axis=-1, keepdims=True)
    )
    grad_branch = z_gather(my_grad_hidden.astype(BF16))
    early = jnp.concatenate([grad_router, grad_norm2[None]])
    early = lax.psum(lax.psum(early, "tensor"), "expert")
    grad_output = expert_sum(mm_rows(attended, grad_branch))

    grad_heads = mm_cols(grad_branch, w_output).astype(BF16)
    grad_heads = grad_heads.reshape(tok_count, heads_kv, group_size, HEAD_DIMENSION)
    grad_queries, grad_keys, grad_values = attend_backward(
        query_rows, rotated_keys, value_rows, grad_heads, log_total
    )
    grad_query_raw = rotate(
        grad_queries.reshape(tok_count, heads_query, HEAD_DIMENSION), cosine, sine_table, -1.0
    )
    grad_query_raw = grad_query_raw.reshape(tok_count, -1).astype(BF16)
    grad_key_raw = rotate(grad_keys, cosine, sine_table, -1.0)
    grad_key_raw = grad_key_raw.reshape(tok_count, -1).astype(BF16)
    grad_value_raw = grad_values.reshape(tok_count, -1).astype(BF16)
    grad_raw = jnp.concatenate([grad_query_raw, grad_key_raw, grad_value_raw], axis=1)
    grad_weights = expert_sum(mm_rows(first_norm, grad_raw))
    q_width, k_width = w_query.shape[1], key_projection_weight.shape[1]
    grad_first = (
        mm_cols(grad_query_raw, w_query)
        + mm_cols(grad_key_raw, key_projection_weight)
        + mm_cols(grad_value_raw, value_projection_weight)
    )
    grad_first = z_scatter(grad_first)
    gained_one = grad_first * norm1_gain
    my_resid, my_first_scale = mine(resid_in), mine(first_scale)
    grad_norm1 = jnp.sum(grad_first * my_resid * my_first_scale, axis=0)
    my_grad_input = (
        my_grad_hidden
        + my_first_scale * gained_one
        - my_resid * my_first_scale**3 * jnp.mean(gained_one * my_resid, axis=-1, keepdims=True)
    )
    grad_input = z_gather(my_grad_input.astype(BF16)).astype(F32)
    grad_norm1 = small_sum(grad_norm1[None], True)[0]

    plane_out, _ = tied(plane_scatter(out_blocks), grad_branch)
    routed = z_scatter(plane_out, axis=1)
    mixed = (piece(hidden, tensor_place, col_width, 1) + routed).astype(BF16)

    width = here * units

    def from_chip(total):
        return total[:, :width] + swap(total[:, width:].astype(BF16), 1).astype(F32)

    def as_experts(total):
        return total.reshape(model_width, here, units).transpose(1, 0, 2)

    grad_gate = as_experts(from_chip(gate_total))
    up_weight_gradient = as_experts(from_chip(up_total))
    grad_down = down_total[:width] + swap(down_total[width:].astype(BF16), 1).astype(F32)
    grad_down = grad_down.reshape(here, units, model_width)
    return (
        mixed,
        grad_input,
        grad_norm1,
        grad_weights[:, :q_width],
        grad_weights[:, q_width : q_width + k_width],
        grad_weights[:, q_width + k_width :],
        grad_output,
        early[experts],
        early[:experts].T,
        grad_gate,
        up_weight_gradient,
        grad_down,
    )


def solution(mesh):
    placed = (
        P("expert", None),
        P(),
        P(None, "tensor"),
        P(None, "tensor"),
        P(None, "tensor"),
        P("tensor", None),
        P(),
        P(),
        P("expert", None, "tensor"),
        P("expert", None, "tensor"),
        P("expert", "tensor", None),
        P("expert", None),
        P("expert", None),
    )
    return jax.shard_map(
        local,
        mesh=mesh,
        in_specs=placed,
        out_specs=(
            P("expert", "tensor"),
            P("expert", None),
            P(),
            P(None, "tensor"),
            P(None, "tensor"),
            P(None, "tensor"),
            P("tensor", None),
            P(),
            P(),
            P("expert", None, "tensor"),
            P("expert", None, "tensor"),
            P("expert", "tensor", None),
        ),
        check_vma=False,
    )
```

```python
import functools
import math

import jax
import jax.numpy as jnp
from jax import lax
from jax.experimental import pallas as pl
from jax.experimental.pallas import tpu as pltpu
from jax.sharding import PartitionSpec as P

HEAD_DIMENSION = 64
SEQ_LEN = 512

EPS = 1e-06
SCALE = 0.125
NEGATIVE = -1e30
THETA = 10000.0
F32 = jnp.float32
BF16 = jnp.bfloat16
EXACT = lax.Precision.HIGHEST
LANES = 128
TILE = 256


def tables(tok_count):
    half = HEAD_DIMENSION // 2
    freq = jnp.exp(-math.log(THETA) * jnp.arange(half, dtype=F32) / half)
    places = (jnp.arange(tok_count) % SEQ_LEN).astype(F32)
    angle = places[:, None] * freq[None, :]
    return (jnp.cos(angle)[:, None, :], jnp.sin(angle)[:, None, :])


def rotate(field, cosine, sine_table, factor):
    half = HEAD_DIMENSION // 2
    first = field[..., :half]
    second = field[..., half:]
    return jnp.concatenate(
        [
            first * cosine - factor * second * sine_table,
            second * cosine + factor * first * sine_table,
        ],
        axis=-1,
    )


def causal_mask():
    places = jnp.arange(SEQ_LEN)
    return places[:, None] >= places[None, :]


def attend_forward(query_rows, rotated_keys, value_rows):
    scores = (
        jnp.einsum("lkgd,mkd->kglm", query_rows, rotated_keys, preferred_element_type=F32) * SCALE
    )
    scores = jnp.where(causal_mask(), scores, NEGATIVE)
    highest = jnp.max(scores, axis=-1, keepdims=True)
    expanded = jnp.exp(scores - highest)
    summed = jnp.sum(expanded, axis=-1, keepdims=True)
    probability = (expanded / summed).astype(BF16)
    heads_out = jnp.einsum("kglm,mkd->lkgd", probability, value_rows, preferred_element_type=F32)
    return (heads_out.astype(BF16), (highest + jnp.log(summed))[..., 0])


def attend_backward(query_rows, rotated_keys, value_rows, grad_heads, log_total):
    scores = (
        jnp.einsum("lkgd,mkd->kglm", query_rows, rotated_keys, preferred_element_type=F32) * SCALE
    )
    probability = jnp.where(causal_mask(), jnp.exp(scores - log_total[..., None]), 0.0)
    prob_low = probability.astype(BF16)
    grad_values = jnp.einsum("kglm,lkgd->mkd", prob_low, grad_heads, preferred_element_type=F32)
    grad_prob = jnp.einsum("lkgd,mkd->kglm", grad_heads, value_rows, preferred_element_type=F32)
    row_delta = jnp.sum(probability * grad_prob, axis=-1, keepdims=True)
    grad_scores = (probability * (grad_prob - row_delta)).astype(BF16)
    grad_queries = (
        jnp.einsum("kglm,mkd->lkgd", grad_scores, rotated_keys, preferred_element_type=F32) * SCALE
    )
    grad_keys = (
        jnp.einsum("kglm,lkgd->mkd", grad_scores, query_rows, preferred_element_type=F32) * SCALE
    )
    return (grad_queries, grad_keys, grad_values)


def mm(left, right):
    return jnp.dot(left, right, preferred_element_type=F32)


def mm_rows(left, right):
    return lax.dot_general(left, right, (((0,), (0,)), ((), ())), preferred_element_type=F32)


def mm_cols(left, right):
    return lax.dot_general(left, right, (((1,), (1,)), ((), ())), preferred_element_type=F32)


def piece(array, index, size, axis=0):
    return lax.dynamic_slice_in_dim(array, index * size, size, axis)


def swap(array, mask):
    size = lax.axis_size("expert")
    return lax.ppermute(array, "expert", [(i, i ^ mask) for i in range(size)])


def z_shift(array, step):
    size = lax.axis_size("tensor")
    return lax.ppermute(array, "tensor", [(i, (i + step) % size) for i in range(size)])


def z_received(array):
    return [array] + [z_shift(array, step) for step in range(1, lax.axis_size("tensor"))]


def z_place(parts):
    size, mine = lax.axis_size("tensor"), lax.axis_index("tensor")
    rows = parts[0].shape[0]
    whole = jnp.zeros((rows * size,) + parts[0].shape[1:], parts[0].dtype)
    for step, part in enumerate(parts):
        whole = lax.dynamic_update_slice_in_dim(whole, part, (mine + size - step) % size * rows, 0)
    return whole


def z_scatter(array, axis=0):
    size, mine = lax.axis_size("tensor"), lax.axis_index("tensor")
    width = array.shape[axis] // size
    total = piece(array, mine, width, axis).astype(F32)
    for step in range(1, size):
        sent = piece(array, (mine + step) % size, width, axis).astype(BF16)
        total = total + z_shift(sent, step).astype(F32)
    return total


def same_core_groups():
    size = lax.axis_size("expert")
    return [list(range(0, size, 2)), list(range(1, size, 2))]


def plane_gather(array):
    if lax.axis_size("expert") != 8:
        return [
            lax.all_gather(
                array, "expert", axis=0, tiled=True, axis_index_groups=same_core_groups()
            )
        ]
    half = array.shape[0] // 2
    from_x = swap(array, 2)
    from_y = swap(array, 4)
    diagonal = jnp.concatenate([swap(from_x[:half], 4), swap(from_y[half:], 2)])
    return [array, from_x, from_y, diagonal]


def plane_scatter(blocks):
    if lax.axis_size("expert") != 8:
        return lax.psum_scatter(
            blocks[0].astype(BF16),
            "expert",
            scatter_dimension=0,
            tiled=True,
            axis_index_groups=same_core_groups(),
        ).astype(F32)
    own, for_x, for_y, diagonal = blocks
    half = own.shape[0] // 2
    diagonal = diagonal.astype(BF16)
    via_x = swap(diagonal[:half], 2).astype(F32)
    via_y = swap(diagonal[half:], 4).astype(F32)
    for_y = jnp.concatenate([for_y[:half] + via_x, for_y[half:]]).astype(BF16)
    for_x = jnp.concatenate([for_x[:half], for_x[half:] + via_y]).astype(BF16)
    return own + swap(for_x, 2).astype(F32) + swap(for_y, 4).astype(F32)


def expert_sum(array):
    if lax.axis_size("expert") != 8:
        return lax.psum(array.astype(BF16), "expert").astype(F32)
    place = lax.axis_index("expert")
    core, chip = place % 2, place // 2
    half = array.shape[0] // 2
    rows = half // 4
    array = array.astype(BF16)
    mine = piece(array, core, half).astype(F32)
    mine = mine + swap(piece(array, 1 - core, half), 1).astype(F32)
    total = piece(mine, chip, rows)
    for mask in (1, 2, 3):
        total = total + swap(piece(mine, chip ^ mask, rows).astype(BF16), 2 * mask).astype(F32)
    total = total.astype(BF16)
    gathered = jnp.zeros((half,) + array.shape[1:], BF16)
    for mask in (0, 1, 2, 3):
        part = swap(total, 2 * mask) if mask else total
        gathered = lax.dynamic_update_slice_in_dim(gathered, part, (chip ^ mask) * rows, 0)
    both = jnp.concatenate([gathered, gathered])
    both = lax.dynamic_update_slice_in_dim(both, swap(gathered, 1), (1 - core) * half, 0)
    return both.astype(F32)


def expert_kernel(
    experts,
    top_count,
    units,
    names_ref,
    normed_ref,
    grad_ref,
    router_ref,
    gate_ref,
    up_ref,
    down_ref,
    out_ref,
    rows_ref,
    gate_grad_ref,
    up_grad_ref,
    inner_ref,
):
    tile, model_width = normed_ref.shape
    width = gate_ref.shape[1]
    normed = normed_ref[...]
    grad = grad_ref[:, :model_width]
    chosen_names = grad_ref[:, model_width:].astype(F32)
    lane = lax.broadcasted_iota(jnp.int32, (tile, LANES), 1)
    lane_float = lane.astype(F32)
    chosen = lane_float == chosen_names[:, 0:1]
    for k in range(1, top_count):
        chosen = chosen | (lane_float == chosen_names[:, k : k + 1])
    logits = jnp.where(chosen, mm(normed, router_ref[...]), NEGATIVE)
    expanded = jnp.exp(logits - jnp.max(logits, axis=-1, keepdims=True))
    expanded = jnp.where(chosen, expanded, 0.0)
    routing = expanded / jnp.sum(expanded, axis=-1, keepdims=True)
    grad_routing = jnp.zeros((tile, LANES), F32)
    columns = min(TILE, width)
    for start in range(0, width, columns):
        part = slice(start, start + columns)
        gate_act = mm(normed, gate_ref[:, part])
        up_act = mm(normed, up_ref[:, part])
        grad_plain = mm_cols(grad, down_ref[part, :])
        weights = []
        for e in range(start // units, (start + columns) // units):
            weight = jnp.sum(
                jnp.where(lane == names_ref[e], routing, 0.0), axis=-1, keepdims=True
            )
            weights.append(jnp.broadcast_to(weight, (tile, units)))
        wide = jnp.concatenate(weights, axis=1) if len(weights) > 1 else weights[0]
        sigmoid_gate = jax.nn.sigmoid(gate_act)
        swish = gate_act * sigmoid_gate
        inner = swish * up_act
        inner_grad = inner * grad_plain
        for i, e in enumerate(range(start // units, (start + columns) // units)):
            total = jnp.sum(inner_grad[:, i * units : (i + 1) * units], axis=-1, keepdims=True)
            grad_routing = jnp.where(lane == names_ref[e], total, grad_routing)
        grad_inner = grad_plain * wide
        inner_ref[:, part] = (inner * wide).astype(BF16)
        up_grad_ref[:, part] = (grad_inner * swish).astype(BF16)
        gate_grad_ref[:, part] = (
            grad_inner * up_act * (sigmoid_gate + swish * (1.0 - sigmoid_gate))
        ).astype(BF16)
    rounded = grad_routing.astype(BF16).astype(F32)
    left = pltpu.roll(grad_routing - rounded, experts, 1)
    rows_ref[:, model_width:] = (rounded + left).astype(BF16)
    rows_ref[:, :model_width] = (
        mm_cols(gate_grad_ref[...], gate_ref[...]) + mm_cols(up_grad_ref[...], up_ref[...])
    ).astype(BF16)
    out_ref[...] = mm(inner_ref[...], down_ref[...]).astype(BF16)


def expert_block(names, normed, grad, router, gate_w, up_w, down_w, experts, top_count, units):
    rows, model_width = normed.shape
    width = gate_w.shape[1]
    tile = min(TILE, rows)

    def tiled(columns):
        return pl.BlockSpec((tile, columns), lambda i, names: (i, 0))

    def fixed(array):
        return pl.BlockSpec(array.shape, lambda i, names: (0, 0))

    def shaped(columns):
        return jax.ShapeDtypeStruct((rows, columns), BF16)

    return pl.pallas_call(
        functools.partial(expert_kernel, experts, top_count, units),
        grid_spec=pltpu.PrefetchScalarGridSpec(
            num_scalar_prefetch=1,
            grid=(rows // tile,),
            in_specs=[
                tiled(model_width),
                tiled(model_width + LANES),
                fixed(router),
                fixed(gate_w),
                fixed(up_w),
                fixed(down_w),
            ],
            out_specs=[
                tiled(model_width),
                tiled(model_width + LANES),
                tiled(width),
                tiled(width),
                tiled(width),
            ],
        ),
        out_shape=[
            shaped(model_width),
            shaped(model_width + LANES),
            shaped(width),
            shaped(width),
            shaped(width),
        ],
        compiler_params=pltpu.CompilerParams(vmem_limit_bytes=60 * 1024 * 1024),
        cost_estimate=pl.CostEstimate(
            flops=12 * rows * model_width * width,
            bytes_accessed=6 * model_width * width + 14 * rows * model_width,
            transcendentals=rows * width,
        ),
        name="experts",
    )(names, normed, grad, router, gate_w, up_w, down_w)


def tied(*arrays):
    return lax.optimization_barrier(arrays)


def norm_scale(field):
    return lax.rsqrt(jnp.mean(field * field, axis=-1, keepdims=True) + EPS)


def route(normed, router, chosen):
    logits = mm(normed, router)
    masked = jnp.where(chosen, logits, NEGATIVE)
    highest = jnp.max(masked, axis=-1, keepdims=True)
    expanded = jnp.where(chosen, jnp.exp(masked - highest), 0.0)
    return expanded / jnp.sum(expanded, axis=-1, keepdims=True)


def local(
    tokens,
    norm1_gain,
    w_query,
    key_projection_weight,
    value_projection_weight,
    w_output,
    norm2_gain,
    w_router,
    expert_gate_weight,
    expert_up_weight,
    expert_down_weight,
    expert_ids,
    cotangent,
):
    tok_count = tokens.shape[0]
    model_width = tokens.shape[1]
    experts, top_count = w_router.shape[1], expert_ids.shape[1]
    here, units = expert_gate_weight.shape[0], expert_gate_weight.shape[2]
    heads_query = w_query.shape[1] // HEAD_DIMENSION
    heads_kv = key_projection_weight.shape[1] // HEAD_DIMENSION
    group_size = heads_query // heads_kv
    cosine, sine_table = tables(tok_count)
    expert_count = lax.axis_size("expert")
    tensor_count = lax.axis_size("tensor")
    expert_place = lax.axis_index("expert")
    tensor_place = lax.axis_index("tensor")
    core = expert_place % 2
    own_rows = tok_count // tensor_count
    col_width = model_width // tensor_count

    names_wide = jnp.pad(expert_ids.astype(BF16), ((0, 0), (0, LANES - top_count)))
    grad_blocks = plane_gather(jnp.concatenate([cotangent, names_wide], axis=1))

    expert_weights = (expert_gate_weight, expert_up_weight, expert_down_weight)
    other_weights = [swap(weight, 1) for weight in expert_weights]

    resid_in = tokens.astype(F32)
    first_scale = norm_scale(resid_in)
    first_norm = (resid_in * first_scale * norm1_gain).astype(BF16)
    query_raw = mm(first_norm, w_query).reshape(tok_count, heads_query, HEAD_DIMENSION)
    key_raw = mm(first_norm, key_projection_weight).reshape(tok_count, heads_kv, HEAD_DIMENSION)
    query_rows = (
        rotate(query_raw, cosine, sine_table, 1.0)
        .astype(BF16)
        .reshape(tok_count, heads_kv, group_size, HEAD_DIMENSION)
    )
    rotated_keys = rotate(key_raw, cosine, sine_table, 1.0).astype(BF16)
    value_rows = (
        mm(first_norm, value_projection_weight)
        .astype(BF16)
        .reshape(tok_count, heads_kv, HEAD_DIMENSION)
    )
    attended, log_total = attend_forward(query_rows, rotated_keys, value_rows)
    attended = attended.reshape(tok_count, heads_query * HEAD_DIMENSION)

    attended, other_weights = tied(attended, other_weights)
    attended_parts = z_received(attended)

    share = w_output.shape[0] // expert_count
    w_piece = piece(w_output, expert_place, share)
    w_pieces = jnp.stack([z_shift(w_piece, step) for step in range(1, tensor_count)])
    if expert_count == 8:
        w_other = swap(w_pieces, 1)
        w_pair = jnp.where(
            core == 0,
            jnp.concatenate([w_pieces, w_other], axis=1),
            jnp.concatenate([w_other, w_pieces], axis=1),
        )
        chip = expert_place // 2
        w_parts = jnp.zeros((tensor_count - 1,) + w_output.shape, BF16)
        grad_blocks[1], grad_blocks[2], w_pair = tied(grad_blocks[1], grad_blocks[2], w_pair)
        w_x, w_y, w_d = swap(w_pair, 2), swap(w_pair, 4), swap(w_pair, 6)
        w_pair, w_x, w_y, w_d, attended_parts = tied(w_pair, w_x, w_y, w_d, attended_parts)
        for mask, part in enumerate((w_pair, w_x, w_y, w_d)):
            w_parts = lax.dynamic_update_slice_in_dim(w_parts, part, (chip ^ mask) * 2 * share, 1)
    else:
        w_parts = lax.all_gather(w_pieces, "expert", axis=1, tiled=True)

    resid_in, attended_parts, other_weights = tied(resid_in, attended_parts, other_weights)
    attended = attended_parts[0]

    def as_columns(weight):
        return weight.transpose(1, 0, 2).reshape(model_width, -1)

    chip_weights = [jnp.concatenate(pair) for pair in zip(expert_weights, other_weights)]
    gate_w, up_w = as_columns(chip_weights[0]), as_columns(chip_weights[1])
    down_w = chip_weights[2].reshape(-1, model_width)
    hidden = resid_in + mm(attended, w_output)
    for step in range(1, tensor_count):
        hidden = hidden + mm(attended_parts[step], w_parts[step - 1])
    second_scale = norm_scale(hidden)
    second_norm = (hidden * second_scale * norm2_gain).astype(BF16)

    local_names = jnp.concatenate(
        [
            expert_place * here + jnp.arange(here, dtype=jnp.int32),
            (expert_place ^ 1) * here + jnp.arange(here, dtype=jnp.int32),
        ]
    )
    router_wide = jnp.pad(w_router, ((0, 0), (0, LANES - experts)))
    if expert_count == 8:
        second_norm, grad_blocks[3] = tied(second_norm, grad_blocks[3])
    normed_blocks = plane_gather(second_norm)
    done = [
        expert_block(
            local_names,
            normed,
            grad,
            router_wide,
            gate_w,
            up_w,
            down_w,
            experts,
            top_count,
            units,
        )
        for normed, grad in zip(normed_blocks, grad_blocks)
    ]
    plane_rows = plane_scatter([block[1].astype(F32) for block in done])
    plane_rows, *out_blocks = tied(plane_rows, *[block[0] for block in done])
    out_blocks = [block.astype(F32) for block in out_blocks]
    held = tied(*[array for block in done for array in block[2:]])
    done = [held[3 * i : 3 * i + 3] for i in range(len(done))]
    gate_total = up_total = down_total = 0.0
    for normed, grad, block in zip(normed_blocks, grad_blocks, done):
        gate_total = gate_total + mm_rows(normed, block[0])
        up_total = up_total + mm_rows(normed, block[1])
        down_total = down_total + mm_rows(block[2], grad[:, :model_width])

    width = here * units

    def from_chip(total):
        return total[:, :width] + swap(total[:, width:].astype(BF16), 1).astype(F32)

    def as_experts(total):
        return total.reshape(model_width, here, units).transpose(1, 0, 2)

    grad_gate = as_experts(from_chip(gate_total))
    up_weight_gradient = as_experts(from_chip(up_total))
    grad_down = down_total[:width] + swap(down_total[width:].astype(BF16), 1).astype(F32)
    grad_down = grad_down.reshape(here, units, model_width)
    row_sum = z_scatter(plane_rows)
    my_routing_grad = (
        row_sum[:, model_width : model_width + experts]
        + row_sum[:, model_width + experts : model_width + 2 * experts]
    )
    row_sum = row_sum[:, :model_width]

    def mine(array):
        return piece(array, tensor_place, own_rows)

    my_hidden, my_scale = mine(hidden), mine(second_scale)
    my_normed = mine(second_norm)
    names = jnp.arange(experts, dtype=jnp.int32)
    my_chosen = jnp.any(mine(expert_ids)[:, :, None] == names[None, None, :], axis=1)
    my_routing = route(my_normed, w_router, my_chosen)
    my_normed = my_normed.astype(F32)
    my_logits = my_routing * (
        my_routing_grad - jnp.sum(my_routing * my_routing_grad, axis=-1, keepdims=True)
    )
    router_float = w_router.astype(F32)
    grad_second = row_sum + jnp.dot(my_logits, router_float.T, precision=EXACT)
    grad_router = lax.dot_general(
        my_logits, my_normed, (((0,), (0,)), ((), ())), precision=EXACT
    )
    grad_norm2 = jnp.sum(grad_second * my_hidden * my_scale, axis=0)
    gained_two = grad_second * norm2_gain
    my_grad_hidden = (
        mine(cotangent).astype(F32)
        + my_scale * gained_two
        - my_hidden * my_scale**3 * jnp.mean(gained_two * my_hidden, axis=-1, keepdims=True)
    )
    small = jnp.concatenate([grad_router, grad_norm2[None]])
    extra = -small.shape[0] % 16
    small = jnp.pad(small, ((0, extra), (0, 0))).astype(BF16)
    parts = z_received(jnp.concatenate([my_grad_hidden.astype(BF16), small]))
    plane_out = plane_scatter(out_blocks)
    plane_out, grad_gate, up_weight_gradient, grad_down, *parts = tied(
        plane_out, grad_gate, up_weight_gradient, grad_down, *parts
    )
    routed = z_scatter(plane_out, axis=1)
    mixed = (piece(hidden, tensor_place, col_width, 1) + routed).astype(BF16)
    grad_branch = z_place([part[:own_rows] for part in parts])
    small = sum(part[own_rows:].astype(F32) for part in parts)
    grad_output = mm_rows(attended, grad_branch)

    grad_heads = mm_cols(grad_branch, w_output).astype(BF16)
    grad_heads = grad_heads.reshape(tok_count, heads_kv, group_size, HEAD_DIMENSION)
    grad_queries, grad_keys, grad_values = attend_backward(
        query_rows, rotated_keys, value_rows, grad_heads, log_total
    )
    grad_query_raw = rotate(
        grad_queries.reshape(tok_count, heads_query, HEAD_DIMENSION), cosine, sine_table, -1.0
    )
    grad_query_raw = grad_query_raw.reshape(tok_count, -1).astype(BF16)
    grad_key_raw = rotate(grad_keys, cosine, sine_table, -1.0)
    grad_key_raw = grad_key_raw.reshape(tok_count, -1).astype(BF16)
    grad_value_raw = grad_values.reshape(tok_count, -1).astype(BF16)
    grad_raw = jnp.concatenate([grad_query_raw, grad_key_raw, grad_value_raw], axis=1)
    grad_first = (
        mm_cols(grad_query_raw, w_query)
        + mm_cols(grad_key_raw, key_projection_weight)
        + mm_cols(grad_value_raw, value_projection_weight)
    )
    norm1_part = jnp.sum(grad_first * resid_in * first_scale, axis=0)

    grad_raw = mm_rows(first_norm, grad_raw)
    raw_width = grad_raw.shape[1]

    def folded(array):
        array = jnp.pad(array.astype(BF16), ((0, -array.shape[0] % 16), (0, 0)))
        return [array[:, i : i + raw_width] for i in range(0, model_width, raw_width)]

    pile = [grad_raw.astype(BF16)] + folded(grad_output) + folded(small) + folded(norm1_part[None])
    places = [0]
    for part in pile:
        places.append(places[-1] + part.shape[0])
    extra = -places[-1] % 128
    pile = expert_sum(jnp.concatenate(pile + [jnp.zeros((extra, raw_width), BF16)]))
    grad_weights = pile[: places[1]]
    folds = model_width // raw_width

    def unfolded(first, rows):
        return jnp.concatenate(
            [pile[places[i] : places[i] + rows] for i in range(first, first + folds)], axis=1
        )

    grad_output = unfolded(1, grad_output.shape[0])
    small = unfolded(1 + folds, experts + 1)
    grad_norm1 = sum(z_received(unfolded(1 + 2 * folds, 1)))[0]
    q_width, k_width = w_query.shape[1], key_projection_weight.shape[1]

    mixed, grad_first = tied(mixed, grad_first)
    grad_first = z_scatter(grad_first)
    gained_one = grad_first * norm1_gain
    my_resid, my_first_scale = mine(resid_in), mine(first_scale)
    my_grad_input = (
        my_grad_hidden
        + my_first_scale * gained_one
        - my_resid * my_first_scale**3 * jnp.mean(gained_one * my_resid, axis=-1, keepdims=True)
    )
    grad_input = z_place(z_received(my_grad_input.astype(BF16))).astype(F32)

    return (
        mixed,
        grad_input,
        grad_norm1,
        grad_weights[:, :q_width],
        grad_weights[:, q_width : q_width + k_width],
        grad_weights[:, q_width + k_width :],
        grad_output,
        small[experts],
        small[:experts].T,
        grad_gate,
        up_weight_gradient,
        grad_down,
    )


def solution(mesh):
    placed = (
        P("expert", None),
        P(),
        P(None, "tensor"),
        P(None, "tensor"),
        P(None, "tensor"),
        P("tensor", None),
        P(),
        P(),
        P("expert", None, "tensor"),
        P("expert", None, "tensor"),
        P("expert", "tensor", None),
        P("expert", None),
        P("expert", None),
    )
    return jax.shard_map(
        local,
        mesh=mesh,
        in_specs=placed,
        out_specs=(
            P("expert", "tensor"),
            P("expert", None),
            P(),
            P(None, "tensor"),
            P(None, "tensor"),
            P(None, "tensor"),
            P("tensor", None),
            P(),
            P(),
            P("expert", None, "tensor"),
            P("expert", None, "tensor"),
            P("expert", "tensor", None),
        ),
        check_vma=False,
    )
```

```python
import functools
import math

import jax
import jax.numpy as jnp
from jax import lax
from jax.experimental import pallas as pl
from jax.experimental.pallas import tpu as pltpu
from jax.sharding import PartitionSpec as P

HEAD_DIMENSION = 64
SEQ_LEN = 512

EPS = 1e-06
SCALE = 0.125
NEGATIVE = -1e30
THETA = 10000.0
F32 = jnp.float32
BF16 = jnp.bfloat16
EXACT = lax.Precision.HIGHEST
LANES = 128
TILE = 256


def tables(tok_count):
    half = HEAD_DIMENSION // 2
    freq = jnp.exp(-math.log(THETA) * jnp.arange(half, dtype=F32) / half)
    places = (jnp.arange(tok_count) % SEQ_LEN).astype(F32)
    angle = places[:, None] * freq[None, :]
    return (jnp.cos(angle)[:, None, :], jnp.sin(angle)[:, None, :])


def rotate(field, cosine, sine_table, factor):
    half = HEAD_DIMENSION // 2
    first = field[..., :half]
    second = field[..., half:]
    return jnp.concatenate(
        [
            first * cosine - factor * second * sine_table,
            second * cosine + factor * first * sine_table,
        ],
        axis=-1,
    )


def causal_mask():
    places = jnp.arange(SEQ_LEN)
    return places[:, None] >= places[None, :]


def attend_forward(query_rows, rotated_keys, value_rows):
    scores = (
        jnp.einsum("lkgd,mkd->kglm", query_rows, rotated_keys, preferred_element_type=F32) * SCALE
    )
    scores = jnp.where(causal_mask(), scores, NEGATIVE)
    highest = jnp.max(scores, axis=-1, keepdims=True)
    expanded = jnp.exp(scores - highest)
    summed = jnp.sum(expanded, axis=-1, keepdims=True)
    probability = (expanded / summed).astype(BF16)
    heads_out = jnp.einsum("kglm,mkd->lkgd", probability, value_rows, preferred_element_type=F32)
    return (heads_out.astype(BF16), (highest + jnp.log(summed))[..., 0])


def attend_backward(query_rows, rotated_keys, value_rows, grad_heads, log_total):
    scores = (
        jnp.einsum("lkgd,mkd->kglm", query_rows, rotated_keys, preferred_element_type=F32) * SCALE
    )
    probability = jnp.where(causal_mask(), jnp.exp(scores - log_total[..., None]), 0.0)
    prob_low = probability.astype(BF16)
    grad_values = jnp.einsum("kglm,lkgd->mkd", prob_low, grad_heads, preferred_element_type=F32)
    grad_prob = jnp.einsum("lkgd,mkd->kglm", grad_heads, value_rows, preferred_element_type=F32)
    row_delta = jnp.sum(probability * grad_prob, axis=-1, keepdims=True)
    grad_scores = (probability * (grad_prob - row_delta)).astype(BF16)
    grad_queries = (
        jnp.einsum("kglm,mkd->lkgd", grad_scores, rotated_keys, preferred_element_type=F32) * SCALE
    )
    grad_keys = (
        jnp.einsum("kglm,lkgd->mkd", grad_scores, query_rows, preferred_element_type=F32) * SCALE
    )
    return (grad_queries, grad_keys, grad_values)


def mm(left, right):
    return jnp.dot(left, right, preferred_element_type=F32)


def mm_rows(left, right):
    return lax.dot_general(left, right, (((0,), (0,)), ((), ())), preferred_element_type=F32)


def mm_cols(left, right):
    return lax.dot_general(left, right, (((1,), (1,)), ((), ())), preferred_element_type=F32)


def piece(array, index, size, axis=0):
    return lax.dynamic_slice_in_dim(array, index * size, size, axis)


def swap(array, mask):
    size = lax.axis_size("expert")
    return lax.ppermute(array, "expert", [(i, i ^ mask) for i in range(size)])


def z_shift(array, step):
    size = lax.axis_size("tensor")
    return lax.ppermute(array, "tensor", [(i, (i + step) % size) for i in range(size)])


def z_received(array):
    return [array] + [z_shift(array, step) for step in range(1, lax.axis_size("tensor"))]


def z_place(parts):
    size, mine = lax.axis_size("tensor"), lax.axis_index("tensor")
    rows = parts[0].shape[0]
    whole = jnp.zeros((rows * size,) + parts[0].shape[1:], parts[0].dtype)
    for step, part in enumerate(parts):
        whole = lax.dynamic_update_slice_in_dim(whole, part, (mine + size - step) % size * rows, 0)
    return whole


def z_scatter(array, axis=0):
    size, mine = lax.axis_size("tensor"), lax.axis_index("tensor")
    width = array.shape[axis] // size
    total = piece(array, mine, width, axis).astype(F32)
    for step in range(1, size):
        sent = piece(array, (mine + step) % size, width, axis).astype(BF16)
        total = total + z_shift(sent, step).astype(F32)
    return total


def same_core_groups():
    size = lax.axis_size("expert")
    return [list(range(0, size, 2)), list(range(1, size, 2))]


def plane_gather(array):
    if lax.axis_size("expert") != 8:
        return [
            lax.all_gather(
                array, "expert", axis=0, tiled=True, axis_index_groups=same_core_groups()
            )
        ]
    half = array.shape[0] // 2
    from_x = swap(array, 2)
    from_y = swap(array, 4)
    return [array, from_x, from_y, swap(from_x[:half], 4), swap(from_y[half:], 2)]


def plane_scatter(blocks):
    if lax.axis_size("expert") != 8:
        return lax.psum_scatter(
            blocks[0].astype(BF16),
            "expert",
            scatter_dimension=0,
            tiled=True,
            axis_index_groups=same_core_groups(),
        ).astype(F32)
    own, for_x, for_y, far_x, far_y = blocks
    half = own.shape[0] // 2
    via_x = swap(far_x, 2).astype(F32)
    via_y = swap(far_y, 4).astype(F32)
    for_y = for_y.at[:half].set((for_y[:half].astype(F32) + via_x).astype(BF16))
    for_x = for_x.at[half:].set((for_x[half:].astype(F32) + via_y).astype(BF16))
    return own.astype(F32) + swap(for_x, 2).astype(F32) + swap(for_y, 4).astype(F32)


def expert_sum(array):
    if lax.axis_size("expert") != 8:
        return lax.psum(array.astype(BF16), "expert").astype(F32)
    place = lax.axis_index("expert")
    core, chip = place % 2, place // 2
    half = array.shape[0] // 2
    rows = half // 4
    array = array.astype(BF16)
    mine = piece(array, core, half).astype(F32)
    mine = mine + swap(piece(array, 1 - core, half), 1).astype(F32)
    total = piece(mine, chip, rows)
    for mask in (1, 2, 3):
        total = total + swap(piece(mine, chip ^ mask, rows).astype(BF16), 2 * mask).astype(F32)
    total = total.astype(BF16)
    gathered = jnp.zeros((half,) + array.shape[1:], BF16)
    for mask in (0, 1, 2, 3):
        part = swap(total, 2 * mask) if mask else total
        gathered = lax.dynamic_update_slice_in_dim(gathered, part, (chip ^ mask) * rows, 0)
    both = jnp.concatenate([gathered, gathered])
    both = lax.dynamic_update_slice_in_dim(both, swap(gathered, 1), (1 - core) * half, 0)
    return both.astype(F32)


def expert_kernel(
    experts,
    top_count,
    units,
    names_ref,
    normed_ref,
    grad_ref,
    router_ref,
    gate_ref,
    up_ref,
    down_ref,
    out_ref,
    rows_ref,
    gate_grad_ref,
    up_grad_ref,
    inner_ref,
):
    tile, model_width = normed_ref.shape
    width = gate_ref.shape[1]
    normed = normed_ref[...]
    grad = grad_ref[:, :model_width]
    chosen_names = grad_ref[:, model_width:].astype(F32)
    lane = lax.broadcasted_iota(jnp.int32, (tile, LANES), 1)
    lane_float = lane.astype(F32)
    chosen = lane_float == chosen_names[:, 0:1]
    for k in range(1, top_count):
        chosen = chosen | (lane_float == chosen_names[:, k : k + 1])
    logits = jnp.where(chosen, mm(normed, router_ref[...]), NEGATIVE)
    expanded = jnp.exp(logits - jnp.max(logits, axis=-1, keepdims=True))
    expanded = jnp.where(chosen, expanded, 0.0)
    routing = expanded / jnp.sum(expanded, axis=-1, keepdims=True)
    grad_routing = jnp.zeros((tile, LANES), F32)
    columns = min(TILE, width)
    for start in range(0, width, columns):
        part = slice(start, start + columns)
        gate_act = mm(normed, gate_ref[:, part])
        up_act = mm(normed, up_ref[:, part])
        grad_plain = mm_cols(grad, down_ref[part, :])
        weights = []
        for e in range(start // units, (start + columns) // units):
            weight = jnp.sum(
                jnp.where(lane == names_ref[e], routing, 0.0), axis=-1, keepdims=True
            )
            weights.append(jnp.broadcast_to(weight, (tile, units)))
        wide = jnp.concatenate(weights, axis=1) if len(weights) > 1 else weights[0]
        sigmoid_gate = jax.nn.sigmoid(gate_act)
        swish = gate_act * sigmoid_gate
        inner = swish * up_act
        inner_grad = inner * grad_plain
        for i, e in enumerate(range(start // units, (start + columns) // units)):
            total = jnp.sum(inner_grad[:, i * units : (i + 1) * units], axis=-1, keepdims=True)
            grad_routing = jnp.where(lane == names_ref[e], total, grad_routing)
        grad_inner = grad_plain * wide
        inner_ref[:, part] = (inner * wide).astype(BF16)
        up_grad_ref[:, part] = (grad_inner * swish).astype(BF16)
        gate_grad_ref[:, part] = (
            grad_inner * up_act * (sigmoid_gate + swish * (1.0 - sigmoid_gate))
        ).astype(BF16)
    rounded = grad_routing.astype(BF16).astype(F32)
    left = pltpu.roll(grad_routing - rounded, experts, 1)
    rows_ref[:, model_width:] = (rounded + left).astype(BF16)
    rows_ref[:, :model_width] = (
        mm_cols(gate_grad_ref[...], gate_ref[...]) + mm_cols(up_grad_ref[...], up_ref[...])
    ).astype(BF16)
    out_ref[...] = mm(inner_ref[...], down_ref[...]).astype(BF16)


def expert_block(names, normed, grad, router, gate_w, up_w, down_w, experts, top_count, units):
    rows, model_width = normed.shape
    width = gate_w.shape[1]
    tile = min(TILE, rows)

    def tiled(columns):
        return pl.BlockSpec((tile, columns), lambda i, names: (i, 0))

    def fixed(array):
        return pl.BlockSpec(array.shape, lambda i, names: (0, 0))

    def shaped(columns):
        return jax.ShapeDtypeStruct((rows, columns), BF16)

    return pl.pallas_call(
        functools.partial(expert_kernel, experts, top_count, units),
        grid_spec=pltpu.PrefetchScalarGridSpec(
            num_scalar_prefetch=1,
            grid=(rows // tile,),
            in_specs=[
                tiled(model_width),
                tiled(model_width + LANES),
                fixed(router),
                fixed(gate_w),
                fixed(up_w),
                fixed(down_w),
            ],
            out_specs=[
                tiled(model_width),
                tiled(model_width + LANES),
                tiled(width),
                tiled(width),
                tiled(width),
            ],
        ),
        out_shape=[
            shaped(model_width),
            shaped(model_width + LANES),
            shaped(width),
            shaped(width),
            shaped(width),
        ],
        compiler_params=pltpu.CompilerParams(vmem_limit_bytes=44 * 1024 * 1024),
        cost_estimate=pl.CostEstimate(
            flops=12 * rows * model_width * width,
            bytes_accessed=6 * model_width * width + 14 * rows * model_width,
            transcendentals=rows * width,
        ),
        name="experts",
    )(names, normed, grad, router, gate_w, up_w, down_w)


def tied(*arrays):
    return lax.optimization_barrier(arrays)


def norm_scale(field):
    return lax.rsqrt(jnp.mean(field * field, axis=-1, keepdims=True) + EPS)


def route(normed, router, chosen):
    logits = mm(normed, router)
    masked = jnp.where(chosen, logits, NEGATIVE)
    highest = jnp.max(masked, axis=-1, keepdims=True)
    expanded = jnp.where(chosen, jnp.exp(masked - highest), 0.0)
    return expanded / jnp.sum(expanded, axis=-1, keepdims=True)


def local(
    tokens,
    norm1_gain,
    w_query,
    key_projection_weight,
    value_projection_weight,
    w_output,
    norm2_gain,
    w_router,
    expert_gate_weight,
    expert_up_weight,
    expert_down_weight,
    expert_ids,
    cotangent,
):
    tok_count = tokens.shape[0]
    model_width = tokens.shape[1]
    experts, top_count = w_router.shape[1], expert_ids.shape[1]
    here, units = expert_gate_weight.shape[0], expert_gate_weight.shape[2]
    heads_query = w_query.shape[1] // HEAD_DIMENSION
    heads_kv = key_projection_weight.shape[1] // HEAD_DIMENSION
    group_size = heads_query // heads_kv
    cosine, sine_table = tables(tok_count)
    expert_count = lax.axis_size("expert")
    tensor_count = lax.axis_size("tensor")
    expert_place = lax.axis_index("expert")
    tensor_place = lax.axis_index("tensor")
    core = expert_place % 2
    own_rows = tok_count // tensor_count
    col_width = model_width // tensor_count

    names_wide = jnp.pad(expert_ids.astype(BF16), ((0, 0), (0, LANES - top_count)))
    grad_blocks = plane_gather(jnp.concatenate([cotangent, names_wide], axis=1))
    if expert_count == 8:
        grad_blocks, grad_far = grad_blocks[:3], grad_blocks[3:]

    half = w_output.shape[0] // 2
    w_halves = [z_shift(piece(w_output, core, half), step) for step in range(1, tensor_count)]
    expert_weights = [expert_gate_weight, expert_up_weight, expert_down_weight]
    if expert_count == 8:
        grad_blocks, w_halves = tied(grad_blocks, w_halves)
    w_halves = jnp.stack(w_halves)
    w_others = swap(w_halves, 1)
    w_parts = jnp.where(
        core == 0,
        jnp.concatenate([w_halves, w_others], axis=1),
        jnp.concatenate([w_others, w_halves], axis=1),
    )

    resid_in = tokens.astype(F32)
    first_scale = norm_scale(resid_in)
    first_norm = (resid_in * first_scale * norm1_gain).astype(BF16)
    query_raw = mm(first_norm, w_query).reshape(tok_count, heads_query, HEAD_DIMENSION)
    key_raw = mm(first_norm, key_projection_weight).reshape(tok_count, heads_kv, HEAD_DIMENSION)
    query_rows = (
        rotate(query_raw, cosine, sine_table, 1.0)
        .astype(BF16)
        .reshape(tok_count, heads_kv, group_size, HEAD_DIMENSION)
    )
    rotated_keys = rotate(key_raw, cosine, sine_table, 1.0).astype(BF16)
    value_rows = (
        mm(first_norm, value_projection_weight)
        .astype(BF16)
        .reshape(tok_count, heads_kv, HEAD_DIMENSION)
    )
    attended, log_total = attend_forward(query_rows, rotated_keys, value_rows)
    attended = attended.reshape(tok_count, heads_query * HEAD_DIMENSION)

    attended_parts = z_received(attended)

    resid_in, attended_parts, expert_weights, w_parts = tied(
        resid_in, attended_parts, expert_weights, w_parts
    )
    other_weights = [swap(weight, 1) for weight in expert_weights]
    attended = attended_parts[0]

    def as_columns(weight):
        return weight.transpose(1, 0, 2).reshape(model_width, -1)

    chip_weights = [jnp.concatenate(pair) for pair in zip(expert_weights, other_weights)]
    gate_w, up_w = as_columns(chip_weights[0]), as_columns(chip_weights[1])
    down_w = chip_weights[2].reshape(-1, model_width)
    hidden = resid_in + mm(attended, w_output)
    for step in range(1, tensor_count):
        hidden = hidden + mm(attended_parts[step], w_parts[step - 1])
    second_scale = norm_scale(hidden)
    second_norm = (hidden * second_scale * norm2_gain).astype(BF16)

    local_names = jnp.concatenate(
        [
            expert_place * here + jnp.arange(here, dtype=jnp.int32),
            (expert_place ^ 1) * here + jnp.arange(here, dtype=jnp.int32),
        ]
    )
    router_wide = jnp.pad(w_router, ((0, 0), (0, LANES - experts)))
    if expert_count == 8:
        second_norm, grad_far = tied(second_norm, grad_far)
        grad_blocks = grad_blocks + grad_far
    normed_blocks = plane_gather(second_norm)
    done = [
        expert_block(
            local_names,
            normed,
            grad,
            router_wide,
            gate_w,
            up_w,
            down_w,
            experts,
            top_count,
            units,
        )
        for normed, grad in zip(normed_blocks, grad_blocks)
    ]
    plane_rows = plane_scatter([block[1] for block in done])
    plane_rows, *out_blocks = tied(plane_rows, *[block[0] for block in done])
    held = tied(*[array for block in done for array in block[2:]])
    done = [held[3 * i : 3 * i + 3] for i in range(len(done))]
    gate_total = up_total = down_total = 0.0
    for normed, grad, block in zip(normed_blocks, grad_blocks, done):
        gate_total = gate_total + mm_rows(normed, block[0])
        up_total = up_total + mm_rows(normed, block[1])
        down_total = down_total + mm_rows(block[2], grad[:, :model_width])

    row_sum = z_scatter(plane_rows)
    plane_out = plane_scatter(out_blocks)
    row_sum, gate_total, up_total, down_total = tied(row_sum, gate_total, up_total, down_total)

    width = here * units

    def from_chip(total):
        return total[:, :width] + swap(total[:, width:].astype(BF16), 1).astype(F32)

    def as_experts(total):
        return total.reshape(model_width, here, units).transpose(1, 0, 2)

    grad_gate = as_experts(from_chip(gate_total))
    up_weight_gradient = as_experts(from_chip(up_total))
    grad_down = down_total[:width] + swap(down_total[width:].astype(BF16), 1).astype(F32)
    grad_down = grad_down.reshape(here, units, model_width)
    my_routing_grad = (
        row_sum[:, model_width : model_width + experts]
        + row_sum[:, model_width + experts : model_width + 2 * experts]
    )
    row_sum = row_sum[:, :model_width]

    def mine(array):
        return piece(array, tensor_place, own_rows)

    my_hidden, my_scale = mine(hidden), mine(second_scale)
    my_normed = mine(second_norm)
    names = jnp.arange(experts, dtype=jnp.int32)
    my_chosen = jnp.any(mine(expert_ids)[:, :, None] == names[None, None, :], axis=1)
    my_routing = route(my_normed, w_router, my_chosen)
    my_normed = my_normed.astype(F32)
    my_logits = my_routing * (
        my_routing_grad - jnp.sum(my_routing * my_routing_grad, axis=-1, keepdims=True)
    )
    router_float = w_router.astype(F32)
    grad_second = row_sum + jnp.dot(my_logits, router_float.T, precision=EXACT)
    grad_router = lax.dot_general(
        my_logits, my_normed, (((0,), (0,)), ((), ())), precision=EXACT
    )
    grad_norm2 = jnp.sum(grad_second * my_hidden * my_scale, axis=0)
    gained_two = grad_second * norm2_gain
    my_grad_hidden = (
        mine(cotangent).astype(F32)
        + my_scale * gained_two
        - my_hidden * my_scale**3 * jnp.mean(gained_two * my_hidden, axis=-1, keepdims=True)
    )
    small = jnp.concatenate([grad_router, grad_norm2[None]])
    extra = -small.shape[0] % 16
    small = jnp.pad(small, ((0, extra), (0, 0))).astype(BF16)
    parts = z_received(jnp.concatenate([my_grad_hidden.astype(BF16), small]))
    grad_gate, up_weight_gradient, grad_down, *parts = tied(
        grad_gate, up_weight_gradient, grad_down, *parts
    )
    routed = z_scatter(plane_out, axis=1)
    mixed = (piece(hidden, tensor_place, col_width, 1) + routed).astype(BF16)
    grad_branch = z_place([part[:own_rows] for part in parts])
    small = sum(part[own_rows:].astype(F32) for part in parts)
    grad_output = mm_rows(attended, grad_branch)

    grad_heads = mm_cols(grad_branch, w_output).astype(BF16)
    grad_heads = grad_heads.reshape(tok_count, heads_kv, group_size, HEAD_DIMENSION)
    grad_queries, grad_keys, grad_values = attend_backward(
        query_rows, rotated_keys, value_rows, grad_heads, log_total
    )
    grad_query_raw = rotate(
        grad_queries.reshape(tok_count, heads_query, HEAD_DIMENSION), cosine, sine_table, -1.0
    )
    grad_query_raw = grad_query_raw.reshape(tok_count, -1).astype(BF16)
    grad_key_raw = rotate(grad_keys, cosine, sine_table, -1.0)
    grad_key_raw = grad_key_raw.reshape(tok_count, -1).astype(BF16)
    grad_value_raw = grad_values.reshape(tok_count, -1).astype(BF16)
    grad_raw = jnp.concatenate([grad_query_raw, grad_key_raw, grad_value_raw], axis=1)
    grad_first = (
        mm_cols(grad_query_raw, w_query)
        + mm_cols(grad_key_raw, key_projection_weight)
        + mm_cols(grad_value_raw, value_projection_weight)
    )
    norm1_part = sum(z_received(jnp.sum(grad_first * resid_in * first_scale, axis=0)[None]))

    grad_raw = mm_rows(first_norm, grad_raw)
    raw_width = grad_raw.shape[1]

    def folded(array):
        array = jnp.pad(array.astype(BF16), ((0, -array.shape[0] % 16), (0, 0)))
        return [array[:, i : i + raw_width] for i in range(0, model_width, raw_width)]

    pile = [grad_raw.astype(BF16)] + folded(grad_output) + folded(small) + folded(norm1_part)
    places = [0]
    for part in pile:
        places.append(places[-1] + part.shape[0])
    extra = -places[-1] % 128
    pile = expert_sum(jnp.concatenate(pile + [jnp.zeros((extra, raw_width), BF16)]))
    grad_weights = pile[: places[1]]
    folds = model_width // raw_width

    def unfolded(first, rows):
        return jnp.concatenate(
            [pile[places[i] : places[i] + rows] for i in range(first, first + folds)], axis=1
        )

    grad_output = unfolded(1, grad_output.shape[0])
    small = unfolded(1 + folds, experts + 1)
    grad_norm1 = unfolded(1 + 2 * folds, 1)[0]
    q_width, k_width = w_query.shape[1], key_projection_weight.shape[1]

    mixed, grad_first = tied(mixed, grad_first)
    grad_first = z_scatter(grad_first)
    gained_one = grad_first * norm1_gain
    my_resid, my_first_scale = mine(resid_in), mine(first_scale)
    my_grad_input = (
        my_grad_hidden
        + my_first_scale * gained_one
        - my_resid * my_first_scale**3 * jnp.mean(gained_one * my_resid, axis=-1, keepdims=True)
    )
    grad_input = z_place(z_received(my_grad_input.astype(BF16))).astype(F32)

    return (
        mixed,
        grad_input,
        grad_norm1,
        grad_weights[:, :q_width],
        grad_weights[:, q_width : q_width + k_width],
        grad_weights[:, q_width + k_width :],
        grad_output,
        small[experts],
        small[:experts].T,
        grad_gate,
        up_weight_gradient,
        grad_down,
    )


def solution(mesh):
    placed = (
        P("expert", None),
        P(),
        P(None, "tensor"),
        P(None, "tensor"),
        P(None, "tensor"),
        P("tensor", None),
        P(),
        P(),
        P("expert", None, "tensor"),
        P("expert", None, "tensor"),
        P("expert", "tensor", None),
        P("expert", None),
        P("expert", None),
    )
    return jax.shard_map(
        local,
        mesh=mesh,
        in_specs=placed,
        out_specs=(
            P("expert", "tensor"),
            P("expert", None),
            P(),
            P(None, "tensor"),
            P(None, "tensor"),
            P(None, "tensor"),
            P("tensor", None),
            P(),
            P(),
            P("expert", None, "tensor"),
            P("expert", None, "tensor"),
            P("expert", "tensor", None),
        ),
        check_vma=False,
    )
```

```python
import functools
import math

import jax
import jax.numpy as jnp
from jax import lax
from jax.experimental import pallas as pl
from jax.experimental.pallas import tpu as pltpu
from jax.sharding import PartitionSpec as P

HEAD_DIMENSION = 64
SEQ_LEN = 512

EPS = 1e-06
SCALE = 0.125
NEGATIVE = -1e30
THETA = 10000.0
F32 = jnp.float32
BF16 = jnp.bfloat16
EXACT = lax.Precision.HIGHEST
LANES = 128
TILE = 256


def tables(tok_count):
    half = HEAD_DIMENSION // 2
    freq = jnp.exp(-math.log(THETA) * jnp.arange(half, dtype=F32) / half)
    places = (jnp.arange(tok_count) % SEQ_LEN).astype(F32)
    angle = places[:, None] * freq[None, :]
    return (jnp.cos(angle)[:, None, :], jnp.sin(angle)[:, None, :])


def rotate(field, cosine, sine_table, factor):
    half = HEAD_DIMENSION // 2
    first = field[..., :half]
    second = field[..., half:]
    return jnp.concatenate(
        [
            first * cosine - factor * second * sine_table,
            second * cosine + factor * first * sine_table,
        ],
        axis=-1,
    )


def causal_mask():
    places = jnp.arange(SEQ_LEN)
    return places[:, None] >= places[None, :]


def attend_forward(query_rows, rotated_keys, value_rows):
    scores = (
        jnp.einsum("lkgd,mkd->kglm", query_rows, rotated_keys, preferred_element_type=F32) * SCALE
    )
    scores = jnp.where(causal_mask(), scores, NEGATIVE)
    highest = jnp.max(scores, axis=-1, keepdims=True)
    expanded = jnp.exp(scores - highest)
    summed = jnp.sum(expanded, axis=-1, keepdims=True)
    probability = (expanded / summed).astype(BF16)
    heads_out = jnp.einsum("kglm,mkd->lkgd", probability, value_rows, preferred_element_type=F32)
    return (heads_out.astype(BF16), (highest + jnp.log(summed))[..., 0])


def attend_backward(query_rows, rotated_keys, value_rows, grad_heads, log_total):
    scores = (
        jnp.einsum("lkgd,mkd->kglm", query_rows, rotated_keys, preferred_element_type=F32) * SCALE
    )
    probability = jnp.where(causal_mask(), jnp.exp(scores - log_total[..., None]), 0.0)
    prob_low = probability.astype(BF16)
    grad_values = jnp.einsum("kglm,lkgd->mkd", prob_low, grad_heads, preferred_element_type=F32)
    grad_prob = jnp.einsum("lkgd,mkd->kglm", grad_heads, value_rows, preferred_element_type=F32)
    row_delta = jnp.sum(probability * grad_prob, axis=-1, keepdims=True)
    grad_scores = (probability * (grad_prob - row_delta)).astype(BF16)
    grad_queries = (
        jnp.einsum("kglm,mkd->lkgd", grad_scores, rotated_keys, preferred_element_type=F32) * SCALE
    )
    grad_keys = (
        jnp.einsum("kglm,lkgd->mkd", grad_scores, query_rows, preferred_element_type=F32) * SCALE
    )
    return (grad_queries, grad_keys, grad_values)


def mm(left, right):
    return jnp.dot(left, right, preferred_element_type=F32)


def mm_rows(left, right):
    return lax.dot_general(left, right, (((0,), (0,)), ((), ())), preferred_element_type=F32)


def mm_cols(left, right):
    return lax.dot_general(left, right, (((1,), (1,)), ((), ())), preferred_element_type=F32)


def piece(array, index, size, axis=0):
    return lax.dynamic_slice_in_dim(array, index * size, size, axis)


def swap(array, mask):
    size = lax.axis_size("expert")
    return lax.ppermute(array, "expert", [(i, i ^ mask) for i in range(size)])


def z_shift(array, step):
    size = lax.axis_size("tensor")
    return lax.ppermute(array, "tensor", [(i, (i + step) % size) for i in range(size)])


def z_received(array):
    return [array] + [z_shift(array, step) for step in range(1, lax.axis_size("tensor"))]


def z_place(parts):
    size, mine = lax.axis_size("tensor"), lax.axis_index("tensor")
    rows = parts[0].shape[0]
    whole = jnp.zeros((rows * size,) + parts[0].shape[1:], parts[0].dtype)
    for step, part in enumerate(parts):
        whole = lax.dynamic_update_slice_in_dim(whole, part, (mine + size - step) % size * rows, 0)
    return whole


def z_scatter(array, axis=0):
    size, mine = lax.axis_size("tensor"), lax.axis_index("tensor")
    width = array.shape[axis] // size
    total = piece(array, mine, width, axis).astype(F32)
    for step in range(1, size):
        sent = piece(array, (mine + step) % size, width, axis).astype(BF16)
        total = total + z_shift(sent, step).astype(F32)
    return total


def same_core_groups():
    size = lax.axis_size("expert")
    return [list(range(0, size, 2)), list(range(1, size, 2))]


def plane_gather(array):
    if lax.axis_size("expert") != 8:
        return [
            lax.all_gather(
                array, "expert", axis=0, tiled=True, axis_index_groups=same_core_groups()
            )
        ]
    half = array.shape[0] // 2
    from_x = swap(array, 2)
    from_y = swap(array, 4)
    return [array, from_x, from_y, swap(from_x[:half], 4), swap(from_y[half:], 2)]


def plane_scatter(blocks):
    if lax.axis_size("expert") != 8:
        return lax.psum_scatter(
            blocks[0].astype(BF16),
            "expert",
            scatter_dimension=0,
            tiled=True,
            axis_index_groups=same_core_groups(),
        ).astype(F32), ()
    own, for_x, for_y, far_x, far_y = blocks
    half = own.shape[0] // 2
    via_x = swap(far_x, 2).astype(F32)
    via_y = swap(far_y, 4).astype(F32)
    for_y = for_y.at[:half].set((for_y[:half].astype(F32) + via_x).astype(BF16))
    for_x = for_x.at[half:].set((for_x[half:].astype(F32) + via_y).astype(BF16))
    total = own.astype(F32) + swap(for_x, 2).astype(F32) + swap(for_y, 4).astype(F32)
    return total, (for_x, for_y)


def expert_sum(array):
    if lax.axis_size("expert") != 8:
        return lax.psum(array.astype(BF16), "expert").astype(F32)
    place = lax.axis_index("expert")
    core, chip = place % 2, place // 2
    half = array.shape[0] // 2
    rows = half // 4
    array = array.astype(BF16)
    mine = piece(array, core, half).astype(F32)
    mine = mine + swap(piece(array, 1 - core, half), 1).astype(F32)
    total = piece(mine, chip, rows)
    for mask in (1, 2, 3):
        total = total + swap(piece(mine, chip ^ mask, rows).astype(BF16), 2 * mask).astype(F32)
    total = total.astype(BF16)
    gathered = jnp.zeros((half,) + array.shape[1:], BF16)
    for mask in (0, 1, 2, 3):
        part = swap(total, 2 * mask) if mask else total
        gathered = lax.dynamic_update_slice_in_dim(gathered, part, (chip ^ mask) * rows, 0)
    both = jnp.concatenate([gathered, gathered])
    both = lax.dynamic_update_slice_in_dim(both, swap(gathered, 1), (1 - core) * half, 0)
    return both.astype(F32)


def expert_kernel(
    experts,
    top_count,
    units,
    names_ref,
    normed_ref,
    grad_ref,
    router_ref,
    gate_ref,
    up_ref,
    down_ref,
    out_ref,
    rows_ref,
    gate_grad_ref,
    up_grad_ref,
    inner_ref,
):
    tile, model_width = normed_ref.shape
    width = gate_ref.shape[1]
    normed = normed_ref[...]
    grad = grad_ref[:, :model_width]
    chosen_names = grad_ref[:, model_width:].astype(F32)
    lane = lax.broadcasted_iota(jnp.int32, (tile, LANES), 1)
    lane_float = lane.astype(F32)
    chosen = lane_float == chosen_names[:, 0:1]
    for k in range(1, top_count):
        chosen = chosen | (lane_float == chosen_names[:, k : k + 1])
    logits = jnp.where(chosen, mm(normed, router_ref[...]), NEGATIVE)
    expanded = jnp.exp(logits - jnp.max(logits, axis=-1, keepdims=True))
    expanded = jnp.where(chosen, expanded, 0.0)
    routing = expanded / jnp.sum(expanded, axis=-1, keepdims=True)
    grad_routing = jnp.zeros((tile, LANES), F32)
    columns = min(TILE, width)
    for start in range(0, width, columns):
        part = slice(start, start + columns)
        gate_act = mm(normed, gate_ref[:, part])
        up_act = mm(normed, up_ref[:, part])
        grad_plain = mm_cols(grad, down_ref[part, :])
        weights = []
        for e in range(start // units, (start + columns) // units):
            weight = jnp.sum(
                jnp.where(lane == names_ref[e], routing, 0.0), axis=-1, keepdims=True
            )
            weights.append(jnp.broadcast_to(weight, (tile, units)))
        wide = jnp.concatenate(weights, axis=1) if len(weights) > 1 else weights[0]
        sigmoid_gate = jax.nn.sigmoid(gate_act)
        swish = gate_act * sigmoid_gate
        inner = swish * up_act
        inner_grad = inner * grad_plain
        for i, e in enumerate(range(start // units, (start + columns) // units)):
            total = jnp.sum(inner_grad[:, i * units : (i + 1) * units], axis=-1, keepdims=True)
            grad_routing = jnp.where(lane == names_ref[e], total, grad_routing)
        grad_inner = grad_plain * wide
        inner_ref[:, part] = (inner * wide).astype(BF16)
        up_grad_ref[:, part] = (grad_inner * swish).astype(BF16)
        gate_grad_ref[:, part] = (
            grad_inner * up_act * (sigmoid_gate + swish * (1.0 - sigmoid_gate))
        ).astype(BF16)
    rounded = grad_routing.astype(BF16).astype(F32)
    left = pltpu.roll(grad_routing - rounded, experts, 1)
    rows_ref[:, model_width:] = (rounded + left).astype(BF16)
    rows_ref[:, :model_width] = (
        mm_cols(gate_grad_ref[...], gate_ref[...]) + mm_cols(up_grad_ref[...], up_ref[...])
    ).astype(BF16)
    out_ref[...] = mm(inner_ref[...], down_ref[...]).astype(BF16)


def expert_block(names, normed, grad, router, gate_w, up_w, down_w, experts, top_count, units):
    rows, model_width = normed.shape
    width = gate_w.shape[1]
    tile = min(TILE, rows)

    def tiled(columns):
        return pl.BlockSpec((tile, columns), lambda i, names: (i, 0))

    def fixed(array):
        return pl.BlockSpec(array.shape, lambda i, names: (0, 0))

    def shaped(columns):
        return jax.ShapeDtypeStruct((rows, columns), BF16)

    return pl.pallas_call(
        functools.partial(expert_kernel, experts, top_count, units),
        grid_spec=pltpu.PrefetchScalarGridSpec(
            num_scalar_prefetch=1,
            grid=(rows // tile,),
            in_specs=[
                tiled(model_width),
                tiled(model_width + LANES),
                fixed(router),
                fixed(gate_w),
                fixed(up_w),
                fixed(down_w),
            ],
            out_specs=[
                tiled(model_width),
                tiled(model_width + LANES),
                tiled(width),
                tiled(width),
                tiled(width),
            ],
        ),
        out_shape=[
            shaped(model_width),
            shaped(model_width + LANES),
            shaped(width),
            shaped(width),
            shaped(width),
        ],
        compiler_params=pltpu.CompilerParams(vmem_limit_bytes=44 * 1024 * 1024),
        cost_estimate=pl.CostEstimate(
            flops=12 * rows * model_width * width,
            bytes_accessed=6 * model_width * width + 14 * rows * model_width,
            transcendentals=rows * width,
        ),
        name="experts",
    )(names, normed, grad, router, gate_w, up_w, down_w)


def tied(*arrays):
    return lax.optimization_barrier(arrays)


def norm_scale(field):
    return lax.rsqrt(jnp.mean(field * field, axis=-1, keepdims=True) + EPS)


def route(normed, router, chosen):
    logits = mm(normed, router)
    masked = jnp.where(chosen, logits, NEGATIVE)
    highest = jnp.max(masked, axis=-1, keepdims=True)
    expanded = jnp.where(chosen, jnp.exp(masked - highest), 0.0)
    return expanded / jnp.sum(expanded, axis=-1, keepdims=True)


def local(
    tokens,
    norm1_gain,
    w_query,
    key_projection_weight,
    value_projection_weight,
    w_output,
    norm2_gain,
    w_router,
    expert_gate_weight,
    expert_up_weight,
    expert_down_weight,
    expert_ids,
    cotangent,
):
    tok_count = tokens.shape[0]
    model_width = tokens.shape[1]
    experts, top_count = w_router.shape[1], expert_ids.shape[1]
    here, units = expert_gate_weight.shape[0], expert_gate_weight.shape[2]
    heads_query = w_query.shape[1] // HEAD_DIMENSION
    heads_kv = key_projection_weight.shape[1] // HEAD_DIMENSION
    group_size = heads_query // heads_kv
    cosine, sine_table = tables(tok_count)
    expert_count = lax.axis_size("expert")
    tensor_count = lax.axis_size("tensor")
    expert_place = lax.axis_index("expert")
    tensor_place = lax.axis_index("tensor")
    core = expert_place % 2
    own_rows = tok_count // tensor_count
    col_width = model_width // tensor_count

    names_wide = jnp.pad(expert_ids.astype(BF16), ((0, 0), (0, LANES - top_count)))
    grad_blocks = plane_gather(jnp.concatenate([cotangent, names_wide], axis=1))
    if expert_count == 8:
        grad_blocks, grad_far = grad_blocks[:3], grad_blocks[3:]

    half = w_output.shape[0] // 2
    w_halves = [z_shift(piece(w_output, core, half), step) for step in range(1, tensor_count)]
    expert_weights = [expert_gate_weight, expert_up_weight, expert_down_weight]
    if expert_count == 8:
        w_halves, expert_weights = tied(w_halves, expert_weights)
    other_weights = [swap(weight, 1) for weight in expert_weights]
    if expert_count == 8:
        grad_blocks, w_halves = tied(grad_blocks, w_halves)
    w_halves = jnp.stack(w_halves)
    w_others = swap(w_halves, 1)
    w_parts = jnp.where(
        core == 0,
        jnp.concatenate([w_halves, w_others], axis=1),
        jnp.concatenate([w_others, w_halves], axis=1),
    )

    resid_in = tokens.astype(F32)
    first_scale = norm_scale(resid_in)
    first_norm = (resid_in * first_scale * norm1_gain).astype(BF16)
    query_raw = mm(first_norm, w_query).reshape(tok_count, heads_query, HEAD_DIMENSION)
    key_raw = mm(first_norm, key_projection_weight).reshape(tok_count, heads_kv, HEAD_DIMENSION)
    query_rows = (
        rotate(query_raw, cosine, sine_table, 1.0)
        .astype(BF16)
        .reshape(tok_count, heads_kv, group_size, HEAD_DIMENSION)
    )
    rotated_keys = rotate(key_raw, cosine, sine_table, 1.0).astype(BF16)
    value_rows = (
        mm(first_norm, value_projection_weight)
        .astype(BF16)
        .reshape(tok_count, heads_kv, HEAD_DIMENSION)
    )
    attended, log_total = attend_forward(query_rows, rotated_keys, value_rows)
    attended = attended.reshape(tok_count, heads_query * HEAD_DIMENSION)

    attended, other_weights = tied(attended, other_weights)
    attended_parts = z_received(attended)

    resid_in, attended_parts, other_weights, w_parts = tied(
        resid_in, attended_parts, other_weights, w_parts
    )
    attended = attended_parts[0]

    def as_columns(weight):
        return weight.transpose(1, 0, 2).reshape(model_width, -1)

    chip_weights = [jnp.concatenate(pair) for pair in zip(expert_weights, other_weights)]
    gate_w, up_w = as_columns(chip_weights[0]), as_columns(chip_weights[1])
    down_w = chip_weights[2].reshape(-1, model_width)
    hidden = resid_in + mm(attended, w_output)
    for step in range(1, tensor_count):
        hidden = hidden + mm(attended_parts[step], w_parts[step - 1])
    second_scale = norm_scale(hidden)
    second_norm = (hidden * second_scale * norm2_gain).astype(BF16)

    local_names = jnp.concatenate(
        [
            expert_place * here + jnp.arange(here, dtype=jnp.int32),
            (expert_place ^ 1) * here + jnp.arange(here, dtype=jnp.int32),
        ]
    )
    router_wide = jnp.pad(w_router, ((0, 0), (0, LANES - experts)))
    if expert_count == 8:
        second_norm, grad_far = tied(second_norm, grad_far)
        grad_blocks = grad_blocks + grad_far

    def through_experts(normed, grad):
        return expert_block(
            local_names,
            normed,
            grad,
            router_wide,
            gate_w,
            up_w,
            down_w,
            experts,
            top_count,
            units,
        )

    if expert_count == 8:
        half = tok_count // 2
        from_x, from_y = swap(second_norm, 2), swap(second_norm, 4)
        own_done = through_experts(second_norm, grad_blocks[0])
        from_x, from_y, own_done = tied(from_x, from_y, own_done)
        normed_blocks = [
            second_norm, from_x, from_y, swap(from_x[:half], 4), swap(from_y[half:], 2)
        ]
        done = [own_done]
    else:
        normed_blocks = plane_gather(second_norm)
        done = []
    for normed, grad in list(zip(normed_blocks, grad_blocks))[len(done) :]:
        done.append(through_experts(normed, grad))
    plane_rows, merged = plane_scatter([block[1] for block in done])
    plane_rows, *out_blocks = tied(plane_rows, *[block[0] for block in done])
    held, merged = tied([array for block in done for array in block[2:]], merged)
    done = [held[3 * i : 3 * i + 3] for i in range(len(done))]
    gate_total = up_total = down_total = 0.0
    for normed, grad, block in zip(normed_blocks, grad_blocks, done):
        gate_total = gate_total + mm_rows(normed, block[0])
        up_total = up_total + mm_rows(normed, block[1])
        down_total = down_total + mm_rows(block[2], grad[:, :model_width])

    row_sum = z_scatter(plane_rows)
    plane_out, _ = plane_scatter(out_blocks)
    row_sum, gate_total, up_total, down_total = tied(row_sum, gate_total, up_total, down_total)

    width = here * units

    def from_chip(total):
        return total[:, :width] + swap(total[:, width:].astype(BF16), 1).astype(F32)

    def as_experts(total):
        return total.reshape(model_width, here, units).transpose(1, 0, 2)

    grad_gate = as_experts(from_chip(gate_total))
    up_weight_gradient = as_experts(from_chip(up_total))
    grad_down = down_total[:width] + swap(down_total[width:].astype(BF16), 1).astype(F32)
    grad_down = grad_down.reshape(here, units, model_width)
    my_routing_grad = (
        row_sum[:, model_width : model_width + experts]
        + row_sum[:, model_width + experts : model_width + 2 * experts]
    )
    row_sum = row_sum[:, :model_width]

    def mine(array):
        return piece(array, tensor_place, own_rows)

    my_hidden, my_scale = mine(hidden), mine(second_scale)
    my_normed = mine(second_norm)
    names = jnp.arange(experts, dtype=jnp.int32)
    my_chosen = jnp.any(mine(expert_ids)[:, :, None] == names[None, None, :], axis=1)
    my_routing = route(my_normed, w_router, my_chosen)
    my_normed = my_normed.astype(F32)
    my_logits = my_routing * (
        my_routing_grad - jnp.sum(my_routing * my_routing_grad, axis=-1, keepdims=True)
    )
    router_float = w_router.astype(F32)
    grad_second = row_sum + jnp.dot(my_logits, router_float.T, precision=EXACT)
    grad_router = lax.dot_general(
        my_logits, my_normed, (((0,), (0,)), ((), ())), precision=EXACT
    )
    grad_norm2 = jnp.sum(grad_second * my_hidden * my_scale, axis=0)
    gained_two = grad_second * norm2_gain
    my_grad_hidden = (
        mine(cotangent).astype(F32)
        + my_scale * gained_two
        - my_hidden * my_scale**3 * jnp.mean(gained_two * my_hidden, axis=-1, keepdims=True)
    )
    small = jnp.concatenate([grad_router, grad_norm2[None]])
    extra = -small.shape[0] % 16
    small = jnp.pad(small, ((0, extra), (0, 0))).astype(BF16)
    parts = z_received(jnp.concatenate([my_grad_hidden.astype(BF16), small]))
    grad_gate, up_weight_gradient, grad_down, *parts = tied(
        grad_gate, up_weight_gradient, grad_down, *parts
    )
    routed = z_scatter(plane_out, axis=1)
    mixed = (piece(hidden, tensor_place, col_width, 1) + routed).astype(BF16)
    grad_branch = z_place([part[:own_rows] for part in parts])
    small = sum(part[own_rows:].astype(F32) for part in parts)
    grad_output = mm_rows(attended, grad_branch)

    grad_heads = mm_cols(grad_branch, w_output).astype(BF16)
    grad_heads = grad_heads.reshape(tok_count, heads_kv, group_size, HEAD_DIMENSION)
    grad_queries, grad_keys, grad_values = attend_backward(
        query_rows, rotated_keys, value_rows, grad_heads, log_total
    )
    grad_query_raw = rotate(
        grad_queries.reshape(tok_count, heads_query, HEAD_DIMENSION), cosine, sine_table, -1.0
    )
    grad_query_raw = grad_query_raw.reshape(tok_count, -1).astype(BF16)
    grad_key_raw = rotate(grad_keys, cosine, sine_table, -1.0)
    grad_key_raw = grad_key_raw.reshape(tok_count, -1).astype(BF16)
    grad_value_raw = grad_values.reshape(tok_count, -1).astype(BF16)
    grad_raw = jnp.concatenate([grad_query_raw, grad_key_raw, grad_value_raw], axis=1)
    grad_first = (
        mm_cols(grad_query_raw, w_query)
        + mm_cols(grad_key_raw, key_projection_weight)
        + mm_cols(grad_value_raw, value_projection_weight)
    )
    norm1_part = jnp.sum(grad_first * resid_in * first_scale, axis=0)[None]

    grad_raw = mm_rows(first_norm, grad_raw)
    raw_width = grad_raw.shape[1]

    def folded(array):
        array = jnp.pad(array.astype(BF16), ((0, -array.shape[0] % 16), (0, 0)))
        return [array[:, i : i + raw_width] for i in range(0, model_width, raw_width)]

    pile = [grad_raw.astype(BF16)] + folded(grad_output) + folded(small) + folded(norm1_part)
    places = [0]
    for part in pile:
        places.append(places[-1] + part.shape[0])
    extra = -places[-1] % 128
    pile = expert_sum(jnp.concatenate(pile + [jnp.zeros((extra, raw_width), BF16)]))
    grad_weights = pile[: places[1]]
    folds = model_width // raw_width

    def unfolded(first, rows):
        return jnp.concatenate(
            [pile[places[i] : places[i] + rows] for i in range(first, first + folds)], axis=1
        )

    grad_output = unfolded(1, grad_output.shape[0])
    small = unfolded(1 + folds, experts + 1)
    grad_norm1 = sum(z_received(unfolded(1 + 2 * folds, 1)))[0]
    q_width, k_width = w_query.shape[1], key_projection_weight.shape[1]

    mixed, grad_first = tied(mixed, grad_first)
    grad_first = z_scatter(grad_first)
    gained_one = grad_first * norm1_gain
    my_resid, my_first_scale = mine(resid_in), mine(first_scale)
    my_grad_input = (
        my_grad_hidden
        + my_first_scale * gained_one
        - my_resid * my_first_scale**3 * jnp.mean(gained_one * my_resid, axis=-1, keepdims=True)
    )
    grad_input = z_place(z_received(my_grad_input.astype(BF16))).astype(F32)

    return (
        mixed,
        grad_input,
        grad_norm1,
        grad_weights[:, :q_width],
        grad_weights[:, q_width : q_width + k_width],
        grad_weights[:, q_width + k_width :],
        grad_output,
        small[experts],
        small[:experts].T,
        grad_gate,
        up_weight_gradient,
        grad_down,
    )


def solution(mesh):
    placed = (
        P("expert", None),
        P(),
        P(None, "tensor"),
        P(None, "tensor"),
        P(None, "tensor"),
        P("tensor", None),
        P(),
        P(),
        P("expert", None, "tensor"),
        P("expert", None, "tensor"),
        P("expert", "tensor", None),
        P("expert", None),
        P("expert", None),
    )
    return jax.shard_map(
        local,
        mesh=mesh,
        in_specs=placed,
        out_specs=(
            P("expert", "tensor"),
            P("expert", None),
            P(),
            P(None, "tensor"),
            P(None, "tensor"),
            P(None, "tensor"),
            P("tensor", None),
            P(),
            P(),
            P("expert", None, "tensor"),
            P("expert", None, "tensor"),
            P("expert", "tensor", None),
        ),
        check_vma=False,
    )
```

```python
import functools
import math

import jax
import jax.numpy as jnp
from jax import lax
from jax.experimental import pallas as pl
from jax.experimental.pallas import tpu as pltpu
from jax.sharding import PartitionSpec as P

HEAD_DIMENSION = 64
SEQ_LEN = 512

EPS = 1e-06
SCALE = 0.125
NEGATIVE = -1e30
THETA = 10000.0
F32 = jnp.float32
BF16 = jnp.bfloat16
EXACT = lax.Precision.HIGHEST
LANES = 128
TILE = 256


def tables(tok_count):
    half = HEAD_DIMENSION // 2
    freq = jnp.exp(-math.log(THETA) * jnp.arange(half, dtype=F32) / half)
    places = (jnp.arange(tok_count) % SEQ_LEN).astype(F32)
    angle = places[:, None] * freq[None, :]
    return (jnp.cos(angle)[:, None, :], jnp.sin(angle)[:, None, :])


def rotate(field, cosine, sine_table, factor):
    half = HEAD_DIMENSION // 2
    first = field[..., :half]
    second = field[..., half:]
    return jnp.concatenate(
        [
            first * cosine - factor * second * sine_table,
            second * cosine + factor * first * sine_table,
        ],
        axis=-1,
    )


def causal_mask():
    places = jnp.arange(SEQ_LEN)
    return places[:, None] >= places[None, :]


def attend_forward(query_rows, rotated_keys, value_rows):
    scores = (
        jnp.einsum("lkgd,mkd->kglm", query_rows, rotated_keys, preferred_element_type=F32) * SCALE
    )
    scores = jnp.where(causal_mask(), scores, NEGATIVE)
    highest = jnp.max(scores, axis=-1, keepdims=True)
    expanded = jnp.exp(scores - highest)
    summed = jnp.sum(expanded, axis=-1, keepdims=True)
    probability = (expanded / summed).astype(BF16)
    heads_out = jnp.einsum("kglm,mkd->lkgd", probability, value_rows, preferred_element_type=F32)
    return (heads_out.astype(BF16), (highest + jnp.log(summed))[..., 0])


def attend_backward(query_rows, rotated_keys, value_rows, grad_heads, log_total):
    scores = (
        jnp.einsum("lkgd,mkd->kglm", query_rows, rotated_keys, preferred_element_type=F32) * SCALE
    )
    probability = jnp.where(causal_mask(), jnp.exp(scores - log_total[..., None]), 0.0)
    prob_low = probability.astype(BF16)
    grad_values = jnp.einsum("kglm,lkgd->mkd", prob_low, grad_heads, preferred_element_type=F32)
    grad_prob = jnp.einsum("lkgd,mkd->kglm", grad_heads, value_rows, preferred_element_type=F32)
    row_delta = jnp.sum(probability * grad_prob, axis=-1, keepdims=True)
    grad_scores = (probability * (grad_prob - row_delta)).astype(BF16)
    grad_queries = (
        jnp.einsum("kglm,mkd->lkgd", grad_scores, rotated_keys, preferred_element_type=F32) * SCALE
    )
    grad_keys = (
        jnp.einsum("kglm,lkgd->mkd", grad_scores, query_rows, preferred_element_type=F32) * SCALE
    )
    return (grad_queries, grad_keys, grad_values)


def mm(left, right):
    return jnp.dot(left, right, preferred_element_type=F32)


def mm_rows(left, right):
    return lax.dot_general(left, right, (((0,), (0,)), ((), ())), preferred_element_type=F32)


def mm_cols(left, right):
    return lax.dot_general(left, right, (((1,), (1,)), ((), ())), preferred_element_type=F32)


def piece(array, index, size, axis=0):
    return lax.dynamic_slice_in_dim(array, index * size, size, axis)


def swap(array, mask):
    size = lax.axis_size("expert")
    return lax.ppermute(array, "expert", [(i, i ^ mask) for i in range(size)])


def z_shift(array, step):
    size = lax.axis_size("tensor")
    return lax.ppermute(array, "tensor", [(i, (i + step) % size) for i in range(size)])


def z_received(array):
    return [array] + [z_shift(array, step) for step in range(1, lax.axis_size("tensor"))]


def z_place(parts):
    size, mine = lax.axis_size("tensor"), lax.axis_index("tensor")
    rows = parts[0].shape[0]
    whole = jnp.zeros((rows * size,) + parts[0].shape[1:], parts[0].dtype)
    for step, part in enumerate(parts):
        whole = lax.dynamic_update_slice_in_dim(whole, part, (mine + size - step) % size * rows, 0)
    return whole


def z_scatter(array, axis=0):
    size, mine = lax.axis_size("tensor"), lax.axis_index("tensor")
    width = array.shape[axis] // size
    total = piece(array, mine, width, axis).astype(F32)
    for step in range(1, size):
        sent = piece(array, (mine + step) % size, width, axis).astype(BF16)
        total = total + z_shift(sent, step).astype(F32)
    return total


def same_core_groups():
    size = lax.axis_size("expert")
    return [list(range(0, size, 2)), list(range(1, size, 2))]


def plane_gather(array):
    if lax.axis_size("expert") != 8:
        return [
            lax.all_gather(
                array, "expert", axis=0, tiled=True, axis_index_groups=same_core_groups()
            )
        ]
    half = array.shape[0] // 2
    from_x = swap(array, 2)
    from_y = swap(array, 4)
    return [array, from_x, from_y, swap(from_x[:half], 4), swap(from_y[half:], 2)]


def plane_scatter_far(blocks):
    return [swap(blocks[3], 2), swap(blocks[4], 4)] if len(blocks) == 5 else []


def plane_scatter(blocks, far=()):
    if lax.axis_size("expert") != 8:
        return lax.psum_scatter(
            blocks[0].astype(BF16),
            "expert",
            scatter_dimension=0,
            tiled=True,
            axis_index_groups=same_core_groups(),
        ).astype(F32), ()
    own, for_x, for_y, far_x, far_y = blocks
    half = own.shape[0] // 2
    via_x, via_y = far if far else plane_scatter_far(blocks)
    via_x, via_y = via_x.astype(F32), via_y.astype(F32)
    for_y = for_y.at[:half].set((for_y[:half].astype(F32) + via_x).astype(BF16))
    for_x = for_x.at[half:].set((for_x[half:].astype(F32) + via_y).astype(BF16))
    total = own.astype(F32) + swap(for_x, 2).astype(F32) + swap(for_y, 4).astype(F32)
    return total, (for_x, for_y)


def expert_sum(array):
    if lax.axis_size("expert") != 8:
        return lax.psum(array.astype(BF16), "expert").astype(F32)
    place = lax.axis_index("expert")
    core, chip = place % 2, place // 2
    half = array.shape[0] // 2
    rows = half // 4
    array = array.astype(BF16)
    mine = piece(array, core, half).astype(F32)
    mine = mine + swap(piece(array, 1 - core, half), 1).astype(F32)
    total = piece(mine, chip, rows)
    for mask in (1, 2, 3):
        total = total + swap(piece(mine, chip ^ mask, rows).astype(BF16), 2 * mask).astype(F32)
    total = total.astype(BF16)
    gathered = jnp.zeros((half,) + array.shape[1:], BF16)
    for mask in (0, 1, 2, 3):
        part = swap(total, 2 * mask) if mask else total
        gathered = lax.dynamic_update_slice_in_dim(gathered, part, (chip ^ mask) * rows, 0)
    both = jnp.concatenate([gathered, gathered])
    both = lax.dynamic_update_slice_in_dim(both, swap(gathered, 1), (1 - core) * half, 0)
    return both.astype(F32)


def expert_kernel(
    experts,
    top_count,
    units,
    names_ref,
    normed_ref,
    grad_ref,
    router_ref,
    gate_ref,
    up_ref,
    down_ref,
    out_ref,
    rows_ref,
    gate_grad_ref,
    up_grad_ref,
    inner_ref,
):
    tile, model_width = normed_ref.shape
    width = gate_ref.shape[1]
    normed = normed_ref[...]
    grad = grad_ref[:, :model_width]
    chosen_names = grad_ref[:, model_width:].astype(F32)
    lane = lax.broadcasted_iota(jnp.int32, (tile, LANES), 1)
    lane_float = lane.astype(F32)
    chosen = lane_float == chosen_names[:, 0:1]
    for k in range(1, top_count):
        chosen = chosen | (lane_float == chosen_names[:, k : k + 1])
    logits = jnp.where(chosen, mm(normed, router_ref[...]), NEGATIVE)
    expanded = jnp.exp(logits - jnp.max(logits, axis=-1, keepdims=True))
    expanded = jnp.where(chosen, expanded, 0.0)
    routing = expanded / jnp.sum(expanded, axis=-1, keepdims=True)
    grad_routing = jnp.zeros((tile, LANES), F32)
    columns = min(TILE, width)
    for start in range(0, width, columns):
        part = slice(start, start + columns)
        gate_act = mm(normed, gate_ref[:, part])
        up_act = mm(normed, up_ref[:, part])
        grad_plain = mm_cols(grad, down_ref[part, :])
        weights = []
        for e in range(start // units, (start + columns) // units):
            weight = jnp.sum(
                jnp.where(lane == names_ref[e], routing, 0.0), axis=-1, keepdims=True
            )
            weights.append(jnp.broadcast_to(weight, (tile, units)))
        wide = jnp.concatenate(weights, axis=1) if len(weights) > 1 else weights[0]
        sigmoid_gate = jax.nn.sigmoid(gate_act)
        swish = gate_act * sigmoid_gate
        inner = swish * up_act
        inner_grad = inner * grad_plain
        for i, e in enumerate(range(start // units, (start + columns) // units)):
            total = jnp.sum(inner_grad[:, i * units : (i + 1) * units], axis=-1, keepdims=True)
            grad_routing = jnp.where(lane == names_ref[e], total, grad_routing)
        grad_inner = grad_plain * wide
        inner_ref[:, part] = (inner * wide).astype(BF16)
        up_grad_ref[:, part] = (grad_inner * swish).astype(BF16)
        gate_grad_ref[:, part] = (
            grad_inner * up_act * (sigmoid_gate + swish * (1.0 - sigmoid_gate))
        ).astype(BF16)
    rounded = grad_routing.astype(BF16).astype(F32)
    left = pltpu.roll(grad_routing - rounded, experts, 1)
    rows_ref[:, model_width:] = (rounded + left).astype(BF16)
    rows_ref[:, :model_width] = (
        mm_cols(gate_grad_ref[...], gate_ref[...]) + mm_cols(up_grad_ref[...], up_ref[...])
    ).astype(BF16)
    out_ref[...] = mm(inner_ref[...], down_ref[...]).astype(BF16)


def expert_block(names, normed, grad, router, gate_w, up_w, down_w, experts, top_count, units):
    rows, model_width = normed.shape
    width = gate_w.shape[1]
    tile = min(TILE, rows)

    def tiled(columns):
        return pl.BlockSpec((tile, columns), lambda i, names: (i, 0))

    def fixed(array):
        return pl.BlockSpec(array.shape, lambda i, names: (0, 0))

    def shaped(columns):
        return jax.ShapeDtypeStruct((rows, columns), BF16)

    return pl.pallas_call(
        functools.partial(expert_kernel, experts, top_count, units),
        grid_spec=pltpu.PrefetchScalarGridSpec(
            num_scalar_prefetch=1,
            grid=(rows // tile,),
            in_specs=[
                tiled(model_width),
                tiled(model_width + LANES),
                fixed(router),
                fixed(gate_w),
                fixed(up_w),
                fixed(down_w),
            ],
            out_specs=[
                tiled(model_width),
                tiled(model_width + LANES),
                tiled(width),
                tiled(width),
                tiled(width),
            ],
        ),
        out_shape=[
            shaped(model_width),
            shaped(model_width + LANES),
            shaped(width),
            shaped(width),
            shaped(width),
        ],
        compiler_params=pltpu.CompilerParams(vmem_limit_bytes=44 * 1024 * 1024),
        cost_estimate=pl.CostEstimate(
            flops=12 * rows * model_width * width,
            bytes_accessed=6 * model_width * width + 14 * rows * model_width,
            transcendentals=rows * width,
        ),
        name="experts",
    )(names, normed, grad, router, gate_w, up_w, down_w)


def half_turn(field, cosine, sine):
    width = field.shape[1]
    half = HEAD_DIMENSION // 2
    lane = lax.broadcasted_iota(jnp.int32, field.shape, 1)
    partner = jnp.where(
        lane % HEAD_DIMENSION < half,
        pltpu.roll(field, width - half, 1),
        pltpu.roll(field, half, 1),
    )
    repeats = width // cosine.shape[1]
    cosine = jnp.concatenate([cosine] * repeats, axis=1)
    sine = jnp.concatenate([sine] * repeats, axis=1)
    return field * cosine + partner * sine


def attention_kernel(
    q_width,
    k_width,
    normed_ref,
    weight_ref,
    output_ref,
    grad_ref,
    cosine_ref,
    sine_ref,
    raw_ref,
    first_ref,
):
    size = HEAD_DIMENSION
    rows = normed_ref.shape[0]
    turned = q_width + k_width
    group = q_width // k_width
    weight = weight_ref[0]
    cosine, sine = cosine_ref[...], sine_ref[...]
    projected = mm(normed_ref[...], weight)
    rotated = half_turn(projected[:, :turned], cosine, sine).astype(BF16)
    values = projected[:, turned:].astype(BF16)
    grad_heads = mm_cols(grad_ref[...], output_ref[0]).astype(BF16)
    tile = rows // 2
    grad_queries, grad_keys, grad_values = [], [], []
    for g in range(k_width // size):
        key = rotated[:, q_width + g * size : q_width + (g + 1) * size]
        value = values[:, g * size : (g + 1) * size]
        key_parts, value_parts = [0.0, 0.0], [0.0, 0.0]
        for h in range(g * group, (g + 1) * group):
            query = rotated[:, h * size : (h + 1) * size]
            grad_head = grad_heads[:, h * size : (h + 1) * size]
            query_parts = []
            for t in range(2):
                here = slice(t * tile, (t + 1) * tile)
                seen = (t + 1) * tile
                scores = mm_cols(query[here], key[:seen]) * SCALE
                place = lax.broadcasted_iota(jnp.int32, scores.shape, 0) + t * tile
                other = lax.broadcasted_iota(jnp.int32, scores.shape, 1)
                scores = jnp.where(place >= other, scores, NEGATIVE)
                expanded = jnp.exp(scores - jnp.max(scores, axis=-1, keepdims=True))
                probability = expanded * (1.0 / jnp.sum(expanded, axis=-1, keepdims=True))
                grad_prob = mm_cols(grad_head[here], value[:seen])
                delta = jnp.sum(probability * grad_prob, axis=-1, keepdims=True)
                grad_scores = (probability * (grad_prob - delta)).astype(BF16)
                query_parts.append(mm(grad_scores, key[:seen]) * SCALE)
                from_keys = mm_rows(grad_scores, query[here])
                from_values = mm_rows(probability.astype(BF16), grad_head[here])
                for u in range(t + 1):
                    block = slice(u * tile, (u + 1) * tile)
                    key_parts[u] = key_parts[u] + from_keys[block]
                    value_parts[u] = value_parts[u] + from_values[block]
            grad_queries.append(jnp.concatenate(query_parts, axis=0))
        grad_keys.append(jnp.concatenate(key_parts, axis=0) * SCALE)
        grad_values.append(jnp.concatenate(value_parts, axis=0))
    grad_turned = jnp.concatenate(grad_queries + grad_keys, axis=1)
    raw_ref[0, :, :turned] = half_turn(grad_turned, cosine, -sine).astype(BF16)
    raw_ref[0, :, turned:] = jnp.concatenate(grad_values, axis=1).astype(BF16)
    total = mm_cols(raw_ref[0], weight)

    @pl.when(pl.program_id(0) == 0)
    def _():
        first_ref[...] = total

    @pl.when(pl.program_id(0) > 0)
    def _():
        first_ref[...] += total


def attention_back(normed, weights, outputs, grad, cosine, sine, q_width, k_width):
    parts, model_width, width = weights.shape
    rows = normed.shape[0]

    def fixed(array):
        return pl.BlockSpec(array.shape, lambda i: (0, 0))

    def stacked(array):
        return pl.BlockSpec((1,) + array.shape[1:], lambda i: (i, 0, 0))

    raw = jax.ShapeDtypeStruct((parts, rows, width), BF16)
    return pl.pallas_call(
        functools.partial(attention_kernel, q_width, k_width),
        grid=(parts,),
        in_specs=[
            fixed(normed),
            stacked(weights),
            stacked(outputs),
            fixed(grad),
            fixed(cosine),
            fixed(sine),
        ],
        out_specs=[stacked(raw), pl.BlockSpec((rows, model_width), lambda i: (0, 0))],
        out_shape=[raw, jax.ShapeDtypeStruct((rows, model_width), F32)],
        compiler_params=pltpu.CompilerParams(vmem_limit_bytes=40 * 1024 * 1024),
        cost_estimate=pl.CostEstimate(
            flops=parts * 6 * rows * model_width * width,
            bytes_accessed=parts * 2 * model_width * width + 8 * rows * model_width,
            transcendentals=parts * rows * rows * 4,
        ),
        name="attention",
    )(normed, weights, outputs, grad, cosine, sine)


def tied(*arrays):
    return lax.optimization_barrier(arrays)


def norm_scale(field):
    return lax.rsqrt(jnp.mean(field * field, axis=-1, keepdims=True) + EPS)


def route(normed, router, chosen):
    logits = mm(normed, router)
    masked = jnp.where(chosen, logits, NEGATIVE)
    highest = jnp.max(masked, axis=-1, keepdims=True)
    expanded = jnp.where(chosen, jnp.exp(masked - highest), 0.0)
    return expanded / jnp.sum(expanded, axis=-1, keepdims=True)


def local(
    tokens,
    norm1_gain,
    w_query,
    key_projection_weight,
    value_projection_weight,
    w_output,
    norm2_gain,
    w_router,
    expert_gate_weight,
    expert_up_weight,
    expert_down_weight,
    expert_ids,
    cotangent,
):
    tok_count = tokens.shape[0]
    model_width = tokens.shape[1]
    experts, top_count = w_router.shape[1], expert_ids.shape[1]
    here, units = expert_gate_weight.shape[0], expert_gate_weight.shape[2]
    heads_query = w_query.shape[1] // HEAD_DIMENSION
    heads_kv = key_projection_weight.shape[1] // HEAD_DIMENSION
    group_size = heads_query // heads_kv
    cosine, sine_table = tables(tok_count)
    expert_count = lax.axis_size("expert")
    tensor_count = lax.axis_size("tensor")
    expert_place = lax.axis_index("expert")
    tensor_place = lax.axis_index("tensor")
    core = expert_place % 2
    own_rows = tok_count // tensor_count
    col_width = model_width // tensor_count

    names_wide = jnp.pad(expert_ids.astype(BF16), ((0, 0), (0, LANES - top_count)))
    grad_blocks = plane_gather(jnp.concatenate([cotangent, names_wide], axis=1))
    if expert_count == 8:
        grad_blocks, grad_far = grad_blocks[:3], grad_blocks[3:]

    half = w_output.shape[0] // 2
    w_halves = [z_shift(piece(w_output, core, half), step) for step in range(1, tensor_count)]
    expert_weights = [expert_gate_weight, expert_up_weight, expert_down_weight]
    if expert_count == 8:
        w_halves, expert_weights = tied(w_halves, expert_weights)
    other_weights = [swap(weight, 1) for weight in expert_weights]
    if expert_count == 8:
        grad_blocks, w_halves = tied(grad_blocks, w_halves)
    w_halves = jnp.stack(w_halves)
    w_others = swap(w_halves, 1)
    w_parts = jnp.where(
        core == 0,
        jnp.concatenate([w_halves, w_others], axis=1),
        jnp.concatenate([w_others, w_halves], axis=1),
    )

    resid_in = tokens.astype(F32)
    first_scale = norm_scale(resid_in)
    first_norm = (resid_in * first_scale * norm1_gain).astype(BF16)
    query_raw = mm(first_norm, w_query).reshape(tok_count, heads_query, HEAD_DIMENSION)
    key_raw = mm(first_norm, key_projection_weight).reshape(tok_count, heads_kv, HEAD_DIMENSION)
    query_rows = (
        rotate(query_raw, cosine, sine_table, 1.0)
        .astype(BF16)
        .reshape(tok_count, heads_kv, group_size, HEAD_DIMENSION)
    )
    rotated_keys = rotate(key_raw, cosine, sine_table, 1.0).astype(BF16)
    value_rows = (
        mm(first_norm, value_projection_weight)
        .astype(BF16)
        .reshape(tok_count, heads_kv, HEAD_DIMENSION)
    )
    attended, log_total = attend_forward(query_rows, rotated_keys, value_rows)
    attended = attended.reshape(tok_count, heads_query * HEAD_DIMENSION)

    attended, other_weights = tied(attended, other_weights)
    attended_parts = z_received(attended)

    resid_in, attended_parts, other_weights, w_parts = tied(
        resid_in, attended_parts, other_weights, w_parts
    )
    attended = attended_parts[0]

    def as_columns(weight):
        return weight.transpose(1, 0, 2).reshape(model_width, -1)

    chip_weights = [jnp.concatenate(pair) for pair in zip(expert_weights, other_weights)]
    gate_w, up_w = as_columns(chip_weights[0]), as_columns(chip_weights[1])
    down_w = chip_weights[2].reshape(-1, model_width)
    hidden = resid_in + mm(attended, w_output)
    for step in range(1, tensor_count):
        hidden = hidden + mm(attended_parts[step], w_parts[step - 1])
    second_scale = norm_scale(hidden)
    second_norm = (hidden * second_scale * norm2_gain).astype(BF16)

    local_names = jnp.concatenate(
        [
            expert_place * here + jnp.arange(here, dtype=jnp.int32),
            (expert_place ^ 1) * here + jnp.arange(here, dtype=jnp.int32),
        ]
    )
    router_wide = jnp.pad(w_router, ((0, 0), (0, LANES - experts)))
    if expert_count == 8:
        second_norm, grad_far = tied(second_norm, grad_far)
        grad_blocks = grad_blocks + grad_far

    def through_experts(normed, grad):
        return expert_block(
            local_names,
            normed,
            grad,
            router_wide,
            gate_w,
            up_w,
            down_w,
            experts,
            top_count,
            units,
        )

    q_width, k_width = w_query.shape[1], key_projection_weight.shape[1]
    replicated = expert_count == 8 and k_width % LANES == 0
    if replicated:
        own_weight = jnp.concatenate([w_query, key_projection_weight, value_projection_weight], 1)
        qkv_half = piece(own_weight, core, model_width // 2)
        second_norm, qkv_half = tied(second_norm, qkv_half)
        qkv_halves = [z_shift(qkv_half, step) for step in range(1, tensor_count)]
    if expert_count == 8:
        half = tok_count // 2
        from_x, from_y = swap(second_norm, 2), swap(second_norm, 4)
        own_done = through_experts(second_norm, grad_blocks[0])
        from_x, from_y, own_done = tied(from_x, from_y, own_done)
        normed_blocks = [
            second_norm, from_x, from_y, swap(from_x[:half], 4), swap(from_y[half:], 2)
        ]
        if replicated:
            normed_blocks[3:], qkv_halves = tied(normed_blocks[3:], qkv_halves)
            qkv_halves = jnp.stack(qkv_halves)
            qkv_others = swap(qkv_halves, 1)
            qkv_parts = jnp.where(
                core == 0,
                jnp.concatenate([qkv_halves, qkv_others], axis=1),
                jnp.concatenate([qkv_others, qkv_halves], axis=1),
            )
        done = [own_done]
    else:
        normed_blocks = plane_gather(second_norm)
        done = []
    if expert_count == 8:
        done.append(through_experts(normed_blocks[1], grad_blocks[1]))
        far_done = [through_experts(normed_blocks[i], grad_blocks[i]) for i in (3, 4)]
        normed_blocks[2], far_done = tied(normed_blocks[2], far_done)
        done.append(through_experts(normed_blocks[2], grad_blocks[2]))
        done += far_done
    else:
        done = [through_experts(normed, grad) for normed, grad in zip(normed_blocks, grad_blocks)]
    plane_rows, merged = plane_scatter([block[1] for block in done])
    plane_rows, *out_blocks = tied(plane_rows, *[block[0] for block in done])
    held, merged = tied([array for block in done for array in block[2:]], merged)
    done = [held[3 * i : 3 * i + 3] for i in range(len(done))]
    gate_total = up_total = down_total = 0.0
    for normed, grad, block in zip(normed_blocks, grad_blocks, done):
        gate_total = gate_total + mm_rows(normed, block[0])
        up_total = up_total + mm_rows(normed, block[1])
        down_total = down_total + mm_rows(block[2], grad[:, :model_width])

    row_sum = z_scatter(plane_rows)
    out_far = plane_scatter_far(out_blocks)
    row_sum, out_far = tied(row_sum, out_far)
    plane_out, _ = plane_scatter(out_blocks, out_far)

    my_routing_grad = (
        row_sum[:, model_width : model_width + experts]
        + row_sum[:, model_width + experts : model_width + 2 * experts]
    )
    row_sum = row_sum[:, :model_width]

    def mine(array):
        return piece(array, tensor_place, own_rows)

    my_hidden, my_scale = mine(hidden), mine(second_scale)
    my_normed = mine(second_norm)
    names = jnp.arange(experts, dtype=jnp.int32)
    my_chosen = jnp.any(mine(expert_ids)[:, :, None] == names[None, None, :], axis=1)
    my_routing = route(my_normed, w_router, my_chosen)
    my_normed = my_normed.astype(F32)
    my_logits = my_routing * (
        my_routing_grad - jnp.sum(my_routing * my_routing_grad, axis=-1, keepdims=True)
    )
    router_float = w_router.astype(F32)
    grad_second = row_sum + jnp.dot(my_logits, router_float.T, precision=EXACT)
    grad_router = lax.dot_general(
        my_logits, my_normed, (((0,), (0,)), ((), ())), precision=EXACT
    )
    grad_norm2 = jnp.sum(grad_second * my_hidden * my_scale, axis=0)
    gained_two = grad_second * norm2_gain
    my_grad_hidden = (
        mine(cotangent).astype(F32)
        + my_scale * gained_two
        - my_hidden * my_scale**3 * jnp.mean(gained_two * my_hidden, axis=-1, keepdims=True)
    )
    small = jnp.concatenate([grad_router, grad_norm2[None]])
    extra = -small.shape[0] % 16
    small = jnp.pad(small, ((0, extra), (0, 0))).astype(BF16)
    parts = z_received(jnp.concatenate([my_grad_hidden.astype(BF16), small]))
    plane_out, gate_total, up_total, down_total, *parts = tied(
        plane_out, gate_total, up_total, down_total, *parts
    )
    width = here * units

    def from_chip(total):
        return total[:, :width] + swap(total[:, width:].astype(BF16), 1).astype(F32)

    def as_experts(total):
        return total.reshape(model_width, here, units).transpose(1, 0, 2)

    grad_gate = as_experts(from_chip(gate_total))
    up_weight_gradient = as_experts(from_chip(up_total))
    grad_down = down_total[:width] + swap(down_total[width:].astype(BF16), 1).astype(F32)
    grad_down = grad_down.reshape(here, units, model_width)
    routed = z_scatter(plane_out, axis=1)
    mixed = (piece(hidden, tensor_place, col_width, 1) + routed).astype(BF16)
    grad_branch = z_place([part[:own_rows] for part in parts])
    small = sum(part[own_rows:].astype(F32) for part in parts)
    grad_output = mm_rows(attended, grad_branch)

    if replicated:
        wide_cosine = jnp.concatenate([cosine[:, 0]] * (LANES // 32), axis=1)
        signed = jnp.concatenate([-sine_table[:, 0], sine_table[:, 0]], axis=1)
        wide_sine = jnp.concatenate([signed] * (LANES // HEAD_DIMENSION), axis=1)
        grad_raw, grad_first = attention_back(
            first_norm,
            own_weight[None],
            w_output[None],
            grad_branch,
            wide_cosine,
            wide_sine,
            q_width,
            k_width,
        )
        grad_raw = grad_raw[0]
        norm1_part = jnp.sum(grad_first * resid_in * first_scale, axis=0)[None]
    else:
        grad_heads = mm_cols(grad_branch, w_output).astype(BF16)
        grad_heads = grad_heads.reshape(tok_count, heads_kv, group_size, HEAD_DIMENSION)
        grad_queries, grad_keys, grad_values = attend_backward(
            query_rows, rotated_keys, value_rows, grad_heads, log_total
        )
        grad_query_raw = rotate(
            grad_queries.reshape(tok_count, heads_query, HEAD_DIMENSION), cosine, sine_table, -1.0
        )
        grad_query_raw = grad_query_raw.reshape(tok_count, -1).astype(BF16)
        grad_key_raw = rotate(grad_keys, cosine, sine_table, -1.0)
        grad_key_raw = grad_key_raw.reshape(tok_count, -1).astype(BF16)
        grad_value_raw = grad_values.reshape(tok_count, -1).astype(BF16)
        grad_raw = jnp.concatenate([grad_query_raw, grad_key_raw, grad_value_raw], axis=1)
        grad_first = (
            mm_cols(grad_query_raw, w_query)
            + mm_cols(grad_key_raw, key_projection_weight)
            + mm_cols(grad_value_raw, value_projection_weight)
        )
        norm1_part = jnp.sum(grad_first * resid_in * first_scale, axis=0)[None]

    grad_raw = mm_rows(first_norm, grad_raw)
    raw_width = grad_raw.shape[1]

    def folded(array):
        array = jnp.pad(array.astype(BF16), ((0, -array.shape[0] % 16), (0, 0)))
        return [array[:, i : i + raw_width] for i in range(0, model_width, raw_width)]

    pile = [grad_raw.astype(BF16)] + folded(grad_output) + folded(small) + folded(norm1_part)
    places = [0]
    for part in pile:
        places.append(places[-1] + part.shape[0])
    extra = -places[-1] % 128
    pile = expert_sum(jnp.concatenate(pile + [jnp.zeros((extra, raw_width), BF16)]))
    grad_weights = pile[: places[1]]
    folds = model_width // raw_width

    def unfolded(first, rows):
        return jnp.concatenate(
            [pile[places[i] : places[i] + rows] for i in range(first, first + folds)], axis=1
        )

    grad_output = unfolded(1, grad_output.shape[0])
    small = unfolded(1 + folds, experts + 1)
    grad_norm1 = sum(z_received(unfolded(1 + 2 * folds, 1)))[0]

    def first_norm_back(grad_first, grad_hidden, resid, scale):
        gained = grad_first * norm1_gain
        return (
            grad_hidden
            + scale * gained
            - resid * scale**3 * jnp.mean(gained * resid, axis=-1, keepdims=True)
        )

    if replicated:
        _, others_first = attention_back(
            first_norm,
            qkv_parts,
            w_parts,
            grad_branch,
            wide_cosine,
            wide_sine,
            q_width,
            k_width,
        )
        grad_input = first_norm_back(
            grad_first + others_first, grad_branch.astype(F32), resid_in, first_scale
        )
    else:
        my_grad_input = first_norm_back(
            z_scatter(grad_first), my_grad_hidden, mine(resid_in), mine(first_scale)
        )
        grad_input = z_place(z_received(my_grad_input.astype(BF16))).astype(F32)

    return (
        mixed,
        grad_input,
        grad_norm1,
        grad_weights[:, :q_width],
        grad_weights[:, q_width : q_width + k_width],
        grad_weights[:, q_width + k_width :],
        grad_output,
        small[experts],
        small[:experts].T,
        grad_gate,
        up_weight_gradient,
        grad_down,
    )


def solution(mesh):
    placed = (
        P("expert", None),
        P(),
        P(None, "tensor"),
        P(None, "tensor"),
        P(None, "tensor"),
        P("tensor", None),
        P(),
        P(),
        P("expert", None, "tensor"),
        P("expert", None, "tensor"),
        P("expert", "tensor", None),
        P("expert", None),
        P("expert", None),
    )
    return jax.shard_map(
        local,
        mesh=mesh,
        in_specs=placed,
        out_specs=(
            P("expert", "tensor"),
            P("expert", None),
            P(),
            P(None, "tensor"),
            P(None, "tensor"),
            P(None, "tensor"),
            P("tensor", None),
            P(),
            P(),
            P("expert", None, "tensor"),
            P("expert", None, "tensor"),
            P("expert", "tensor", None),
        ),
        check_vma=False,
    )
```

```python
import functools
import math

import jax
import jax.numpy as jnp
from jax import lax
from jax.experimental import pallas as pl
from jax.experimental.pallas import tpu as pltpu
from jax.sharding import PartitionSpec as P

HEAD_DIMENSION = 64
SEQ_LEN = 512

EPS = 1e-06
SCALE = 0.125
NEGATIVE = -1e30
THETA = 10000.0
F32 = jnp.float32
BF16 = jnp.bfloat16
EXACT = lax.Precision.HIGHEST
LANES = 128
TILE = 256


def tables(tok_count):
    half = HEAD_DIMENSION // 2
    freq = jnp.exp(-math.log(THETA) * jnp.arange(half, dtype=F32) / half)
    places = (jnp.arange(tok_count) % SEQ_LEN).astype(F32)
    angle = places[:, None] * freq[None, :]
    return (jnp.cos(angle)[:, None, :], jnp.sin(angle)[:, None, :])


def rotate(field, cosine, sine_table, factor):
    half = HEAD_DIMENSION // 2
    first = field[..., :half]
    second = field[..., half:]
    return jnp.concatenate(
        [
            first * cosine - factor * second * sine_table,
            second * cosine + factor * first * sine_table,
        ],
        axis=-1,
    )


def causal_mask():
    places = jnp.arange(SEQ_LEN)
    return places[:, None] >= places[None, :]


def attend_forward(query_rows, rotated_keys, value_rows):
    scores = (
        jnp.einsum("lkgd,mkd->kglm", query_rows, rotated_keys, preferred_element_type=F32) * SCALE
    )
    scores = jnp.where(causal_mask(), scores, NEGATIVE)
    highest = jnp.max(scores, axis=-1, keepdims=True)
    expanded = jnp.exp(scores - highest)
    summed = jnp.sum(expanded, axis=-1, keepdims=True)
    probability = (expanded / summed).astype(BF16)
    heads_out = jnp.einsum("kglm,mkd->lkgd", probability, value_rows, preferred_element_type=F32)
    return (heads_out.astype(BF16), (highest + jnp.log(summed))[..., 0])


def attend_backward(query_rows, rotated_keys, value_rows, grad_heads, log_total):
    scores = (
        jnp.einsum("lkgd,mkd->kglm", query_rows, rotated_keys, preferred_element_type=F32) * SCALE
    )
    probability = jnp.where(causal_mask(), jnp.exp(scores - log_total[..., None]), 0.0)
    prob_low = probability.astype(BF16)
    grad_values = jnp.einsum("kglm,lkgd->mkd", prob_low, grad_heads, preferred_element_type=F32)
    grad_prob = jnp.einsum("lkgd,mkd->kglm", grad_heads, value_rows, preferred_element_type=F32)
    row_delta = jnp.sum(probability * grad_prob, axis=-1, keepdims=True)
    grad_scores = (probability * (grad_prob - row_delta)).astype(BF16)
    grad_queries = (
        jnp.einsum("kglm,mkd->lkgd", grad_scores, rotated_keys, preferred_element_type=F32) * SCALE
    )
    grad_keys = (
        jnp.einsum("kglm,lkgd->mkd", grad_scores, query_rows, preferred_element_type=F32) * SCALE
    )
    return (grad_queries, grad_keys, grad_values)


def mm(left, right):
    return jnp.dot(left, right, preferred_element_type=F32)


def mm_rows(left, right):
    return lax.dot_general(left, right, (((0,), (0,)), ((), ())), preferred_element_type=F32)


def mm_cols(left, right):
    return lax.dot_general(left, right, (((1,), (1,)), ((), ())), preferred_element_type=F32)


def piece(array, index, size, axis=0):
    return lax.dynamic_slice_in_dim(array, index * size, size, axis)


def swap(array, mask):
    size = lax.axis_size("expert")
    return lax.ppermute(array, "expert", [(i, i ^ mask) for i in range(size)])


def z_shift(array, step):
    size = lax.axis_size("tensor")
    return lax.ppermute(array, "tensor", [(i, (i + step) % size) for i in range(size)])


def z_received(array):
    return [array] + [z_shift(array, step) for step in range(1, lax.axis_size("tensor"))]


def z_place(parts):
    size, mine = lax.axis_size("tensor"), lax.axis_index("tensor")
    rows = parts[0].shape[0]
    whole = jnp.zeros((rows * size,) + parts[0].shape[1:], parts[0].dtype)
    for step, part in enumerate(parts):
        whole = lax.dynamic_update_slice_in_dim(whole, part, (mine + size - step) % size * rows, 0)
    return whole


def z_scatter(array, axis=0):
    size, mine = lax.axis_size("tensor"), lax.axis_index("tensor")
    width = array.shape[axis] // size
    total = piece(array, mine, width, axis).astype(F32)
    for step in range(1, size):
        sent = piece(array, (mine + step) % size, width, axis).astype(BF16)
        total = total + z_shift(sent, step).astype(F32)
    return total


def same_core_groups():
    size = lax.axis_size("expert")
    return [list(range(0, size, 2)), list(range(1, size, 2))]


def plane_gather(array):
    if lax.axis_size("expert") != 8:
        return [
            lax.all_gather(
                array, "expert", axis=0, tiled=True, axis_index_groups=same_core_groups()
            )
        ]
    half = array.shape[0] // 2
    from_x = swap(array, 2)
    from_y = swap(array, 4)
    return [array, from_x, from_y, swap(from_x[:half], 4), swap(from_y[half:], 2)]


def plane_scatter_far(blocks):
    return [swap(blocks[3], 2), swap(blocks[4], 4)] if len(blocks) == 5 else []


def plane_scatter(blocks, far=()):
    if lax.axis_size("expert") != 8:
        return lax.psum_scatter(
            blocks[0].astype(BF16),
            "expert",
            scatter_dimension=0,
            tiled=True,
            axis_index_groups=same_core_groups(),
        ).astype(F32), ()
    own, for_x, for_y, far_x, far_y = blocks
    half = own.shape[0] // 2
    via_x, via_y = far if far else plane_scatter_far(blocks)
    via_x, via_y = via_x.astype(F32), via_y.astype(F32)
    for_y = for_y.at[:half].set((for_y[:half].astype(F32) + via_x).astype(BF16))
    for_x = for_x.at[half:].set((for_x[half:].astype(F32) + via_y).astype(BF16))
    total = own.astype(F32) + swap(for_x, 2).astype(F32) + swap(for_y, 4).astype(F32)
    return total, (for_x, for_y)


def expert_sum(array, first=(), second=()):
    if lax.axis_size("expert") != 8:
        return lax.psum(array.astype(BF16), "expert").astype(F32), first, second
    place = lax.axis_index("expert")
    core, chip = place % 2, place // 2
    half = array.shape[0] // 2
    rows = half // 4
    array = array.astype(BF16)
    mine = piece(array, core, half).astype(F32)
    mine = mine + swap(piece(array, 1 - core, half), 1).astype(F32)
    mine, first = tied(mine, first)
    total = piece(mine, chip, rows)
    for mask in (1, 2, 3):
        total = total + swap(piece(mine, chip ^ mask, rows).astype(BF16), 2 * mask).astype(F32)
    total, second = tied(total.astype(BF16), second)
    gathered = jnp.zeros((half,) + array.shape[1:], BF16)
    for mask in (0, 1, 2, 3):
        part = swap(total, 2 * mask) if mask else total
        gathered = lax.dynamic_update_slice_in_dim(gathered, part, (chip ^ mask) * rows, 0)
    both = jnp.concatenate([gathered, gathered])
    both = lax.dynamic_update_slice_in_dim(both, swap(gathered, 1), (1 - core) * half, 0)
    return both.astype(F32), first, second


def expert_kernel(
    experts,
    top_count,
    units,
    names_ref,
    normed_ref,
    grad_ref,
    router_ref,
    gate_ref,
    up_ref,
    down_ref,
    out_ref,
    rows_ref,
    gate_grad_ref,
    up_grad_ref,
    inner_ref,
):
    tile, model_width = normed_ref.shape
    width = gate_ref.shape[1]
    normed = normed_ref[...]
    grad = grad_ref[:, :model_width]
    chosen_names = grad_ref[:, model_width:].astype(F32)
    lane = lax.broadcasted_iota(jnp.int32, (tile, LANES), 1)
    lane_float = lane.astype(F32)
    chosen = lane_float == chosen_names[:, 0:1]
    for k in range(1, top_count):
        chosen = chosen | (lane_float == chosen_names[:, k : k + 1])
    logits = jnp.where(chosen, mm(normed, router_ref[...]), NEGATIVE)
    expanded = jnp.exp(logits - jnp.max(logits, axis=-1, keepdims=True))
    expanded = jnp.where(chosen, expanded, 0.0)
    routing = expanded / jnp.sum(expanded, axis=-1, keepdims=True)
    grad_routing = jnp.zeros((tile, LANES), F32)
    columns = min(TILE, width)
    for start in range(0, width, columns):
        part = slice(start, start + columns)
        gate_act = mm(normed, gate_ref[:, part])
        up_act = mm(normed, up_ref[:, part])
        grad_plain = mm_cols(grad, down_ref[part, :])
        weights = []
        for e in range(start // units, (start + columns) // units):
            weight = jnp.sum(
                jnp.where(lane == names_ref[e], routing, 0.0), axis=-1, keepdims=True
            )
            weights.append(jnp.broadcast_to(weight, (tile, units)))
        wide = jnp.concatenate(weights, axis=1) if len(weights) > 1 else weights[0]
        sigmoid_gate = jax.nn.sigmoid(gate_act)
        swish = gate_act * sigmoid_gate
        inner = swish * up_act
        inner_grad = inner * grad_plain
        for i, e in enumerate(range(start // units, (start + columns) // units)):
            total = jnp.sum(inner_grad[:, i * units : (i + 1) * units], axis=-1, keepdims=True)
            grad_routing = jnp.where(lane == names_ref[e], total, grad_routing)
        grad_inner = grad_plain * wide
        inner_ref[:, part] = (inner * wide).astype(BF16)
        up_grad_ref[:, part] = (grad_inner * swish).astype(BF16)
        gate_grad_ref[:, part] = (
            grad_inner * up_act * (sigmoid_gate + swish * (1.0 - sigmoid_gate))
        ).astype(BF16)
    rounded = grad_routing.astype(BF16).astype(F32)
    left = pltpu.roll(grad_routing - rounded, experts, 1)
    rows_ref[:, model_width:] = (rounded + left).astype(BF16)
    rows_ref[:, :model_width] = (
        mm_cols(gate_grad_ref[...], gate_ref[...]) + mm_cols(up_grad_ref[...], up_ref[...])
    ).astype(BF16)
    out_ref[...] = mm(inner_ref[...], down_ref[...]).astype(BF16)


def expert_block(names, normed, grad, router, gate_w, up_w, down_w, experts, top_count, units):
    rows, model_width = normed.shape
    width = gate_w.shape[1]
    tile = min(TILE, rows)

    def tiled(columns):
        return pl.BlockSpec((tile, columns), lambda i, names: (i, 0))

    def fixed(array):
        return pl.BlockSpec(array.shape, lambda i, names: (0, 0))

    def shaped(columns):
        return jax.ShapeDtypeStruct((rows, columns), BF16)

    return pl.pallas_call(
        functools.partial(expert_kernel, experts, top_count, units),
        grid_spec=pltpu.PrefetchScalarGridSpec(
            num_scalar_prefetch=1,
            grid=(rows // tile,),
            in_specs=[
                tiled(model_width),
                tiled(model_width + LANES),
                fixed(router),
                fixed(gate_w),
                fixed(up_w),
                fixed(down_w),
            ],
            out_specs=[
                tiled(model_width),
                tiled(model_width + LANES),
                tiled(width),
                tiled(width),
                tiled(width),
            ],
        ),
        out_shape=[
            shaped(model_width),
            shaped(model_width + LANES),
            shaped(width),
            shaped(width),
            shaped(width),
        ],
        compiler_params=pltpu.CompilerParams(vmem_limit_bytes=44 * 1024 * 1024),
        cost_estimate=pl.CostEstimate(
            flops=12 * rows * model_width * width,
            bytes_accessed=6 * model_width * width + 14 * rows * model_width,
            transcendentals=rows * width,
        ),
        name="experts",
    )(names, normed, grad, router, gate_w, up_w, down_w)


def half_turn(field, cosine, sine):
    width = field.shape[1]
    half = HEAD_DIMENSION // 2
    lane = lax.broadcasted_iota(jnp.int32, field.shape, 1)
    partner = jnp.where(
        lane % HEAD_DIMENSION < half,
        pltpu.roll(field, width - half, 1),
        pltpu.roll(field, half, 1),
    )
    repeats = width // cosine.shape[1]
    cosine = jnp.concatenate([cosine] * repeats, axis=1)
    sine = jnp.concatenate([sine] * repeats, axis=1)
    return field * cosine + partner * sine


def forward_kernel(
    tokens_ref, gain_ref, query_ref, key_ref, value_ref, cosine_ref, sine_ref, normed_ref, out_ref
):
    size = HEAD_DIMENSION
    tokens = tokens_ref[...].astype(F32)
    normed = (tokens * norm_scale(tokens) * gain_ref[...]).astype(BF16)
    normed_ref[...] = normed
    cosine, sine = cosine_ref[...], sine_ref[...]
    queries = half_turn(mm(normed, query_ref[...]), cosine, sine).astype(BF16)
    keys = half_turn(mm(normed, key_ref[...]), cosine, sine).astype(BF16)
    values = mm(normed, value_ref[...]).astype(BF16)
    group = queries.shape[1] // keys.shape[1]
    tile = tokens.shape[0] // 2
    for t in range(2):
        heads = []
        seen = (t + 1) * tile
        for h in range(queries.shape[1] // size):
            g = h // group
            query = queries[t * tile : seen, h * size : (h + 1) * size]
            scores = mm_cols(query, keys[:seen, g * size : (g + 1) * size]) * SCALE
            place = lax.broadcasted_iota(jnp.int32, scores.shape, 0) + t * tile
            other = lax.broadcasted_iota(jnp.int32, scores.shape, 1)
            scores = jnp.where(place >= other, scores, NEGATIVE)
            expanded = jnp.exp(scores - jnp.max(scores, axis=-1, keepdims=True))
            probability = expanded * (1.0 / jnp.sum(expanded, axis=-1, keepdims=True))
            heads.append(mm(probability.astype(BF16), values[:seen, g * size : (g + 1) * size]))
        out_ref[t * tile : seen, :] = jnp.concatenate(heads, axis=1).astype(BF16)


def attention_forward(tokens, gain, query_w, key_w, value_w, cosine, sine):
    rows, model_width = tokens.shape
    return pl.pallas_call(
        forward_kernel,
        out_shape=[
            jax.ShapeDtypeStruct((rows, model_width), BF16),
            jax.ShapeDtypeStruct((rows, query_w.shape[1]), BF16),
        ],
        compiler_params=pltpu.CompilerParams(vmem_limit_bytes=32 * 1024 * 1024),
        cost_estimate=pl.CostEstimate(
            flops=4 * rows * model_width * query_w.shape[1],
            bytes_accessed=4 * rows * model_width,
            transcendentals=rows * rows * 4,
        ),
        name="forward",
    )(tokens, gain[None], query_w, key_w, value_w, cosine, sine)


def attention_kernel(
    q_width,
    k_width,
    normed_ref,
    weight_ref,
    output_ref,
    grad_ref,
    cosine_ref,
    sine_ref,
    raw_ref,
    first_ref,
):
    size = HEAD_DIMENSION
    rows = normed_ref.shape[0]
    turned = q_width + k_width
    group = q_width // k_width
    weight = weight_ref[0]
    cosine, sine = cosine_ref[...], sine_ref[...]
    projected = mm(normed_ref[...], weight)
    rotated = half_turn(projected[:, :turned], cosine, sine).astype(BF16)
    values = projected[:, turned:].astype(BF16)
    grad_heads = mm_cols(grad_ref[...], output_ref[0]).astype(BF16)
    tile = rows // 2
    grad_queries, grad_keys, grad_values = [], [], []
    for g in range(k_width // size):
        key = rotated[:, q_width + g * size : q_width + (g + 1) * size]
        value = values[:, g * size : (g + 1) * size]
        key_parts, value_parts = [0.0, 0.0], [0.0, 0.0]
        for h in range(g * group, (g + 1) * group):
            query = rotated[:, h * size : (h + 1) * size]
            grad_head = grad_heads[:, h * size : (h + 1) * size]
            query_parts = []
            for t in range(2):
                here = slice(t * tile, (t + 1) * tile)
                seen = (t + 1) * tile
                scores = mm_cols(query[here], key[:seen]) * SCALE
                place = lax.broadcasted_iota(jnp.int32, scores.shape, 0) + t * tile
                other = lax.broadcasted_iota(jnp.int32, scores.shape, 1)
                scores = jnp.where(place >= other, scores, NEGATIVE)
                expanded = jnp.exp(scores - jnp.max(scores, axis=-1, keepdims=True))
                probability = expanded * (1.0 / jnp.sum(expanded, axis=-1, keepdims=True))
                grad_prob = mm_cols(grad_head[here], value[:seen])
                delta = jnp.sum(probability * grad_prob, axis=-1, keepdims=True)
                grad_scores = (probability * (grad_prob - delta)).astype(BF16)
                query_parts.append(mm(grad_scores, key[:seen]) * SCALE)
                from_keys = mm_rows(grad_scores, query[here])
                from_values = mm_rows(probability.astype(BF16), grad_head[here])
                for u in range(t + 1):
                    block = slice(u * tile, (u + 1) * tile)
                    key_parts[u] = key_parts[u] + from_keys[block]
                    value_parts[u] = value_parts[u] + from_values[block]
            grad_queries.append(jnp.concatenate(query_parts, axis=0))
        grad_keys.append(jnp.concatenate(key_parts, axis=0) * SCALE)
        grad_values.append(jnp.concatenate(value_parts, axis=0))
    grad_turned = jnp.concatenate(grad_queries + grad_keys, axis=1)
    raw_ref[0, :, :turned] = half_turn(grad_turned, cosine, -sine).astype(BF16)
    raw_ref[0, :, turned:] = jnp.concatenate(grad_values, axis=1).astype(BF16)
    total = mm_cols(raw_ref[0], weight)

    @pl.when(pl.program_id(0) == 0)
    def _():
        first_ref[...] = total

    @pl.when(pl.program_id(0) > 0)
    def _():
        first_ref[...] += total


def attention_back(normed, weights, outputs, grad, cosine, sine, q_width, k_width):
    parts, model_width, width = weights.shape
    rows = normed.shape[0]

    def fixed(array):
        return pl.BlockSpec(array.shape, lambda i: (0, 0))

    def stacked(array):
        return pl.BlockSpec((1,) + array.shape[1:], lambda i: (i, 0, 0))

    raw = jax.ShapeDtypeStruct((parts, rows, width), BF16)
    return pl.pallas_call(
        functools.partial(attention_kernel, q_width, k_width),
        grid=(parts,),
        in_specs=[
            fixed(normed),
            stacked(weights),
            stacked(outputs),
            fixed(grad),
            fixed(cosine),
            fixed(sine),
        ],
        out_specs=[stacked(raw), pl.BlockSpec((rows, model_width), lambda i: (0, 0))],
        out_shape=[raw, jax.ShapeDtypeStruct((rows, model_width), F32)],
        compiler_params=pltpu.CompilerParams(vmem_limit_bytes=40 * 1024 * 1024),
        cost_estimate=pl.CostEstimate(
            flops=parts * 6 * rows * model_width * width,
            bytes_accessed=parts * 2 * model_width * width + 8 * rows * model_width,
            transcendentals=parts * rows * rows * 4,
        ),
        name="attention",
    )(normed, weights, outputs, grad, cosine, sine)


def tied(*arrays):
    return lax.optimization_barrier(arrays)


def norm_scale(field):
    return lax.rsqrt(jnp.mean(field * field, axis=-1, keepdims=True) + EPS)


def route(normed, router, chosen):
    logits = mm(normed, router)
    masked = jnp.where(chosen, logits, NEGATIVE)
    highest = jnp.max(masked, axis=-1, keepdims=True)
    expanded = jnp.where(chosen, jnp.exp(masked - highest), 0.0)
    return expanded / jnp.sum(expanded, axis=-1, keepdims=True)


def local(
    tokens,
    norm1_gain,
    w_query,
    key_projection_weight,
    value_projection_weight,
    w_output,
    norm2_gain,
    w_router,
    expert_gate_weight,
    expert_up_weight,
    expert_down_weight,
    expert_ids,
    cotangent,
):
    tok_count = tokens.shape[0]
    model_width = tokens.shape[1]
    experts, top_count = w_router.shape[1], expert_ids.shape[1]
    here, units = expert_gate_weight.shape[0], expert_gate_weight.shape[2]
    heads_query = w_query.shape[1] // HEAD_DIMENSION
    heads_kv = key_projection_weight.shape[1] // HEAD_DIMENSION
    group_size = heads_query // heads_kv
    cosine, sine_table = tables(tok_count)
    expert_count = lax.axis_size("expert")
    tensor_count = lax.axis_size("tensor")
    expert_place = lax.axis_index("expert")
    tensor_place = lax.axis_index("tensor")
    core = expert_place % 2
    own_rows = tok_count // tensor_count
    col_width = model_width // tensor_count

    names_wide = jnp.pad(expert_ids.astype(BF16), ((0, 0), (0, LANES - top_count)))
    grad_blocks = plane_gather(jnp.concatenate([cotangent, names_wide], axis=1))
    if expert_count == 8:
        grad_blocks, grad_far = grad_blocks[:3], grad_blocks[3:]

    half = w_output.shape[0] // 2
    w_halves = [z_shift(piece(w_output, core, half), step) for step in range(1, tensor_count)]
    expert_weights = [expert_gate_weight, expert_up_weight, expert_down_weight]
    if expert_count == 8:
        w_halves, expert_weights = tied(w_halves, expert_weights)
    other_weights = [swap(weight, 1) for weight in expert_weights]
    if expert_count == 8:
        grad_blocks, w_halves = tied(grad_blocks, w_halves)
    w_halves = jnp.stack(w_halves)
    w_others = swap(w_halves, 1)
    w_parts = jnp.where(
        core == 0,
        jnp.concatenate([w_halves, w_others], axis=1),
        jnp.concatenate([w_others, w_halves], axis=1),
    )

    q_width, k_width = w_query.shape[1], key_projection_weight.shape[1]
    replicated = expert_count == 8 and k_width % LANES == 0
    resid_in = tokens.astype(F32)
    first_scale = norm_scale(resid_in)
    if replicated:
        wide_cosine = jnp.concatenate([cosine[:, 0]] * (LANES // 32), axis=1)
        signed = jnp.concatenate([-sine_table[:, 0], sine_table[:, 0]], axis=1)
        wide_sine = jnp.concatenate([signed] * (LANES // HEAD_DIMENSION), axis=1)
        first_norm, attended = attention_forward(
            tokens,
            norm1_gain,
            w_query,
            key_projection_weight,
            value_projection_weight,
            wide_cosine,
            wide_sine,
        )
    else:
        first_norm = (resid_in * first_scale * norm1_gain).astype(BF16)
        query_raw = mm(first_norm, w_query).reshape(tok_count, heads_query, HEAD_DIMENSION)
        key_raw = mm(first_norm, key_projection_weight).reshape(tok_count, heads_kv, HEAD_DIMENSION)
        query_rows = (
            rotate(query_raw, cosine, sine_table, 1.0)
            .astype(BF16)
            .reshape(tok_count, heads_kv, group_size, HEAD_DIMENSION)
        )
        rotated_keys = rotate(key_raw, cosine, sine_table, 1.0).astype(BF16)
        value_rows = (
            mm(first_norm, value_projection_weight)
            .astype(BF16)
            .reshape(tok_count, heads_kv, HEAD_DIMENSION)
        )
        attended, log_total = attend_forward(query_rows, rotated_keys, value_rows)
        attended = attended.reshape(tok_count, heads_query * HEAD_DIMENSION)

    attended, other_weights = tied(attended, other_weights)
    attended_parts = z_received(attended)

    tokens, attended_parts, other_weights, w_parts, w_router, qkv_weights = tied(
        tokens,
        attended_parts,
        other_weights,
        w_parts,
        w_router,
        (w_query, key_projection_weight, value_projection_weight),
    )
    resid_in = tokens.astype(F32)
    first_scale = norm_scale(resid_in)
    attended = attended_parts[0]

    def as_columns(weight):
        return weight.transpose(1, 0, 2).reshape(model_width, -1)

    chip_weights = [jnp.concatenate(pair) for pair in zip(expert_weights, other_weights)]
    gate_w, up_w = as_columns(chip_weights[0]), as_columns(chip_weights[1])
    down_w = chip_weights[2].reshape(-1, model_width)
    hidden = resid_in + mm(attended, w_output)
    for step in range(1, tensor_count):
        hidden = hidden + mm(attended_parts[step], w_parts[step - 1])
    second_scale = norm_scale(hidden)
    second_norm = (hidden * second_scale * norm2_gain).astype(BF16)

    local_names = jnp.concatenate(
        [
            expert_place * here + jnp.arange(here, dtype=jnp.int32),
            (expert_place ^ 1) * here + jnp.arange(here, dtype=jnp.int32),
        ]
    )
    router_wide = jnp.pad(w_router, ((0, 0), (0, LANES - experts)))
    if expert_count == 8:
        second_norm, grad_far = tied(second_norm, grad_far)
        grad_blocks = grad_blocks + grad_far

    def through_experts(normed, grad):
        return expert_block(
            local_names,
            normed,
            grad,
            router_wide,
            gate_w,
            up_w,
            down_w,
            experts,
            top_count,
            units,
        )

    if replicated:
        own_weight = jnp.concatenate(qkv_weights, axis=1)
        qkv_half = piece(own_weight, core, model_width // 2)
        second_norm, qkv_half = tied(second_norm, qkv_half)
        qkv_halves = [z_shift(qkv_half, step) for step in range(1, tensor_count)]
    if expert_count == 8:
        half = tok_count // 2
        from_x, from_y = swap(second_norm, 2), swap(second_norm, 4)
        own_done = through_experts(second_norm, grad_blocks[0])
        from_x, from_y, own_done = tied(from_x, from_y, own_done)
        normed_blocks = [
            second_norm, from_x, from_y, swap(from_x[:half], 4), swap(from_y[half:], 2)
        ]
        if replicated:
            normed_blocks[3:], qkv_halves = tied(normed_blocks[3:], qkv_halves)
            qkv_halves = jnp.stack(qkv_halves)
            qkv_others = swap(qkv_halves, 1)
            qkv_parts = jnp.where(
                core == 0,
                jnp.concatenate([qkv_halves, qkv_others], axis=1),
                jnp.concatenate([qkv_others, qkv_halves], axis=1),
            )
        done = [own_done]
    else:
        normed_blocks = plane_gather(second_norm)
        done = []
    if expert_count == 8:
        done.append(through_experts(normed_blocks[1], grad_blocks[1]))
        far_done = [through_experts(normed_blocks[i], grad_blocks[i]) for i in (3, 4)]
        normed_blocks[2], far_done = tied(normed_blocks[2], far_done)
        done.append(through_experts(normed_blocks[2], grad_blocks[2]))
        done += far_done
    else:
        done = [through_experts(normed, grad) for normed, grad in zip(normed_blocks, grad_blocks)]
    plane_rows, merged = plane_scatter([block[1] for block in done])
    plane_rows, *out_blocks = tied(plane_rows, *[block[0] for block in done])
    gate_grads, merged = tied([block[2] for block in done], merged)
    up_grads, plane_rows = tied([block[3] for block in done], plane_rows)
    inners = [block[4] for block in done]
    row_sum = z_scatter(plane_rows)
    out_far = plane_scatter_far(out_blocks)
    row_sum, out_far, inners = tied(row_sum, out_far, inners)
    gate_total = up_total = down_total = 0.0
    for normed, grad, gate_grad, up_grad, inner in zip(
        normed_blocks, grad_blocks, gate_grads, up_grads, inners
    ):
        gate_total = gate_total + mm_rows(normed, gate_grad)
        up_total = up_total + mm_rows(normed, up_grad)
        down_total = down_total + mm_rows(inner, grad[:, :model_width])
    plane_out, _ = plane_scatter(out_blocks, out_far)

    my_routing_grad = (
        row_sum[:, model_width : model_width + experts]
        + row_sum[:, model_width + experts : model_width + 2 * experts]
    )
    row_sum = row_sum[:, :model_width]

    def mine(array):
        return piece(array, tensor_place, own_rows)

    my_hidden, my_scale = mine(hidden), mine(second_scale)
    my_normed = mine(second_norm)
    names = jnp.arange(experts, dtype=jnp.int32)
    my_chosen = jnp.any(mine(expert_ids)[:, :, None] == names[None, None, :], axis=1)
    my_routing = route(my_normed, w_router, my_chosen)
    my_normed = my_normed.astype(F32)
    my_logits = my_routing * (
        my_routing_grad - jnp.sum(my_routing * my_routing_grad, axis=-1, keepdims=True)
    )
    router_float = w_router.astype(F32)
    grad_second = row_sum + jnp.dot(my_logits, router_float.T, precision=EXACT)
    grad_router = lax.dot_general(
        my_logits, my_normed, (((0,), (0,)), ((), ())), precision=EXACT
    )
    grad_norm2 = jnp.sum(grad_second * my_hidden * my_scale, axis=0)
    gained_two = grad_second * norm2_gain
    my_grad_hidden = (
        mine(cotangent).astype(F32)
        + my_scale * gained_two
        - my_hidden * my_scale**3 * jnp.mean(gained_two * my_hidden, axis=-1, keepdims=True)
    )
    small = jnp.concatenate([grad_router, grad_norm2[None]])
    extra = -small.shape[0] % 16
    small = jnp.pad(small, ((0, extra), (0, 0))).astype(BF16)
    parts = z_received(jnp.concatenate([my_grad_hidden.astype(BF16), small]))
    plane_out, gate_total, up_total, down_total, *parts = tied(
        plane_out, gate_total, up_total, down_total, *parts
    )
    routed = z_scatter(plane_out, axis=1)
    mixed = (piece(hidden, tensor_place, col_width, 1) + routed).astype(BF16)
    grad_branch = z_place([part[:own_rows] for part in parts])
    small = sum(part[own_rows:].astype(F32) for part in parts)
    grad_output = mm_rows(attended, grad_branch)

    if replicated:
        grad_raw, grad_first = attention_back(
            first_norm,
            own_weight[None],
            w_output[None],
            grad_branch,
            wide_cosine,
            wide_sine,
            q_width,
            k_width,
        )
        grad_raw = grad_raw[0]
        norm1_part = jnp.sum(grad_first * resid_in * first_scale, axis=0)[None]
    else:
        grad_heads = mm_cols(grad_branch, w_output).astype(BF16)
        grad_heads = grad_heads.reshape(tok_count, heads_kv, group_size, HEAD_DIMENSION)
        grad_queries, grad_keys, grad_values = attend_backward(
            query_rows, rotated_keys, value_rows, grad_heads, log_total
        )
        grad_query_raw = rotate(
            grad_queries.reshape(tok_count, heads_query, HEAD_DIMENSION), cosine, sine_table, -1.0
        )
        grad_query_raw = grad_query_raw.reshape(tok_count, -1).astype(BF16)
        grad_key_raw = rotate(grad_keys, cosine, sine_table, -1.0)
        grad_key_raw = grad_key_raw.reshape(tok_count, -1).astype(BF16)
        grad_value_raw = grad_values.reshape(tok_count, -1).astype(BF16)
        grad_raw = jnp.concatenate([grad_query_raw, grad_key_raw, grad_value_raw], axis=1)
        grad_first = (
            mm_cols(grad_query_raw, w_query)
            + mm_cols(grad_key_raw, key_projection_weight)
            + mm_cols(grad_value_raw, value_projection_weight)
        )
        norm1_part = jnp.sum(grad_first * resid_in * first_scale, axis=0)[None]

    grad_raw = mm_rows(first_norm, grad_raw)
    raw_width = grad_raw.shape[1]

    def folded(array):
        array = jnp.pad(array.astype(BF16), ((0, -array.shape[0] % 16), (0, 0)))
        return [array[:, i : i + raw_width] for i in range(0, model_width, raw_width)]

    pile = [grad_raw.astype(BF16)] + folded(grad_output) + folded(small) + folded(norm1_part)
    places = [0]
    for part in pile:
        places.append(places[-1] + part.shape[0])
    extra = -places[-1] % 128
    pile, (mixed, branch_first, gate_total, up_total), (branch_second, down_total) = expert_sum(
        jnp.concatenate(pile + [jnp.zeros((extra, raw_width), BF16)]),
        (mixed, grad_branch, gate_total, up_total),
        (grad_branch, down_total),
    )

    width = here * units

    def from_chip(total):
        return total[:, :width] + swap(total[:, width:].astype(BF16), 1).astype(F32)

    def as_experts(total):
        return total.reshape(model_width, here, units).transpose(1, 0, 2)

    grad_gate = as_experts(from_chip(gate_total))
    up_weight_gradient = as_experts(from_chip(up_total))
    grad_down = down_total[:width] + swap(down_total[width:].astype(BF16), 1).astype(F32)
    grad_down = grad_down.reshape(here, units, model_width)
    grad_weights = pile[: places[1]]
    folds = model_width // raw_width

    def unfolded(first, rows):
        return jnp.concatenate(
            [pile[places[i] : places[i] + rows] for i in range(first, first + folds)], axis=1
        )

    grad_output = unfolded(1, grad_output.shape[0])
    small = unfolded(1 + folds, experts + 1)
    grad_norm1 = sum(z_received(unfolded(1 + 2 * folds, 1)))[0]

    def first_norm_back(grad_first, grad_hidden, resid, scale):
        gained = grad_first * norm1_gain
        return (
            grad_hidden
            + scale * gained
            - resid * scale**3 * jnp.mean(gained * resid, axis=-1, keepdims=True)
        )

    if replicated:
        branches = [branch_first] + [branch_second] * (tensor_count - 2)
        for step, branch in enumerate(branches):
            _, part_first = attention_back(
                first_norm,
                qkv_parts[step][None],
                w_parts[step][None],
                branch,
                wide_cosine,
                wide_sine,
                q_width,
                k_width,
            )
            grad_first = grad_first + part_first
        grad_input = first_norm_back(
            grad_first, grad_branch.astype(F32), resid_in, first_scale
        )
    else:
        my_grad_input = first_norm_back(
            z_scatter(grad_first), my_grad_hidden, mine(resid_in), mine(first_scale)
        )
        grad_input = z_place(z_received(my_grad_input.astype(BF16))).astype(F32)

    return (
        mixed,
        grad_input,
        grad_norm1,
        grad_weights[:, :q_width],
        grad_weights[:, q_width : q_width + k_width],
        grad_weights[:, q_width + k_width :],
        grad_output,
        small[experts],
        small[:experts].T,
        grad_gate,
        up_weight_gradient,
        grad_down,
    )


def solution(mesh):
    placed = (
        P("expert", None),
        P(),
        P(None, "tensor"),
        P(None, "tensor"),
        P(None, "tensor"),
        P("tensor", None),
        P(),
        P(),
        P("expert", None, "tensor"),
        P("expert", None, "tensor"),
        P("expert", "tensor", None),
        P("expert", None),
        P("expert", None),
    )
    return jax.shard_map(
        local,
        mesh=mesh,
        in_specs=placed,
        out_specs=(
            P("expert", "tensor"),
            P("expert", None),
            P(),
            P(None, "tensor"),
            P(None, "tensor"),
            P(None, "tensor"),
            P("tensor", None),
            P(),
            P(),
            P("expert", None, "tensor"),
            P("expert", None, "tensor"),
            P("expert", "tensor", None),
        ),
        check_vma=False,
    )
```

```python
import functools
import math

import jax
import jax.numpy as jnp
from jax import lax
from jax.experimental import pallas as pl
from jax.experimental.pallas import tpu as pltpu
from jax.sharding import PartitionSpec as P

HEAD_DIMENSION = 64
SEQ_LEN = 512

EPS = 1e-06
SCALE = 0.125
NEGATIVE = -1e30
THETA = 10000.0
F32 = jnp.float32
BF16 = jnp.bfloat16
EXACT = lax.Precision.HIGHEST
LANES = 128
TILE = 256


def tables(tok_count):
    half = HEAD_DIMENSION // 2
    freq = jnp.exp(-math.log(THETA) * jnp.arange(half, dtype=F32) / half)
    places = (jnp.arange(tok_count) % SEQ_LEN).astype(F32)
    angle = places[:, None] * freq[None, :]
    return (jnp.cos(angle)[:, None, :], jnp.sin(angle)[:, None, :])


def rotate(field, cosine, sine_table, factor):
    half = HEAD_DIMENSION // 2
    first = field[..., :half]
    second = field[..., half:]
    return jnp.concatenate(
        [
            first * cosine - factor * second * sine_table,
            second * cosine + factor * first * sine_table,
        ],
        axis=-1,
    )


def causal_mask():
    places = jnp.arange(SEQ_LEN)
    return places[:, None] >= places[None, :]


def attend_forward(query_rows, rotated_keys, value_rows):
    scores = (
        jnp.einsum("lkgd,mkd->kglm", query_rows, rotated_keys, preferred_element_type=F32) * SCALE
    )
    scores = jnp.where(causal_mask(), scores, NEGATIVE)
    highest = jnp.max(scores, axis=-1, keepdims=True)
    expanded = jnp.exp(scores - highest)
    summed = jnp.sum(expanded, axis=-1, keepdims=True)
    probability = (expanded / summed).astype(BF16)
    heads_out = jnp.einsum("kglm,mkd->lkgd", probability, value_rows, preferred_element_type=F32)
    return (heads_out.astype(BF16), (highest + jnp.log(summed))[..., 0])


def attend_backward(query_rows, rotated_keys, value_rows, grad_heads, log_total):
    scores = (
        jnp.einsum("lkgd,mkd->kglm", query_rows, rotated_keys, preferred_element_type=F32) * SCALE
    )
    probability = jnp.where(causal_mask(), jnp.exp(scores - log_total[..., None]), 0.0)
    prob_low = probability.astype(BF16)
    grad_values = jnp.einsum("kglm,lkgd->mkd", prob_low, grad_heads, preferred_element_type=F32)
    grad_prob = jnp.einsum("lkgd,mkd->kglm", grad_heads, value_rows, preferred_element_type=F32)
    row_delta = jnp.sum(probability * grad_prob, axis=-1, keepdims=True)
    grad_scores = (probability * (grad_prob - row_delta)).astype(BF16)
    grad_queries = (
        jnp.einsum("kglm,mkd->lkgd", grad_scores, rotated_keys, preferred_element_type=F32) * SCALE
    )
    grad_keys = (
        jnp.einsum("kglm,lkgd->mkd", grad_scores, query_rows, preferred_element_type=F32) * SCALE
    )
    return (grad_queries, grad_keys, grad_values)


def mm(left, right):
    return jnp.dot(left, right, preferred_element_type=F32)


def mm_rows(left, right):
    return lax.dot_general(left, right, (((0,), (0,)), ((), ())), preferred_element_type=F32)


def mm_cols(left, right):
    return lax.dot_general(left, right, (((1,), (1,)), ((), ())), preferred_element_type=F32)


def piece(array, index, size, axis=0):
    return lax.dynamic_slice_in_dim(array, index * size, size, axis)


def swap(array, mask):
    size = lax.axis_size("expert")
    return lax.ppermute(array, "expert", [(i, i ^ mask) for i in range(size)])


def z_shift(array, step):
    size = lax.axis_size("tensor")
    return lax.ppermute(array, "tensor", [(i, (i + step) % size) for i in range(size)])


def z_received(array):
    return [array] + [z_shift(array, step) for step in range(1, lax.axis_size("tensor"))]


def z_place(parts):
    size, mine = lax.axis_size("tensor"), lax.axis_index("tensor")
    rows = parts[0].shape[0]
    whole = jnp.zeros((rows * size,) + parts[0].shape[1:], parts[0].dtype)
    for step, part in enumerate(parts):
        whole = lax.dynamic_update_slice_in_dim(whole, part, (mine + size - step) % size * rows, 0)
    return whole


def z_scatter(array, axis=0):
    size, mine = lax.axis_size("tensor"), lax.axis_index("tensor")
    width = array.shape[axis] // size
    total = piece(array, mine, width, axis).astype(F32)
    for step in range(1, size):
        sent = piece(array, (mine + step) % size, width, axis).astype(BF16)
        total = total + z_shift(sent, step).astype(F32)
    return total


def same_core_groups():
    size = lax.axis_size("expert")
    return [list(range(0, size, 2)), list(range(1, size, 2))]


def plane_gather(array):
    if lax.axis_size("expert") != 8:
        return [
            lax.all_gather(
                array, "expert", axis=0, tiled=True, axis_index_groups=same_core_groups()
            )
        ]
    half = array.shape[0] // 2
    from_x = swap(array, 2)
    from_y = swap(array, 4)
    return [array, from_x, from_y, swap(from_x[:half], 4), swap(from_y[half:], 2)]


def plane_scatter_far(blocks):
    return [swap(blocks[3], 2), swap(blocks[4], 4)] if len(blocks) == 5 else []


def plane_scatter(blocks, far=()):
    if lax.axis_size("expert") != 8:
        return lax.psum_scatter(
            blocks[0].astype(BF16),
            "expert",
            scatter_dimension=0,
            tiled=True,
            axis_index_groups=same_core_groups(),
        ).astype(F32), ()
    own, for_x, for_y, far_x, far_y = blocks
    half = own.shape[0] // 2
    via_x, via_y = far if far else plane_scatter_far(blocks)
    via_x, via_y = via_x.astype(F32), via_y.astype(F32)
    for_y = for_y.at[:half].set((for_y[:half].astype(F32) + via_x).astype(BF16))
    for_x = for_x.at[half:].set((for_x[half:].astype(F32) + via_y).astype(BF16))
    total = own.astype(F32) + swap(for_x, 2).astype(F32) + swap(for_y, 4).astype(F32)
    return total, (for_x, for_y)


def expert_sum(array, late, first=(), second=()):
    if lax.axis_size("expert") != 8:
        array, late = lax.psum((array.astype(BF16), late.astype(BF16)), "expert")
        return array.astype(F32), late.astype(F32), first, second
    place = lax.axis_index("expert")
    core, chip = place % 2, place // 2
    half = array.shape[0] // 2
    rows = half // 4
    array = array.astype(BF16)
    mine = piece(array, core, half).astype(F32)
    mine = mine + swap(piece(array, 1 - core, half), 1).astype(F32)
    mine, first = tied(mine, first)
    total = piece(mine, chip, rows)
    for mask in (1, 2, 3):
        total = total + swap(piece(mine, chip ^ mask, rows).astype(BF16), 2 * mask).astype(F32)
    total, second = tied(total.astype(BF16), second)
    late_rows = late.shape[0]
    total = jnp.concatenate([total, late.astype(BF16)])
    gathered = jnp.zeros((half + late_rows,) + array.shape[1:], BF16)
    late = 0.0
    for mask in (0, 1, 2, 3):
        part = swap(total, 2 * mask) if mask else total
        late = late + part[rows:].astype(F32)
        gathered = lax.dynamic_update_slice_in_dim(gathered, part[:rows], (chip ^ mask) * rows, 0)
    gathered = lax.dynamic_update_slice_in_dim(gathered, late.astype(BF16), half, 0)
    other = swap(gathered, 1)
    late = late + other[half:].astype(F32)
    both = jnp.concatenate([gathered[:half], gathered[:half]])
    both = lax.dynamic_update_slice_in_dim(both, other[:half], (1 - core) * half, 0)
    return both.astype(F32), late, first, second


def expert_kernel(
    experts,
    top_count,
    units,
    names_ref,
    normed_ref,
    grad_ref,
    router_ref,
    gate_ref,
    up_ref,
    down_ref,
    other_gate_ref,
    other_up_ref,
    other_down_ref,
    out_ref,
    rows_ref,
    gate_grad_ref,
    up_grad_ref,
    inner_ref,
):
    tile, model_width = normed_ref.shape
    here = gate_ref.shape[0]
    width = 2 * here * units

    def joined(own_ref, other_ref, chosen_units, axis):
        parts = [own_ref[e] if e < here else other_ref[e - here] for e in chosen_units]
        return jnp.concatenate(parts, axis=axis) if len(parts) > 1 else parts[0]

    normed = normed_ref[...]
    grad = grad_ref[:, :model_width]
    chosen_names = grad_ref[:, model_width:].astype(F32)
    lane = lax.broadcasted_iota(jnp.int32, (tile, LANES), 1)
    lane_float = lane.astype(F32)
    chosen = lane_float == chosen_names[:, 0:1]
    for k in range(1, top_count):
        chosen = chosen | (lane_float == chosen_names[:, k : k + 1])
    logits = jnp.where(chosen, mm(normed, router_ref[...]), NEGATIVE)
    expanded = jnp.exp(logits - jnp.max(logits, axis=-1, keepdims=True))
    expanded = jnp.where(chosen, expanded, 0.0)
    routing = expanded / jnp.sum(expanded, axis=-1, keepdims=True)
    grad_routing = jnp.zeros((tile, LANES), F32)
    columns = min(TILE, width)
    for start in range(0, width, columns):
        part = slice(start, start + columns)
        held = range(start // units, (start + columns) // units)
        gate_act = mm(normed, joined(gate_ref, other_gate_ref, held, 1))
        up_act = mm(normed, joined(up_ref, other_up_ref, held, 1))
        grad_plain = mm_cols(grad, joined(down_ref, other_down_ref, held, 0))
        weights = []
        for e in range(start // units, (start + columns) // units):
            weight = jnp.sum(
                jnp.where(lane == names_ref[e], routing, 0.0), axis=-1, keepdims=True
            )
            weights.append(jnp.broadcast_to(weight, (tile, units)))
        wide = jnp.concatenate(weights, axis=1) if len(weights) > 1 else weights[0]
        sigmoid_gate = jax.nn.sigmoid(gate_act)
        swish = gate_act * sigmoid_gate
        inner = swish * up_act
        inner_grad = inner * grad_plain
        for i, e in enumerate(range(start // units, (start + columns) // units)):
            total = jnp.sum(inner_grad[:, i * units : (i + 1) * units], axis=-1, keepdims=True)
            grad_routing = jnp.where(lane == names_ref[e], total, grad_routing)
        grad_inner = grad_plain * wide
        inner_ref[:, part] = (inner * wide).astype(BF16)
        up_grad_ref[:, part] = (grad_inner * swish).astype(BF16)
        gate_grad_ref[:, part] = (
            grad_inner * up_act * (sigmoid_gate + swish * (1.0 - sigmoid_gate))
        ).astype(BF16)
    rounded = grad_routing.astype(BF16).astype(F32)
    left = pltpu.roll(grad_routing - rounded, experts, 1)
    rows_ref[:, model_width:] = (rounded + left).astype(BF16)
    held = range(2 * here)
    rows_ref[:, :model_width] = (
        mm_cols(gate_grad_ref[...], joined(gate_ref, other_gate_ref, held, 1))
        + mm_cols(up_grad_ref[...], joined(up_ref, other_up_ref, held, 1))
    ).astype(BF16)
    out_ref[...] = mm(inner_ref[...], joined(down_ref, other_down_ref, held, 0)).astype(BF16)


def expert_block(names, normed, grad, router, weights, experts, top_count):
    rows, model_width = normed.shape
    units = weights[0].shape[2]
    width = 2 * weights[0].shape[0] * units
    tile = min(TILE, rows)

    def tiled(columns):
        return pl.BlockSpec((tile, columns), lambda i, names: (i, 0))

    def fixed(array):
        return pl.BlockSpec(array.shape, lambda i, names: (0,) * array.ndim)

    def shaped(columns):
        return jax.ShapeDtypeStruct((rows, columns), BF16)

    return pl.pallas_call(
        functools.partial(expert_kernel, experts, top_count, units),
        grid_spec=pltpu.PrefetchScalarGridSpec(
            num_scalar_prefetch=1,
            grid=(rows // tile,),
            in_specs=[
                tiled(model_width),
                tiled(model_width + LANES),
                fixed(router),
            ]
            + [fixed(weight) for weight in weights],
            out_specs=[
                tiled(model_width),
                tiled(model_width + LANES),
                tiled(width),
                tiled(width),
                tiled(width),
            ],
        ),
        out_shape=[
            shaped(model_width),
            shaped(model_width + LANES),
            shaped(width),
            shaped(width),
            shaped(width),
        ],
        compiler_params=pltpu.CompilerParams(vmem_limit_bytes=60 * 1024 * 1024),
        cost_estimate=pl.CostEstimate(
            flops=12 * rows * model_width * width,
            bytes_accessed=6 * model_width * width + 14 * rows * model_width,
            transcendentals=rows * width,
        ),
        name="experts",
    )(names, normed, grad, router, *weights)


def half_turn(field, cosine, sine):
    width = field.shape[1]
    half = HEAD_DIMENSION // 2
    lane = lax.broadcasted_iota(jnp.int32, field.shape, 1)
    partner = jnp.where(
        lane % HEAD_DIMENSION < half,
        pltpu.roll(field, width - half, 1),
        pltpu.roll(field, half, 1),
    )
    repeats = width // cosine.shape[1]
    cosine = jnp.concatenate([cosine] * repeats, axis=1)
    sine = jnp.concatenate([sine] * repeats, axis=1)
    return field * cosine + partner * sine


def forward_kernel(
    tokens_ref, gain_ref, query_ref, key_ref, value_ref, cosine_ref, sine_ref, normed_ref, out_ref
):
    size = HEAD_DIMENSION
    tokens = tokens_ref[...].astype(F32)
    normed = (tokens * norm_scale(tokens) * gain_ref[...]).astype(BF16)
    normed_ref[...] = normed
    cosine, sine = cosine_ref[...], sine_ref[...]
    queries = half_turn(mm(normed, query_ref[...]), cosine, sine).astype(BF16)
    keys = half_turn(mm(normed, key_ref[...]), cosine, sine).astype(BF16)
    values = mm(normed, value_ref[...]).astype(BF16)
    group = queries.shape[1] // keys.shape[1]
    tile = tokens.shape[0] // 2
    for t in range(2):
        heads = []
        seen = (t + 1) * tile
        for h in range(queries.shape[1] // size):
            g = h // group
            query = queries[t * tile : seen, h * size : (h + 1) * size]
            scores = mm_cols(query, keys[:seen, g * size : (g + 1) * size]) * SCALE
            place = lax.broadcasted_iota(jnp.int32, scores.shape, 0) + t * tile
            other = lax.broadcasted_iota(jnp.int32, scores.shape, 1)
            scores = jnp.where(place >= other, scores, NEGATIVE)
            expanded = jnp.exp(scores - jnp.max(scores, axis=-1, keepdims=True))
            probability = expanded * (1.0 / jnp.sum(expanded, axis=-1, keepdims=True))
            heads.append(mm(probability.astype(BF16), values[:seen, g * size : (g + 1) * size]))
        out_ref[t * tile : seen, :] = jnp.concatenate(heads, axis=1).astype(BF16)


def attention_forward(tokens, gain, query_w, key_w, value_w, cosine, sine):
    rows, model_width = tokens.shape
    return pl.pallas_call(
        forward_kernel,
        out_shape=[
            jax.ShapeDtypeStruct((rows, model_width), BF16),
            jax.ShapeDtypeStruct((rows, query_w.shape[1]), BF16),
        ],
        compiler_params=pltpu.CompilerParams(vmem_limit_bytes=32 * 1024 * 1024),
        cost_estimate=pl.CostEstimate(
            flops=4 * rows * model_width * query_w.shape[1],
            bytes_accessed=4 * rows * model_width,
            transcendentals=rows * rows * 4,
        ),
        name="forward",
    )(tokens, gain[None], query_w, key_w, value_w, cosine, sine)


def attention_kernel(
    q_width,
    k_width,
    normed_ref,
    weight_ref,
    output_ref,
    grad_ref,
    cosine_ref,
    sine_ref,
    raw_ref,
    first_ref,
):
    size = HEAD_DIMENSION
    rows = normed_ref.shape[0]
    turned = q_width + k_width
    group = q_width // k_width
    weight = weight_ref[0]
    cosine, sine = cosine_ref[...], sine_ref[...]
    projected = mm(normed_ref[...], weight)
    rotated = half_turn(projected[:, :turned], cosine, sine).astype(BF16)
    values = projected[:, turned:].astype(BF16)
    grad_heads = mm_cols(grad_ref[...], output_ref[0]).astype(BF16)
    tile = rows // 2
    grad_queries, grad_keys, grad_values = [], [], []
    for g in range(k_width // size):
        key = rotated[:, q_width + g * size : q_width + (g + 1) * size]
        value = values[:, g * size : (g + 1) * size]
        key_parts, value_parts = [0.0, 0.0], [0.0, 0.0]
        for h in range(g * group, (g + 1) * group):
            query = rotated[:, h * size : (h + 1) * size]
            grad_head = grad_heads[:, h * size : (h + 1) * size]
            query_parts = []
            for t in range(2):
                here = slice(t * tile, (t + 1) * tile)
                seen = (t + 1) * tile
                scores = mm_cols(query[here], key[:seen]) * SCALE
                place = lax.broadcasted_iota(jnp.int32, scores.shape, 0) + t * tile
                other = lax.broadcasted_iota(jnp.int32, scores.shape, 1)
                scores = jnp.where(place >= other, scores, NEGATIVE)
                expanded = jnp.exp(scores - jnp.max(scores, axis=-1, keepdims=True))
                probability = expanded * (1.0 / jnp.sum(expanded, axis=-1, keepdims=True))
                grad_prob = mm_cols(grad_head[here], value[:seen])
                delta = jnp.sum(probability * grad_prob, axis=-1, keepdims=True)
                grad_scores = (probability * (grad_prob - delta)).astype(BF16)
                query_parts.append(mm(grad_scores, key[:seen]) * SCALE)
                from_keys = mm_rows(grad_scores, query[here])
                from_values = mm_rows(probability.astype(BF16), grad_head[here])
                for u in range(t + 1):
                    block = slice(u * tile, (u + 1) * tile)
                    key_parts[u] = key_parts[u] + from_keys[block]
                    value_parts[u] = value_parts[u] + from_values[block]
            grad_queries.append(jnp.concatenate(query_parts, axis=0))
        grad_keys.append(jnp.concatenate(key_parts, axis=0) * SCALE)
        grad_values.append(jnp.concatenate(value_parts, axis=0))
    grad_turned = jnp.concatenate(grad_queries + grad_keys, axis=1)
    raw_ref[0, :, :turned] = half_turn(grad_turned, cosine, -sine).astype(BF16)
    raw_ref[0, :, turned:] = jnp.concatenate(grad_values, axis=1).astype(BF16)
    total = mm_cols(raw_ref[0], weight)

    @pl.when(pl.program_id(0) == 0)
    def _():
        first_ref[...] = total

    @pl.when(pl.program_id(0) > 0)
    def _():
        first_ref[...] += total


def attention_back(normed, weights, outputs, grad, cosine, sine, q_width, k_width):
    parts, model_width, width = weights.shape
    rows = normed.shape[0]

    def fixed(array):
        return pl.BlockSpec(array.shape, lambda i: (0, 0))

    def stacked(array):
        return pl.BlockSpec((1,) + array.shape[1:], lambda i: (i, 0, 0))

    raw = jax.ShapeDtypeStruct((parts, rows, width), BF16)
    return pl.pallas_call(
        functools.partial(attention_kernel, q_width, k_width),
        grid=(parts,),
        in_specs=[
            fixed(normed),
            stacked(weights),
            stacked(outputs),
            fixed(grad),
            fixed(cosine),
            fixed(sine),
        ],
        out_specs=[stacked(raw), pl.BlockSpec((rows, model_width), lambda i: (0, 0))],
        out_shape=[raw, jax.ShapeDtypeStruct((rows, model_width), F32)],
        compiler_params=pltpu.CompilerParams(vmem_limit_bytes=40 * 1024 * 1024),
        cost_estimate=pl.CostEstimate(
            flops=parts * 6 * rows * model_width * width,
            bytes_accessed=parts * 2 * model_width * width + 8 * rows * model_width,
            transcendentals=parts * rows * rows * 4,
        ),
        name="attention",
    )(normed, weights, outputs, grad, cosine, sine)


def tied(*arrays):
    return lax.optimization_barrier(arrays)


def norm_scale(field):
    return lax.rsqrt(jnp.mean(field * field, axis=-1, keepdims=True) + EPS)


def route(normed, router, chosen):
    logits = mm(normed, router)
    masked = jnp.where(chosen, logits, NEGATIVE)
    highest = jnp.max(masked, axis=-1, keepdims=True)
    expanded = jnp.where(chosen, jnp.exp(masked - highest), 0.0)
    return expanded / jnp.sum(expanded, axis=-1, keepdims=True)


def local(
    tokens,
    norm1_gain,
    w_query,
    key_projection_weight,
    value_projection_weight,
    w_output,
    norm2_gain,
    w_router,
    expert_gate_weight,
    expert_up_weight,
    expert_down_weight,
    expert_ids,
    cotangent,
):
    tok_count = tokens.shape[0]
    model_width = tokens.shape[1]
    experts, top_count = w_router.shape[1], expert_ids.shape[1]
    here, units = expert_gate_weight.shape[0], expert_gate_weight.shape[2]
    heads_query = w_query.shape[1] // HEAD_DIMENSION
    heads_kv = key_projection_weight.shape[1] // HEAD_DIMENSION
    group_size = heads_query // heads_kv
    cosine, sine_table = tables(tok_count)
    expert_count = lax.axis_size("expert")
    tensor_count = lax.axis_size("tensor")
    expert_place = lax.axis_index("expert")
    tensor_place = lax.axis_index("tensor")
    core = expert_place % 2
    own_rows = tok_count // tensor_count
    col_width = model_width // tensor_count

    names_wide = jnp.pad(expert_ids.astype(BF16), ((0, 0), (0, LANES - top_count)))
    grad_blocks = plane_gather(jnp.concatenate([cotangent, names_wide], axis=1))
    if expert_count == 8:
        grad_blocks, grad_far = grad_blocks[:3], grad_blocks[3:]

    half = w_output.shape[0] // 2
    w_halves = [z_shift(piece(w_output, core, half), step) for step in range(1, tensor_count)]
    expert_weights = [expert_gate_weight, expert_up_weight, expert_down_weight]
    if expert_count == 8:
        grad_blocks, w_halves = tied(grad_blocks, w_halves)
    w_halves = jnp.stack(w_halves)
    w_others = swap(w_halves, 1)
    w_parts = jnp.where(
        core == 0,
        jnp.concatenate([w_halves, w_others], axis=1),
        jnp.concatenate([w_others, w_halves], axis=1),
    )

    q_width, k_width = w_query.shape[1], key_projection_weight.shape[1]
    replicated = expert_count == 8 and k_width % LANES == 0
    resid_in = tokens.astype(F32)
    first_scale = norm_scale(resid_in)
    if replicated:
        wide_cosine = jnp.concatenate([cosine[:, 0]] * (LANES // 32), axis=1)
        signed = jnp.concatenate([-sine_table[:, 0], sine_table[:, 0]], axis=1)
        wide_sine = jnp.concatenate([signed] * (LANES // HEAD_DIMENSION), axis=1)
        first_norm, attended = attention_forward(
            tokens,
            norm1_gain,
            w_query,
            key_projection_weight,
            value_projection_weight,
            wide_cosine,
            wide_sine,
        )
    else:
        first_norm = (resid_in * first_scale * norm1_gain).astype(BF16)
        query_raw = mm(first_norm, w_query).reshape(tok_count, heads_query, HEAD_DIMENSION)
        key_raw = mm(first_norm, key_projection_weight).reshape(tok_count, heads_kv, HEAD_DIMENSION)
        query_rows = (
            rotate(query_raw, cosine, sine_table, 1.0)
            .astype(BF16)
            .reshape(tok_count, heads_kv, group_size, HEAD_DIMENSION)
        )
        rotated_keys = rotate(key_raw, cosine, sine_table, 1.0).astype(BF16)
        value_rows = (
            mm(first_norm, value_projection_weight)
            .astype(BF16)
            .reshape(tok_count, heads_kv, HEAD_DIMENSION)
        )
        attended, log_total = attend_forward(query_rows, rotated_keys, value_rows)
        attended = attended.reshape(tok_count, heads_query * HEAD_DIMENSION)

    attended_parts = z_received(attended)

    tokens, attended_parts, expert_weights, w_parts, w_router, qkv_weights = tied(
        tokens,
        attended_parts,
        expert_weights,
        w_parts,
        w_router,
        (w_query, key_projection_weight, value_projection_weight),
    )
    other_weights = [swap(weight, 1) for weight in expert_weights]
    resid_in = tokens.astype(F32)
    first_scale = norm_scale(resid_in)
    attended = attended_parts[0]

    hidden = resid_in + mm(attended, w_output)
    for step in range(1, tensor_count):
        hidden = hidden + mm(attended_parts[step], w_parts[step - 1])
    second_scale = norm_scale(hidden)
    second_norm = (hidden * second_scale * norm2_gain).astype(BF16)

    local_names = jnp.concatenate(
        [
            expert_place * here + jnp.arange(here, dtype=jnp.int32),
            (expert_place ^ 1) * here + jnp.arange(here, dtype=jnp.int32),
        ]
    )
    router_wide = jnp.pad(w_router, ((0, 0), (0, LANES - experts)))
    if expert_count == 8:
        second_norm, grad_far = tied(second_norm, grad_far)
        grad_blocks = grad_blocks + grad_far

    def through_experts(normed, grad):
        return expert_block(
            local_names,
            normed,
            grad,
            router_wide,
            expert_weights + other_weights,
            experts,
            top_count,
        )

    if replicated:
        own_weight = jnp.concatenate(qkv_weights, axis=1)
        qkv_half = piece(own_weight, core, model_width // 2)
        other_weights, qkv_half = tied(other_weights, qkv_half)
        qkv_halves = [z_shift(qkv_half, step) for step in range(1, tensor_count)]
    if expert_count == 8:
        half = tok_count // 2
        from_x, from_y = swap(second_norm, 2), swap(second_norm, 4)
        own_done = through_experts(second_norm, grad_blocks[0])
        from_x, from_y, own_done = tied(from_x, from_y, own_done)
        normed_blocks = [
            second_norm, from_x, from_y, swap(from_x[:half], 4), swap(from_y[half:], 2)
        ]
        if replicated:
            own_done, qkv_halves = tied(own_done, qkv_halves)
            qkv_halves = jnp.stack(qkv_halves)
            qkv_others = swap(qkv_halves, 1)
            qkv_parts = jnp.where(
                core == 0,
                jnp.concatenate([qkv_halves, qkv_others], axis=1),
                jnp.concatenate([qkv_others, qkv_halves], axis=1),
            )
        done = [own_done]
    else:
        normed_blocks = plane_gather(second_norm)
        done = []
    if expert_count == 8:
        done.append(through_experts(normed_blocks[1], grad_blocks[1]))
        far_done = [through_experts(normed_blocks[i], grad_blocks[i]) for i in (3, 4)]
        normed_blocks[2], far_done = tied(normed_blocks[2], far_done)
        done.append(through_experts(normed_blocks[2], grad_blocks[2]))
        done += far_done
    else:
        done = [through_experts(normed, grad) for normed, grad in zip(normed_blocks, grad_blocks)]
    plane_rows, merged = plane_scatter([block[1] for block in done])
    plane_rows, *out_blocks = tied(plane_rows, *[block[0] for block in done])
    gate_grads, merged = tied([block[2] for block in done], merged)
    up_grads, plane_rows = tied([block[3] for block in done], plane_rows)
    inners = [block[4] for block in done]
    row_sum = z_scatter(plane_rows)
    out_far = plane_scatter_far(out_blocks)
    row_sum, out_far, inners = tied(row_sum, out_far, inners)
    gate_total = up_total = down_total = 0.0
    for normed, grad, gate_grad, up_grad, inner in zip(
        normed_blocks, grad_blocks, gate_grads, up_grads, inners
    ):
        gate_total = gate_total + mm_rows(normed, gate_grad)
        up_total = up_total + mm_rows(normed, up_grad)
        down_total = down_total + mm_rows(inner, grad[:, :model_width])
    plane_out, _ = plane_scatter(out_blocks, out_far)

    my_routing_grad = (
        row_sum[:, model_width : model_width + experts]
        + row_sum[:, model_width + experts : model_width + 2 * experts]
    )
    row_sum = row_sum[:, :model_width]

    def mine(array):
        return piece(array, tensor_place, own_rows)

    my_hidden, my_scale = mine(hidden), mine(second_scale)
    my_normed = mine(second_norm)
    names = jnp.arange(experts, dtype=jnp.int32)
    my_chosen = jnp.any(mine(expert_ids)[:, :, None] == names[None, None, :], axis=1)
    my_routing = route(my_normed, w_router, my_chosen)
    my_normed = my_normed.astype(F32)
    my_logits = my_routing * (
        my_routing_grad - jnp.sum(my_routing * my_routing_grad, axis=-1, keepdims=True)
    )
    router_float = w_router.astype(F32)
    grad_second = row_sum + jnp.dot(my_logits, router_float.T, precision=EXACT)
    grad_router = lax.dot_general(
        my_logits, my_normed, (((0,), (0,)), ((), ())), precision=EXACT
    )
    grad_norm2 = jnp.sum(grad_second * my_hidden * my_scale, axis=0)
    gained_two = grad_second * norm2_gain
    my_grad_hidden = (
        mine(cotangent).astype(F32)
        + my_scale * gained_two
        - my_hidden * my_scale**3 * jnp.mean(gained_two * my_hidden, axis=-1, keepdims=True)
    )
    small = jnp.concatenate([grad_router, grad_norm2[None]])
    extra = -small.shape[0] % 16
    small = jnp.pad(small, ((0, extra), (0, 0))).astype(BF16)
    parts = z_received(jnp.concatenate([my_grad_hidden.astype(BF16), small]))
    plane_out, gate_total, up_total, down_total, *parts = tied(
        plane_out, gate_total, up_total, down_total, *parts
    )
    routed = z_scatter(plane_out, axis=1)
    mixed = (piece(hidden, tensor_place, col_width, 1) + routed).astype(BF16)
    grad_branch = z_place([part[:own_rows] for part in parts])
    small = sum(part[own_rows:].astype(F32) for part in parts)
    grad_output = mm_rows(attended, grad_branch)

    if replicated:
        grad_raw, grad_first = attention_back(
            first_norm,
            own_weight[None],
            w_output[None],
            grad_branch,
            wide_cosine,
            wide_sine,
            q_width,
            k_width,
        )
        grad_raw = grad_raw[0]
        norm1_part = jnp.sum(grad_first * resid_in * first_scale, axis=0)[None]
    else:
        grad_heads = mm_cols(grad_branch, w_output).astype(BF16)
        grad_heads = grad_heads.reshape(tok_count, heads_kv, group_size, HEAD_DIMENSION)
        grad_queries, grad_keys, grad_values = attend_backward(
            query_rows, rotated_keys, value_rows, grad_heads, log_total
        )
        grad_query_raw = rotate(
            grad_queries.reshape(tok_count, heads_query, HEAD_DIMENSION), cosine, sine_table, -1.0
        )
        grad_query_raw = grad_query_raw.reshape(tok_count, -1).astype(BF16)
        grad_key_raw = rotate(grad_keys, cosine, sine_table, -1.0)
        grad_key_raw = grad_key_raw.reshape(tok_count, -1).astype(BF16)
        grad_value_raw = grad_values.reshape(tok_count, -1).astype(BF16)
        grad_raw = jnp.concatenate([grad_query_raw, grad_key_raw, grad_value_raw], axis=1)
        grad_first = (
            mm_cols(grad_query_raw, w_query)
            + mm_cols(grad_key_raw, key_projection_weight)
            + mm_cols(grad_value_raw, value_projection_weight)
        )
        norm1_part = jnp.sum(grad_first * resid_in * first_scale, axis=0)[None]

    grad_raw = mm_rows(first_norm, grad_raw)
    raw_width = grad_raw.shape[1]

    def folded(array):
        array = jnp.pad(array.astype(BF16), ((0, -array.shape[0] % 16), (0, 0)))
        return [array[:, i : i + raw_width] for i in range(0, model_width, raw_width)]

    pile = [grad_raw.astype(BF16)] + folded(grad_output) + folded(small)
    norm1_part = jnp.pad(norm1_part.reshape(-1, raw_width), ((0, 16 - model_width // raw_width), (0, 0)))
    norm1_part = sum(z_received(norm1_part))
    places = [0]
    for part in pile:
        places.append(places[-1] + part.shape[0])
    extra = -places[-1] % 128
    pile = jnp.concatenate(pile + [jnp.zeros((extra, raw_width), BF16)])
    pile, branch_zero = tied(pile, grad_branch)
    pile, late, (branch_first, down_total), (mixed, branch_second) = expert_sum(
        pile, norm1_part, (grad_branch, down_total), (mixed, grad_branch)
    )

    width = here * units

    def from_chip(total):
        return total[:, :width] + swap(total[:, width:].astype(BF16), 1).astype(F32)

    def as_experts(total):
        return total.reshape(model_width, here, units).transpose(1, 0, 2)

    grad_gate = as_experts(from_chip(gate_total))
    up_weight_gradient = as_experts(from_chip(up_total))
    grad_down = down_total[:width] + swap(down_total[width:].astype(BF16), 1).astype(F32)
    grad_down = grad_down.reshape(here, units, model_width)
    grad_weights = pile[: places[1]]
    folds = model_width // raw_width

    def unfolded(first, rows):
        return jnp.concatenate(
            [pile[places[i] : places[i] + rows] for i in range(first, first + folds)], axis=1
        )

    grad_output = unfolded(1, grad_output.shape[0])
    small = unfolded(1 + folds, experts + 1)
    grad_norm1 = late[:folds].reshape(-1)

    def first_norm_back(grad_first, grad_hidden, resid, scale):
        gained = grad_first * norm1_gain
        return (
            grad_hidden
            + scale * gained
            - resid * scale**3 * jnp.mean(gained * resid, axis=-1, keepdims=True)
        )

    if replicated:
        branches = [branch_zero, branch_first] + [branch_second] * (tensor_count - 3)
        for step, branch in enumerate(branches[: tensor_count - 1]):
            _, part_first = attention_back(
                first_norm,
                qkv_parts[step][None],
                w_parts[step][None],
                branch,
                wide_cosine,
                wide_sine,
                q_width,
                k_width,
            )
            grad_first = grad_first + part_first
        grad_input = first_norm_back(
            grad_first, grad_branch.astype(F32), resid_in, first_scale
        )
    else:
        my_grad_input = first_norm_back(
            z_scatter(grad_first), my_grad_hidden, mine(resid_in), mine(first_scale)
        )
        grad_input = z_place(z_received(my_grad_input.astype(BF16))).astype(F32)

    return (
        mixed,
        grad_input,
        grad_norm1,
        grad_weights[:, :q_width],
        grad_weights[:, q_width : q_width + k_width],
        grad_weights[:, q_width + k_width :],
        grad_output,
        small[experts],
        small[:experts].T,
        grad_gate,
        up_weight_gradient,
        grad_down,
    )


def solution(mesh):
    placed = (
        P("expert", None),
        P(),
        P(None, "tensor"),
        P(None, "tensor"),
        P(None, "tensor"),
        P("tensor", None),
        P(),
        P(),
        P("expert", None, "tensor"),
        P("expert", None, "tensor"),
        P("expert", "tensor", None),
        P("expert", None),
        P("expert", None),
    )
    return jax.shard_map(
        local,
        mesh=mesh,
        in_specs=placed,
        out_specs=(
            P("expert", "tensor"),
            P("expert", None),
            P(),
            P(None, "tensor"),
            P(None, "tensor"),
            P(None, "tensor"),
            P("tensor", None),
            P(),
            P(),
            P("expert", None, "tensor"),
            P("expert", None, "tensor"),
            P("expert", "tensor", None),
        ),
        check_vma=False,
    )
```

```python
import functools
import math

import jax
import jax.numpy as jnp
from jax import lax
from jax.experimental import pallas as pl
from jax.experimental.pallas import tpu as pltpu
from jax.sharding import PartitionSpec as P

HEAD_DIMENSION = 64
SEQ_LEN = 512

EPS = 1e-06
SCALE = 0.125
NEGATIVE = -1e30
THETA = 10000.0
F32 = jnp.float32
BF16 = jnp.bfloat16
EXACT = lax.Precision.HIGHEST
LANES = 128
TILE = 256


def tables(tok_count):
    half = HEAD_DIMENSION // 2
    freq = jnp.exp(-math.log(THETA) * jnp.arange(half, dtype=F32) / half)
    places = (jnp.arange(tok_count) % SEQ_LEN).astype(F32)
    angle = places[:, None] * freq[None, :]
    return (jnp.cos(angle)[:, None, :], jnp.sin(angle)[:, None, :])


def rotate(field, cosine, sine_table, factor):
    half = HEAD_DIMENSION // 2
    first = field[..., :half]
    second = field[..., half:]
    return jnp.concatenate(
        [
            first * cosine - factor * second * sine_table,
            second * cosine + factor * first * sine_table,
        ],
        axis=-1,
    )


def causal_mask():
    places = jnp.arange(SEQ_LEN)
    return places[:, None] >= places[None, :]


def attend_forward(query_rows, rotated_keys, value_rows):
    scores = (
        jnp.einsum("lkgd,mkd->kglm", query_rows, rotated_keys, preferred_element_type=F32) * SCALE
    )
    scores = jnp.where(causal_mask(), scores, NEGATIVE)
    highest = jnp.max(scores, axis=-1, keepdims=True)
    expanded = jnp.exp(scores - highest)
    summed = jnp.sum(expanded, axis=-1, keepdims=True)
    probability = (expanded / summed).astype(BF16)
    heads_out = jnp.einsum("kglm,mkd->lkgd", probability, value_rows, preferred_element_type=F32)
    return (heads_out.astype(BF16), (highest + jnp.log(summed))[..., 0])


def attend_backward(query_rows, rotated_keys, value_rows, grad_heads, log_total):
    scores = (
        jnp.einsum("lkgd,mkd->kglm", query_rows, rotated_keys, preferred_element_type=F32) * SCALE
    )
    probability = jnp.where(causal_mask(), jnp.exp(scores - log_total[..., None]), 0.0)
    prob_low = probability.astype(BF16)
    grad_values = jnp.einsum("kglm,lkgd->mkd", prob_low, grad_heads, preferred_element_type=F32)
    grad_prob = jnp.einsum("lkgd,mkd->kglm", grad_heads, value_rows, preferred_element_type=F32)
    row_delta = jnp.sum(probability * grad_prob, axis=-1, keepdims=True)
    grad_scores = (probability * (grad_prob - row_delta)).astype(BF16)
    grad_queries = (
        jnp.einsum("kglm,mkd->lkgd", grad_scores, rotated_keys, preferred_element_type=F32) * SCALE
    )
    grad_keys = (
        jnp.einsum("kglm,lkgd->mkd", grad_scores, query_rows, preferred_element_type=F32) * SCALE
    )
    return (grad_queries, grad_keys, grad_values)


def mm(left, right):
    return jnp.dot(left, right, preferred_element_type=F32)


def mm_rows(left, right):
    return lax.dot_general(left, right, (((0,), (0,)), ((), ())), preferred_element_type=F32)


def mm_cols(left, right):
    return lax.dot_general(left, right, (((1,), (1,)), ((), ())), preferred_element_type=F32)


def piece(array, index, size, axis=0):
    return lax.dynamic_slice_in_dim(array, index * size, size, axis)


def swap(array, mask):
    size = lax.axis_size("expert")
    return lax.ppermute(array, "expert", [(i, i ^ mask) for i in range(size)])


def z_shift(array, step):
    size = lax.axis_size("tensor")
    return lax.ppermute(array, "tensor", [(i, (i + step) % size) for i in range(size)])


def z_received(array):
    return [array] + [z_shift(array, step) for step in range(1, lax.axis_size("tensor"))]


def z_place(parts):
    size, mine = lax.axis_size("tensor"), lax.axis_index("tensor")
    rows = parts[0].shape[0]
    whole = jnp.zeros((rows * size,) + parts[0].shape[1:], parts[0].dtype)
    for step, part in enumerate(parts):
        whole = lax.dynamic_update_slice_in_dim(whole, part, (mine + size - step) % size * rows, 0)
    return whole


def z_scatter(array, axis=0):
    size, mine = lax.axis_size("tensor"), lax.axis_index("tensor")
    width = array.shape[axis] // size
    total = piece(array, mine, width, axis).astype(F32)
    for step in range(1, size):
        sent = piece(array, (mine + step) % size, width, axis).astype(BF16)
        total = total + z_shift(sent, step).astype(F32)
    return total


def same_core_groups():
    size = lax.axis_size("expert")
    return [list(range(0, size, 2)), list(range(1, size, 2))]


def plane_gather(array):
    if lax.axis_size("expert") != 8:
        return [
            lax.all_gather(
                array, "expert", axis=0, tiled=True, axis_index_groups=same_core_groups()
            )
        ]
    half = array.shape[0] // 2
    from_x = swap(array, 2)
    from_y = swap(array, 4)
    return [array, from_x, from_y, swap(from_x[:half], 4), swap(from_y[half:], 2)]


def plane_scatter_far(blocks):
    return [swap(blocks[3], 2), swap(blocks[4], 4)] if len(blocks) == 5 else []


def plane_scatter(blocks, far=()):
    if lax.axis_size("expert") != 8:
        return lax.psum_scatter(
            blocks[0].astype(BF16),
            "expert",
            scatter_dimension=0,
            tiled=True,
            axis_index_groups=same_core_groups(),
        ).astype(F32), ()
    own, for_x, for_y, far_x, far_y = blocks
    half = own.shape[0] // 2
    via_x, via_y = far if far else plane_scatter_far(blocks)
    via_x, via_y = via_x.astype(F32), via_y.astype(F32)
    for_y = for_y.at[:half].set((for_y[:half].astype(F32) + via_x).astype(BF16))
    for_x = for_x.at[half:].set((for_x[half:].astype(F32) + via_y).astype(BF16))
    total = own.astype(F32) + swap(for_x, 2).astype(F32) + swap(for_y, 4).astype(F32)
    return total, (for_x, for_y)


def expert_sum(array, late, first=(), second=()):
    if lax.axis_size("expert") != 8:
        array, late = lax.psum((array.astype(BF16), late.astype(BF16)), "expert")
        return array.astype(F32), late.astype(F32), first, second
    place = lax.axis_index("expert")
    core, chip = place % 2, place // 2
    half = array.shape[0] // 2
    rows = half // 4
    array = array.astype(BF16)
    mine = piece(array, core, half).astype(F32)
    mine = mine + swap(piece(array, 1 - core, half), 1).astype(F32)
    mine, late, first = tied(mine, late, first)
    total = piece(mine, chip, rows)
    for mask in (1, 2, 3):
        total = total + swap(piece(mine, chip ^ mask, rows).astype(BF16), 2 * mask).astype(F32)
    total, second = tied(total.astype(BF16), second)
    late_rows = late.shape[0]
    total = jnp.concatenate([total, late.astype(BF16)])
    gathered = jnp.zeros((half + late_rows,) + array.shape[1:], BF16)
    late = 0.0
    for mask in (0, 1, 2, 3):
        part = swap(total, 2 * mask) if mask else total
        late = late + part[rows:].astype(F32)
        gathered = lax.dynamic_update_slice_in_dim(gathered, part[:rows], (chip ^ mask) * rows, 0)
    gathered = lax.dynamic_update_slice_in_dim(gathered, late.astype(BF16), half, 0)
    other = swap(gathered, 1)
    late = late + other[half:].astype(F32)
    both = jnp.concatenate([gathered[:half], gathered[:half]])
    both = lax.dynamic_update_slice_in_dim(both, other[:half], (1 - core) * half, 0)
    return both.astype(F32), late, first, second


def expert_kernel(
    experts,
    top_count,
    units,
    names_ref,
    normed_ref,
    grad_ref,
    router_ref,
    gate_ref,
    up_ref,
    down_ref,
    other_gate_ref,
    other_up_ref,
    other_down_ref,
    out_ref,
    rows_ref,
    gate_grad_ref,
    up_grad_ref,
    inner_ref,
):
    tile, model_width = normed_ref.shape
    here = gate_ref.shape[0]
    width = 2 * here * units

    def joined(own_ref, other_ref, chosen_units, axis):
        parts = [own_ref[e] if e < here else other_ref[e - here] for e in chosen_units]
        return jnp.concatenate(parts, axis=axis) if len(parts) > 1 else parts[0]

    normed = normed_ref[...]
    grad = grad_ref[:, :model_width]
    chosen_names = grad_ref[:, model_width:].astype(F32)
    lane = lax.broadcasted_iota(jnp.int32, (tile, LANES), 1)
    lane_float = lane.astype(F32)
    chosen = lane_float == chosen_names[:, 0:1]
    for k in range(1, top_count):
        chosen = chosen | (lane_float == chosen_names[:, k : k + 1])
    logits = jnp.where(chosen, mm(normed, router_ref[...]), NEGATIVE)
    expanded = jnp.exp(logits - jnp.max(logits, axis=-1, keepdims=True))
    expanded = jnp.where(chosen, expanded, 0.0)
    routing = expanded / jnp.sum(expanded, axis=-1, keepdims=True)
    grad_routing = jnp.zeros((tile, LANES), F32)
    columns = min(TILE, width)
    for start in range(0, width, columns):
        part = slice(start, start + columns)
        held = range(start // units, (start + columns) // units)
        gate_act = mm(normed, joined(gate_ref, other_gate_ref, held, 1))
        up_act = mm(normed, joined(up_ref, other_up_ref, held, 1))
        grad_plain = mm_cols(grad, joined(down_ref, other_down_ref, held, 0))
        weights = []
        for e in range(start // units, (start + columns) // units):
            weight = jnp.sum(
                jnp.where(lane == names_ref[e], routing, 0.0), axis=-1, keepdims=True
            )
            weights.append(jnp.broadcast_to(weight, (tile, units)))
        wide = jnp.concatenate(weights, axis=1) if len(weights) > 1 else weights[0]
        sigmoid_gate = jax.nn.sigmoid(gate_act)
        swish = gate_act * sigmoid_gate
        inner = swish * up_act
        inner_grad = inner * grad_plain
        for i, e in enumerate(range(start // units, (start + columns) // units)):
            total = jnp.sum(inner_grad[:, i * units : (i + 1) * units], axis=-1, keepdims=True)
            grad_routing = jnp.where(lane == names_ref[e], total, grad_routing)
        grad_inner = grad_plain * wide
        inner_ref[:, part] = (inner * wide).astype(BF16)
        up_grad_ref[:, part] = (grad_inner * swish).astype(BF16)
        gate_grad_ref[:, part] = (
            grad_inner * up_act * (sigmoid_gate + swish * (1.0 - sigmoid_gate))
        ).astype(BF16)
    rounded = grad_routing.astype(BF16).astype(F32)
    left = pltpu.roll(grad_routing - rounded, experts, 1)
    rows_ref[:, model_width:] = (rounded + left).astype(BF16)
    held = range(2 * here)
    rows_ref[:, :model_width] = (
        mm_cols(gate_grad_ref[...], joined(gate_ref, other_gate_ref, held, 1))
        + mm_cols(up_grad_ref[...], joined(up_ref, other_up_ref, held, 1))
    ).astype(BF16)
    out_ref[...] = mm(inner_ref[...], joined(down_ref, other_down_ref, held, 0)).astype(BF16)


def expert_block(names, normed, grad, router, weights, experts, top_count):
    rows, model_width = normed.shape
    units = weights[0].shape[2]
    width = 2 * weights[0].shape[0] * units
    tile = min(TILE, rows)

    def tiled(columns):
        return pl.BlockSpec((tile, columns), lambda i, names: (i, 0))

    def fixed(array):
        return pl.BlockSpec(array.shape, lambda i, names: (0,) * array.ndim)

    def shaped(columns):
        return jax.ShapeDtypeStruct((rows, columns), BF16)

    return pl.pallas_call(
        functools.partial(expert_kernel, experts, top_count, units),
        grid_spec=pltpu.PrefetchScalarGridSpec(
            num_scalar_prefetch=1,
            grid=(rows // tile,),
            in_specs=[
                tiled(model_width),
                tiled(model_width + LANES),
                fixed(router),
            ]
            + [fixed(weight) for weight in weights],
            out_specs=[
                tiled(model_width),
                tiled(model_width + LANES),
                tiled(width),
                tiled(width),
                tiled(width),
            ],
        ),
        out_shape=[
            shaped(model_width),
            shaped(model_width + LANES),
            shaped(width),
            shaped(width),
            shaped(width),
        ],
        compiler_params=pltpu.CompilerParams(vmem_limit_bytes=28 * 1024 * 1024),
        cost_estimate=pl.CostEstimate(
            flops=12 * rows * model_width * width,
            bytes_accessed=6 * model_width * width + 14 * rows * model_width,
            transcendentals=rows * width,
        ),
        name="experts",
    )(names, normed, grad, router, *weights)


def half_turn(field, cosine, sine):
    width = field.shape[1]
    half = HEAD_DIMENSION // 2
    lane = lax.broadcasted_iota(jnp.int32, field.shape, 1)
    partner = jnp.where(
        lane % HEAD_DIMENSION < half,
        pltpu.roll(field, width - half, 1),
        pltpu.roll(field, half, 1),
    )
    repeats = width // cosine.shape[1]
    cosine = jnp.concatenate([cosine] * repeats, axis=1)
    sine = jnp.concatenate([sine] * repeats, axis=1)
    return field * cosine + partner * sine


def forward_kernel(
    tokens_ref, gain_ref, query_ref, key_ref, value_ref, cosine_ref, sine_ref, normed_ref, out_ref
):
    size = HEAD_DIMENSION
    tokens = tokens_ref[...].astype(F32)
    normed = (tokens * norm_scale(tokens) * gain_ref[...]).astype(BF16)
    normed_ref[...] = normed
    cosine, sine = cosine_ref[...], sine_ref[...]
    queries = half_turn(mm(normed, query_ref[...]), cosine, sine).astype(BF16)
    keys = half_turn(mm(normed, key_ref[...]), cosine, sine).astype(BF16)
    values = mm(normed, value_ref[...]).astype(BF16)
    group = queries.shape[1] // keys.shape[1]
    tile = tokens.shape[0] // 2
    for t in range(2):
        heads = []
        seen = (t + 1) * tile
        for h in range(queries.shape[1] // size):
            g = h // group
            query = queries[t * tile : seen, h * size : (h + 1) * size]
            scores = mm_cols(query, keys[:seen, g * size : (g + 1) * size]) * SCALE
            place = lax.broadcasted_iota(jnp.int32, scores.shape, 0) + t * tile
            other = lax.broadcasted_iota(jnp.int32, scores.shape, 1)
            scores = jnp.where(place >= other, scores, NEGATIVE)
            expanded = jnp.exp(scores - jnp.max(scores, axis=-1, keepdims=True))
            probability = expanded * (1.0 / jnp.sum(expanded, axis=-1, keepdims=True))
            heads.append(mm(probability.astype(BF16), values[:seen, g * size : (g + 1) * size]))
        out_ref[t * tile : seen, :] = jnp.concatenate(heads, axis=1).astype(BF16)


def attention_forward(tokens, gain, query_w, key_w, value_w, cosine, sine):
    rows, model_width = tokens.shape
    return pl.pallas_call(
        forward_kernel,
        out_shape=[
            jax.ShapeDtypeStruct((rows, model_width), BF16),
            jax.ShapeDtypeStruct((rows, query_w.shape[1]), BF16),
        ],
        compiler_params=pltpu.CompilerParams(vmem_limit_bytes=20 * 1024 * 1024),
        cost_estimate=pl.CostEstimate(
            flops=4 * rows * model_width * query_w.shape[1],
            bytes_accessed=4 * rows * model_width,
            transcendentals=rows * rows * 4,
        ),
        name="forward",
    )(tokens, gain[None], query_w, key_w, value_w, cosine, sine)


def attention_kernel(
    q_width,
    k_width,
    normed_ref,
    weight_ref,
    output_ref,
    grad_ref,
    cosine_ref,
    sine_ref,
    raw_ref,
    first_ref,
):
    size = HEAD_DIMENSION
    rows = normed_ref.shape[0]
    turned = q_width + k_width
    group = q_width // k_width
    weight = weight_ref[0]
    cosine, sine = cosine_ref[...], sine_ref[...]
    projected = mm(normed_ref[...], weight)
    rotated = half_turn(projected[:, :turned], cosine, sine).astype(BF16)
    values = projected[:, turned:].astype(BF16)
    grad_heads = mm_cols(grad_ref[...], output_ref[0]).astype(BF16)
    tile = rows // 2
    grad_queries, grad_keys, grad_values = [], [], []
    for g in range(k_width // size):
        key = rotated[:, q_width + g * size : q_width + (g + 1) * size]
        value = values[:, g * size : (g + 1) * size]
        key_parts, value_parts = [0.0, 0.0], [0.0, 0.0]
        for h in range(g * group, (g + 1) * group):
            query = rotated[:, h * size : (h + 1) * size]
            grad_head = grad_heads[:, h * size : (h + 1) * size]
            query_parts = []
            for t in range(2):
                here = slice(t * tile, (t + 1) * tile)
                seen = (t + 1) * tile
                scores = mm_cols(query[here], key[:seen]) * SCALE
                place = lax.broadcasted_iota(jnp.int32, scores.shape, 0) + t * tile
                other = lax.broadcasted_iota(jnp.int32, scores.shape, 1)
                scores = jnp.where(place >= other, scores, NEGATIVE)
                expanded = jnp.exp(scores - jnp.max(scores, axis=-1, keepdims=True))
                probability = expanded * (1.0 / jnp.sum(expanded, axis=-1, keepdims=True))
                grad_prob = mm_cols(grad_head[here], value[:seen])
                delta = jnp.sum(probability * grad_prob, axis=-1, keepdims=True)
                grad_scores = (probability * (grad_prob - delta)).astype(BF16)
                query_parts.append(mm(grad_scores, key[:seen]) * SCALE)
                from_keys = mm_rows(grad_scores, query[here])
                from_values = mm_rows(probability.astype(BF16), grad_head[here])
                for u in range(t + 1):
                    block = slice(u * tile, (u + 1) * tile)
                    key_parts[u] = key_parts[u] + from_keys[block]
                    value_parts[u] = value_parts[u] + from_values[block]
            grad_queries.append(jnp.concatenate(query_parts, axis=0))
        grad_keys.append(jnp.concatenate(key_parts, axis=0) * SCALE)
        grad_values.append(jnp.concatenate(value_parts, axis=0))
    grad_turned = jnp.concatenate(grad_queries + grad_keys, axis=1)
    raw_ref[0, :, :turned] = half_turn(grad_turned, cosine, -sine).astype(BF16)
    raw_ref[0, :, turned:] = jnp.concatenate(grad_values, axis=1).astype(BF16)
    total = mm_cols(raw_ref[0], weight)

    @pl.when(pl.program_id(0) == 0)
    def _():
        first_ref[...] = total

    @pl.when(pl.program_id(0) > 0)
    def _():
        first_ref[...] += total


def attention_back(normed, weights, outputs, grad, cosine, sine, q_width, k_width):
    parts, model_width, width = weights.shape
    rows = normed.shape[0]

    def fixed(array):
        return pl.BlockSpec(array.shape, lambda i: (0, 0))

    def stacked(array):
        return pl.BlockSpec((1,) + array.shape[1:], lambda i: (i, 0, 0))

    raw = jax.ShapeDtypeStruct((parts, rows, width), BF16)
    return pl.pallas_call(
        functools.partial(attention_kernel, q_width, k_width),
        grid=(parts,),
        in_specs=[
            fixed(normed),
            stacked(weights),
            stacked(outputs),
            fixed(grad),
            fixed(cosine),
            fixed(sine),
        ],
        out_specs=[stacked(raw), pl.BlockSpec((rows, model_width), lambda i: (0, 0))],
        out_shape=[raw, jax.ShapeDtypeStruct((rows, model_width), F32)],
        compiler_params=pltpu.CompilerParams(vmem_limit_bytes=24 * 1024 * 1024),
        cost_estimate=pl.CostEstimate(
            flops=parts * 6 * rows * model_width * width,
            bytes_accessed=parts * 2 * model_width * width + 8 * rows * model_width,
            transcendentals=parts * rows * rows * 4,
        ),
        name="attention",
    )(normed, weights, outputs, grad, cosine, sine)


def tied(*arrays):
    return lax.optimization_barrier(arrays)


def norm_scale(field):
    return lax.rsqrt(jnp.mean(field * field, axis=-1, keepdims=True) + EPS)


def route(normed, router, chosen):
    logits = mm(normed, router)
    masked = jnp.where(chosen, logits, NEGATIVE)
    highest = jnp.max(masked, axis=-1, keepdims=True)
    expanded = jnp.where(chosen, jnp.exp(masked - highest), 0.0)
    return expanded / jnp.sum(expanded, axis=-1, keepdims=True)


def local(
    tokens,
    norm1_gain,
    w_query,
    key_projection_weight,
    value_projection_weight,
    w_output,
    norm2_gain,
    w_router,
    expert_gate_weight,
    expert_up_weight,
    expert_down_weight,
    expert_ids,
    cotangent,
):
    tok_count = tokens.shape[0]
    model_width = tokens.shape[1]
    experts, top_count = w_router.shape[1], expert_ids.shape[1]
    here, units = expert_gate_weight.shape[0], expert_gate_weight.shape[2]
    heads_query = w_query.shape[1] // HEAD_DIMENSION
    heads_kv = key_projection_weight.shape[1] // HEAD_DIMENSION
    group_size = heads_query // heads_kv
    cosine, sine_table = tables(tok_count)
    expert_count = lax.axis_size("expert")
    tensor_count = lax.axis_size("tensor")
    expert_place = lax.axis_index("expert")
    tensor_place = lax.axis_index("tensor")
    core = expert_place % 2
    own_rows = tok_count // tensor_count
    col_width = model_width // tensor_count

    names_wide = jnp.pad(expert_ids.astype(BF16), ((0, 0), (0, LANES - top_count)))
    grad_blocks = plane_gather(jnp.concatenate([cotangent, names_wide], axis=1))
    if expert_count == 8:
        grad_blocks, grad_far = grad_blocks[:3], grad_blocks[3:]

    half = w_output.shape[0] // 2
    w_halves = [z_shift(piece(w_output, core, half), step) for step in range(1, tensor_count)]
    expert_weights = [expert_gate_weight, expert_up_weight, expert_down_weight]
    w_halves = jnp.stack(w_halves)
    w_others = swap(w_halves, 1)
    w_parts = jnp.where(
        core == 0,
        jnp.concatenate([w_halves, w_others], axis=1),
        jnp.concatenate([w_others, w_halves], axis=1),
    )

    q_width, k_width = w_query.shape[1], key_projection_weight.shape[1]
    replicated = expert_count == 8 and k_width % LANES == 0
    resid_in = tokens.astype(F32)
    first_scale = norm_scale(resid_in)
    if replicated:
        wide_cosine = jnp.concatenate([cosine[:, 0]] * (LANES // 32), axis=1)
        signed = jnp.concatenate([-sine_table[:, 0], sine_table[:, 0]], axis=1)
        wide_sine = jnp.concatenate([signed] * (LANES // HEAD_DIMENSION), axis=1)
        first_norm, attended = attention_forward(
            tokens,
            norm1_gain,
            w_query,
            key_projection_weight,
            value_projection_weight,
            wide_cosine,
            wide_sine,
        )
    else:
        first_norm = (resid_in * first_scale * norm1_gain).astype(BF16)
        query_raw = mm(first_norm, w_query).reshape(tok_count, heads_query, HEAD_DIMENSION)
        key_raw = mm(first_norm, key_projection_weight).reshape(tok_count, heads_kv, HEAD_DIMENSION)
        query_rows = (
            rotate(query_raw, cosine, sine_table, 1.0)
            .astype(BF16)
            .reshape(tok_count, heads_kv, group_size, HEAD_DIMENSION)
        )
        rotated_keys = rotate(key_raw, cosine, sine_table, 1.0).astype(BF16)
        value_rows = (
            mm(first_norm, value_projection_weight)
            .astype(BF16)
            .reshape(tok_count, heads_kv, HEAD_DIMENSION)
        )
        attended, log_total = attend_forward(query_rows, rotated_keys, value_rows)
        attended = attended.reshape(tok_count, heads_query * HEAD_DIMENSION)

    attended_parts = z_received(attended)

    if expert_count == 8:
        attended_parts, grad_far = tied(attended_parts, grad_far)
    tokens, attended_parts, expert_weights, w_parts, w_router, qkv_weights = tied(
        tokens,
        attended_parts,
        expert_weights,
        w_parts,
        w_router,
        (w_query, key_projection_weight, value_projection_weight),
    )
    other_weights = [swap(weight, 1) for weight in expert_weights]
    resid_in = tokens.astype(F32)
    first_scale = norm_scale(resid_in)
    attended = attended_parts[0]

    hidden = resid_in + mm(attended, w_output)
    for step in range(1, tensor_count):
        hidden = hidden + mm(attended_parts[step], w_parts[step - 1])
    second_scale = norm_scale(hidden)
    second_norm = (hidden * second_scale * norm2_gain).astype(BF16)

    local_names = jnp.concatenate(
        [
            expert_place * here + jnp.arange(here, dtype=jnp.int32),
            (expert_place ^ 1) * here + jnp.arange(here, dtype=jnp.int32),
        ]
    )
    router_wide = jnp.pad(w_router, ((0, 0), (0, LANES - experts)))
    if expert_count == 8:
        grad_blocks = grad_blocks + grad_far

    def through_experts(normed, grad):
        return expert_block(
            local_names,
            normed,
            grad,
            router_wide,
            expert_weights + other_weights,
            experts,
            top_count,
        )

    if replicated:
        own_weight = jnp.concatenate(qkv_weights, axis=1)
        qkv_half = piece(own_weight, core, model_width // 2)
        other_weights, qkv_half = tied(other_weights, qkv_half)
        qkv_halves = [z_shift(qkv_half, step) for step in range(1, tensor_count)]
    if expert_count == 8:
        half = tok_count // 2
        from_x, from_y = swap(second_norm, 2), swap(second_norm, 4)
        own_done = through_experts(second_norm, grad_blocks[0])
        from_x, from_y, own_done = tied(from_x, from_y, own_done)
        normed_blocks = [
            second_norm, from_x, from_y, swap(from_x[:half], 4), swap(from_y[half:], 2)
        ]
        if replicated:
            own_done, qkv_halves = tied(own_done, qkv_halves)
            qkv_halves = jnp.stack(qkv_halves)
            qkv_others = swap(qkv_halves, 1)
            qkv_parts = jnp.where(
                core == 0,
                jnp.concatenate([qkv_halves, qkv_others], axis=1),
                jnp.concatenate([qkv_others, qkv_halves], axis=1),
            )
        done = [own_done]
    else:
        normed_blocks = plane_gather(second_norm)
        done = []
    if expert_count == 8:
        done.append(through_experts(normed_blocks[1], grad_blocks[1]))
        far_done = [through_experts(normed_blocks[i], grad_blocks[i]) for i in (3, 4)]
        normed_blocks[2], far_done = tied(normed_blocks[2], far_done)
        done.append(through_experts(normed_blocks[2], grad_blocks[2]))
        done += far_done
    else:
        done = [through_experts(normed, grad) for normed, grad in zip(normed_blocks, grad_blocks)]
    plane_rows, merged = plane_scatter([block[1] for block in done])
    plane_rows, *out_blocks = tied(plane_rows, *[block[0] for block in done])
    gate_grads, merged = tied([block[2] for block in done], merged)
    up_grads, plane_rows = tied([block[3] for block in done], plane_rows)
    inners = [block[4] for block in done]
    row_sum = z_scatter(plane_rows)
    out_far = plane_scatter_far(out_blocks)
    row_sum, out_far, inners = tied(row_sum, out_far, inners)
    gate_total = up_total = down_total = 0.0
    for normed, grad, gate_grad, up_grad, inner in zip(
        normed_blocks, grad_blocks, gate_grads, up_grads, inners
    ):
        gate_total = gate_total + mm_rows(normed, gate_grad)
        up_total = up_total + mm_rows(normed, up_grad)
        down_total = down_total + mm_rows(inner, grad[:, :model_width])
    plane_out, _ = plane_scatter(out_blocks, out_far)

    my_routing_grad = (
        row_sum[:, model_width : model_width + experts]
        + row_sum[:, model_width + experts : model_width + 2 * experts]
    )
    row_sum = row_sum[:, :model_width]

    def mine(array):
        return piece(array, tensor_place, own_rows)

    my_hidden, my_scale = mine(hidden), mine(second_scale)
    my_normed = mine(second_norm)
    names = jnp.arange(experts, dtype=jnp.int32)
    my_chosen = jnp.any(mine(expert_ids)[:, :, None] == names[None, None, :], axis=1)
    my_routing = route(my_normed, w_router, my_chosen)
    my_normed = my_normed.astype(F32)
    my_logits = my_routing * (
        my_routing_grad - jnp.sum(my_routing * my_routing_grad, axis=-1, keepdims=True)
    )
    router_float = w_router.astype(F32)
    grad_second = row_sum + jnp.dot(my_logits, router_float.T, precision=EXACT)
    grad_router = lax.dot_general(
        my_logits, my_normed, (((0,), (0,)), ((), ())), precision=EXACT
    )
    grad_norm2 = jnp.sum(grad_second * my_hidden * my_scale, axis=0)
    gained_two = grad_second * norm2_gain
    my_grad_hidden = (
        mine(cotangent).astype(F32)
        + my_scale * gained_two
        - my_hidden * my_scale**3 * jnp.mean(gained_two * my_hidden, axis=-1, keepdims=True)
    )
    small = jnp.concatenate([grad_router, grad_norm2[None]])
    extra = -small.shape[0] % 16
    small = jnp.pad(small, ((0, extra), (0, 0))).astype(BF16)
    parts = z_received(jnp.concatenate([my_grad_hidden.astype(BF16), small]))
    plane_out, down_total, *parts = tied(plane_out, down_total, *parts)
    routed = piece(hidden, tensor_place, col_width, 1) + piece(
        plane_out, tensor_place, col_width, 1
    )
    out_pieces = [
        piece(plane_out, (tensor_place + step) % tensor_count, col_width, 1).astype(BF16)
        for step in range(1, tensor_count)
    ]
    grad_branch = z_place([part[:own_rows] for part in parts])
    small = sum(part[own_rows:].astype(F32) for part in parts)
    grad_output = mm_rows(attended, grad_branch)

    if replicated:
        grad_raw, grad_first = attention_back(
            first_norm,
            own_weight[None],
            w_output[None],
            grad_branch,
            wide_cosine,
            wide_sine,
            q_width,
            k_width,
        )
        grad_raw = grad_raw[0]
        norm1_part = jnp.sum(grad_first * resid_in * first_scale, axis=0)[None]
    else:
        grad_heads = mm_cols(grad_branch, w_output).astype(BF16)
        grad_heads = grad_heads.reshape(tok_count, heads_kv, group_size, HEAD_DIMENSION)
        grad_queries, grad_keys, grad_values = attend_backward(
            query_rows, rotated_keys, value_rows, grad_heads, log_total
        )
        grad_query_raw = rotate(
            grad_queries.reshape(tok_count, heads_query, HEAD_DIMENSION), cosine, sine_table, -1.0
        )
        grad_query_raw = grad_query_raw.reshape(tok_count, -1).astype(BF16)
        grad_key_raw = rotate(grad_keys, cosine, sine_table, -1.0)
        grad_key_raw = grad_key_raw.reshape(tok_count, -1).astype(BF16)
        grad_value_raw = grad_values.reshape(tok_count, -1).astype(BF16)
        grad_raw = jnp.concatenate([grad_query_raw, grad_key_raw, grad_value_raw], axis=1)
        grad_first = (
            mm_cols(grad_query_raw, w_query)
            + mm_cols(grad_key_raw, key_projection_weight)
            + mm_cols(grad_value_raw, value_projection_weight)
        )
        norm1_part = jnp.sum(grad_first * resid_in * first_scale, axis=0)[None]

    grad_raw = mm_rows(first_norm, grad_raw)
    raw_width = grad_raw.shape[1]

    def folded(array):
        array = jnp.pad(array.astype(BF16), ((0, -array.shape[0] % 16), (0, 0)))
        return [array[:, i : i + raw_width] for i in range(0, model_width, raw_width)]

    pile = [grad_raw.astype(BF16)] + folded(grad_output) + folded(small)
    norm1_part = jnp.pad(norm1_part.reshape(-1, raw_width), ((0, 16 - model_width // raw_width), (0, 0)))
    norm1_part = sum(z_received(norm1_part))
    places = [0]
    for part in pile:
        places.append(places[-1] + part.shape[0])
    extra = -places[-1] % 128
    pile = jnp.concatenate(pile + [jnp.zeros((extra, raw_width), BF16)])
    pile, branch_zero = tied(pile, grad_branch)
    pile, late, (branch_first, out_first), (branch_second, out_second, down_total) = expert_sum(
        pile,
        norm1_part,
        (grad_branch, out_pieces[:2]),
        (grad_branch, out_pieces[2:], down_total),
    )
    for step, sent in enumerate(out_first + out_second):
        routed = routed + z_shift(sent, step + 1).astype(F32)
    mixed = routed.astype(BF16)

    width = here * units

    def from_chip(total):
        return total[:, :width] + swap(total[:, width:].astype(BF16), 1).astype(F32)

    def as_experts(total):
        return total.reshape(model_width, here, units).transpose(1, 0, 2)

    grad_gate = as_experts(from_chip(gate_total))
    up_weight_gradient = as_experts(from_chip(up_total))
    grad_down = down_total[:width] + swap(down_total[width:].astype(BF16), 1).astype(F32)
    grad_down = grad_down.reshape(here, units, model_width)
    grad_weights = pile[: places[1]]
    folds = model_width // raw_width

    def unfolded(first, rows):
        return jnp.concatenate(
            [pile[places[i] : places[i] + rows] for i in range(first, first + folds)], axis=1
        )

    grad_output = unfolded(1, grad_output.shape[0])
    small = unfolded(1 + folds, experts + 1)
    grad_norm1 = late[:folds].reshape(-1)

    def first_norm_back(grad_first, grad_hidden, resid, scale):
        gained = grad_first * norm1_gain
        return (
            grad_hidden
            + scale * gained
            - resid * scale**3 * jnp.mean(gained * resid, axis=-1, keepdims=True)
        )

    if replicated:
        branches = [branch_zero, branch_first] + [branch_second] * (tensor_count - 3)
        for step, branch in enumerate(branches[: tensor_count - 1]):
            _, part_first = attention_back(
                first_norm,
                qkv_parts[step][None],
                w_parts[step][None],
                branch,
                wide_cosine,
                wide_sine,
                q_width,
                k_width,
            )
            grad_first = grad_first + part_first
        grad_input = first_norm_back(
            grad_first, grad_branch.astype(F32), resid_in, first_scale
        )
    else:
        my_grad_input = first_norm_back(
            z_scatter(grad_first), my_grad_hidden, mine(resid_in), mine(first_scale)
        )
        grad_input = z_place(z_received(my_grad_input.astype(BF16))).astype(F32)

    return (
        mixed,
        grad_input,
        grad_norm1,
        grad_weights[:, :q_width],
        grad_weights[:, q_width : q_width + k_width],
        grad_weights[:, q_width + k_width :],
        grad_output,
        small[experts],
        small[:experts].T,
        grad_gate,
        up_weight_gradient,
        grad_down,
    )


def solution(mesh):
    placed = (
        P("expert", None),
        P(),
        P(None, "tensor"),
        P(None, "tensor"),
        P(None, "tensor"),
        P("tensor", None),
        P(),
        P(),
        P("expert", None, "tensor"),
        P("expert", None, "tensor"),
        P("expert", "tensor", None),
        P("expert", None),
        P("expert", None),
    )
    return jax.shard_map(
        local,
        mesh=mesh,
        in_specs=placed,
        out_specs=(
            P("expert", "tensor"),
            P("expert", None),
            P(),
            P(None, "tensor"),
            P(None, "tensor"),
            P(None, "tensor"),
            P("tensor", None),
            P(),
            P(),
            P("expert", None, "tensor"),
            P("expert", None, "tensor"),
            P("expert", "tensor", None),
        ),
        check_vma=False,
    )
```

```python
import functools
import math

import jax
import jax.numpy as jnp
from jax import lax
from jax.experimental import pallas as pl
from jax.experimental.pallas import tpu as pltpu
from jax.sharding import PartitionSpec as P

HEAD_DIMENSION = 64
SEQ_LEN = 512

EPS = 1e-06
SCALE = 0.125
NEGATIVE = -1e30
THETA = 10000.0
F32 = jnp.float32
BF16 = jnp.bfloat16
EXACT = lax.Precision.HIGHEST
LANES = 128
TILE = 256


def tables(tok_count):
    half = HEAD_DIMENSION // 2
    freq = jnp.exp(-math.log(THETA) * jnp.arange(half, dtype=F32) / half)
    places = (jnp.arange(tok_count) % SEQ_LEN).astype(F32)
    angle = places[:, None] * freq[None, :]
    return (jnp.cos(angle)[:, None, :], jnp.sin(angle)[:, None, :])


def rotate(field, cosine, sine_table, factor):
    half = HEAD_DIMENSION // 2
    first = field[..., :half]
    second = field[..., half:]
    return jnp.concatenate(
        [
            first * cosine - factor * second * sine_table,
            second * cosine + factor * first * sine_table,
        ],
        axis=-1,
    )


def causal_mask():
    places = jnp.arange(SEQ_LEN)
    return places[:, None] >= places[None, :]


def attend_forward(query_rows, rotated_keys, value_rows):
    scores = (
        jnp.einsum("lkgd,mkd->kglm", query_rows, rotated_keys, preferred_element_type=F32) * SCALE
    )
    scores = jnp.where(causal_mask(), scores, NEGATIVE)
    highest = jnp.max(scores, axis=-1, keepdims=True)
    expanded = jnp.exp(scores - highest)
    summed = jnp.sum(expanded, axis=-1, keepdims=True)
    probability = (expanded / summed).astype(BF16)
    heads_out = jnp.einsum("kglm,mkd->lkgd", probability, value_rows, preferred_element_type=F32)
    return (heads_out.astype(BF16), (highest + jnp.log(summed))[..., 0])


def attend_backward(query_rows, rotated_keys, value_rows, grad_heads, log_total):
    scores = (
        jnp.einsum("lkgd,mkd->kglm", query_rows, rotated_keys, preferred_element_type=F32) * SCALE
    )
    probability = jnp.where(causal_mask(), jnp.exp(scores - log_total[..., None]), 0.0)
    prob_low = probability.astype(BF16)
    grad_values = jnp.einsum("kglm,lkgd->mkd", prob_low, grad_heads, preferred_element_type=F32)
    grad_prob = jnp.einsum("lkgd,mkd->kglm", grad_heads, value_rows, preferred_element_type=F32)
    row_delta = jnp.sum(probability * grad_prob, axis=-1, keepdims=True)
    grad_scores = (probability * (grad_prob - row_delta)).astype(BF16)
    grad_queries = (
        jnp.einsum("kglm,mkd->lkgd", grad_scores, rotated_keys, preferred_element_type=F32) * SCALE
    )
    grad_keys = (
        jnp.einsum("kglm,lkgd->mkd", grad_scores, query_rows, preferred_element_type=F32) * SCALE
    )
    return (grad_queries, grad_keys, grad_values)


def mm(left, right):
    return jnp.dot(left, right, preferred_element_type=F32)


def mm_rows(left, right):
    return lax.dot_general(left, right, (((0,), (0,)), ((), ())), preferred_element_type=F32)


def mm_cols(left, right):
    return lax.dot_general(left, right, (((1,), (1,)), ((), ())), preferred_element_type=F32)


def piece(array, index, size, axis=0):
    return lax.dynamic_slice_in_dim(array, index * size, size, axis)


def swap(array, mask):
    size = lax.axis_size("expert")
    return lax.ppermute(array, "expert", [(i, i ^ mask) for i in range(size)])


def z_shift(array, step):
    size = lax.axis_size("tensor")
    return lax.ppermute(array, "tensor", [(i, (i + step) % size) for i in range(size)])


def z_received(array):
    return [array] + [z_shift(array, step) for step in range(1, lax.axis_size("tensor"))]


def z_place(parts):
    size, mine = lax.axis_size("tensor"), lax.axis_index("tensor")
    rows = parts[0].shape[0]
    whole = jnp.zeros((rows * size,) + parts[0].shape[1:], parts[0].dtype)
    for step, part in enumerate(parts):
        whole = lax.dynamic_update_slice_in_dim(whole, part, (mine + size - step) % size * rows, 0)
    return whole


def z_scatter(array, axis=0):
    size, mine = lax.axis_size("tensor"), lax.axis_index("tensor")
    width = array.shape[axis] // size
    total = piece(array, mine, width, axis).astype(F32)
    for step in range(1, size):
        sent = piece(array, (mine + step) % size, width, axis).astype(BF16)
        total = total + z_shift(sent, step).astype(F32)
    return total


def same_core_groups():
    size = lax.axis_size("expert")
    return [list(range(0, size, 2)), list(range(1, size, 2))]


def plane_gather(array):
    if lax.axis_size("expert") != 8:
        return [
            lax.all_gather(
                array, "expert", axis=0, tiled=True, axis_index_groups=same_core_groups()
            )
        ]
    half = array.shape[0] // 2
    from_x = swap(array, 2)
    from_y = swap(array, 4)
    return [array, from_x, from_y, swap(from_x[:half], 4), swap(from_y[half:], 2)]


def plane_scatter_far(blocks):
    return [swap(blocks[3], 2), swap(blocks[4], 4)] if len(blocks) == 5 else []


def plane_scatter(blocks, far=()):
    if lax.axis_size("expert") != 8:
        return lax.psum_scatter(
            blocks[0].astype(BF16),
            "expert",
            scatter_dimension=0,
            tiled=True,
            axis_index_groups=same_core_groups(),
        ).astype(F32)
    own, for_x, for_y, far_x, far_y = blocks
    half = own.shape[0] // 2
    via_x, via_y = far if far else plane_scatter_far(blocks)
    via_x, via_y = via_x.astype(F32), via_y.astype(F32)
    for_y = for_y.at[:half].set((for_y[:half].astype(F32) + via_x).astype(BF16))
    for_x = for_x.at[half:].set((for_x[half:].astype(F32) + via_y).astype(BF16))
    return own.astype(F32) + swap(for_x, 2).astype(F32) + swap(for_y, 4).astype(F32)


def expert_sum(array, late, first=(), second=()):
    if lax.axis_size("expert") != 8:
        array, late = lax.psum((array.astype(BF16), late.astype(BF16)), "expert")
        return array.astype(F32), late.astype(F32), first, second
    place = lax.axis_index("expert")
    core, chip = place % 2, place // 2
    half = array.shape[0] // 2
    rows = half // 4
    array = array.astype(BF16)
    mine = piece(array, core, half).astype(F32)
    mine = mine + swap(piece(array, 1 - core, half), 1).astype(F32)
    mine, first = tied(mine, first)
    total = piece(mine, chip, rows)
    for mask in (1, 2, 3):
        total = total + swap(piece(mine, chip ^ mask, rows).astype(BF16), 2 * mask).astype(F32)
    total, second = tied(total.astype(BF16), second)
    late_rows = late.shape[0]
    total = jnp.concatenate([total, late.astype(BF16)])
    gathered = jnp.zeros((half + late_rows,) + array.shape[1:], BF16)
    late = 0.0
    for mask in (0, 1, 2, 3):
        part = swap(total, 2 * mask) if mask else total
        late = late + part[rows:].astype(F32)
        gathered = lax.dynamic_update_slice_in_dim(gathered, part[:rows], (chip ^ mask) * rows, 0)
    gathered = lax.dynamic_update_slice_in_dim(gathered, late.astype(BF16), half, 0)
    other = swap(gathered, 1)
    late = late + other[half:].astype(F32)
    both = jnp.concatenate([gathered[:half], gathered[:half]])
    both = lax.dynamic_update_slice_in_dim(both, other[:half], (1 - core) * half, 0)
    return both.astype(F32), late, first, second


def expert_kernel(
    experts,
    top_count,
    units,
    names_ref,
    normed_ref,
    grad_ref,
    router_ref,
    gate_ref,
    up_ref,
    down_ref,
    other_gate_ref,
    other_up_ref,
    other_down_ref,
    out_ref,
    rows_ref,
    gate_grad_ref,
    up_grad_ref,
    inner_ref,
):
    tile, model_width = normed_ref.shape
    here = gate_ref.shape[0]
    width = 2 * here * units

    def joined(own_ref, other_ref, chosen_units, axis):
        parts = [own_ref[e] if e < here else other_ref[e - here] for e in chosen_units]
        return jnp.concatenate(parts, axis=axis) if len(parts) > 1 else parts[0]

    normed = normed_ref[...]
    grad = grad_ref[:, :model_width]
    chosen_names = grad_ref[:, model_width:].astype(F32)
    lane = lax.broadcasted_iota(jnp.int32, (tile, LANES), 1)
    lane_float = lane.astype(F32)
    chosen = lane_float == chosen_names[:, 0:1]
    for k in range(1, top_count):
        chosen = chosen | (lane_float == chosen_names[:, k : k + 1])
    logits = jnp.where(chosen, mm(normed, router_ref[...]), NEGATIVE)
    expanded = jnp.exp(logits - jnp.max(logits, axis=-1, keepdims=True))
    expanded = jnp.where(chosen, expanded, 0.0)
    routing = expanded / jnp.sum(expanded, axis=-1, keepdims=True)
    grad_routing = jnp.zeros((tile, LANES), F32)
    columns = min(TILE, width)
    for start in range(0, width, columns):
        part = slice(start, start + columns)
        held = range(start // units, (start + columns) // units)
        gate_act = mm(normed, joined(gate_ref, other_gate_ref, held, 1))
        up_act = mm(normed, joined(up_ref, other_up_ref, held, 1))
        grad_plain = mm_cols(grad, joined(down_ref, other_down_ref, held, 0))
        weights = []
        for e in range(start // units, (start + columns) // units):
            weight = jnp.sum(
                jnp.where(lane == names_ref[e], routing, 0.0), axis=-1, keepdims=True
            )
            weights.append(jnp.broadcast_to(weight, (tile, units)))
        wide = jnp.concatenate(weights, axis=1) if len(weights) > 1 else weights[0]
        sigmoid_gate = jax.nn.sigmoid(gate_act)
        swish = gate_act * sigmoid_gate
        inner = swish * up_act
        inner_grad = inner * grad_plain
        for i, e in enumerate(range(start // units, (start + columns) // units)):
            total = jnp.sum(inner_grad[:, i * units : (i + 1) * units], axis=-1, keepdims=True)
            grad_routing = jnp.where(lane == names_ref[e], total, grad_routing)
        grad_inner = grad_plain * wide
        inner_ref[:, part] = (inner * wide).astype(BF16)
        up_grad_ref[:, part] = (grad_inner * swish).astype(BF16)
        gate_grad_ref[:, part] = (
            grad_inner * up_act * (sigmoid_gate + swish * (1.0 - sigmoid_gate))
        ).astype(BF16)
    rounded = grad_routing.astype(BF16).astype(F32)
    left = pltpu.roll(grad_routing - rounded, experts, 1)
    rows_ref[:, model_width:] = (rounded + left).astype(BF16)
    held = range(2 * here)
    rows_ref[:, :model_width] = (
        mm_cols(gate_grad_ref[...], joined(gate_ref, other_gate_ref, held, 1))
        + mm_cols(up_grad_ref[...], joined(up_ref, other_up_ref, held, 1))
    ).astype(BF16)
    out_ref[...] = mm(inner_ref[...], joined(down_ref, other_down_ref, held, 0)).astype(BF16)


def expert_block(names, normed, grad, router, weights, experts, top_count):
    rows, model_width = normed.shape
    units = weights[0].shape[2]
    width = 2 * weights[0].shape[0] * units
    tile = min(TILE, rows)

    def tiled(columns):
        return pl.BlockSpec((tile, columns), lambda i, names: (i, 0))

    def fixed(array):
        return pl.BlockSpec(array.shape, lambda i, names: (0,) * array.ndim)

    def shaped(columns):
        return jax.ShapeDtypeStruct((rows, columns), BF16)

    return pl.pallas_call(
        functools.partial(expert_kernel, experts, top_count, units),
        grid_spec=pltpu.PrefetchScalarGridSpec(
            num_scalar_prefetch=1,
            grid=(rows // tile,),
            in_specs=[
                tiled(model_width),
                tiled(model_width + LANES),
                fixed(router),
            ]
            + [fixed(weight) for weight in weights],
            out_specs=[
                tiled(model_width),
                tiled(model_width + LANES),
                tiled(width),
                tiled(width),
                tiled(width),
            ],
        ),
        out_shape=[
            shaped(model_width),
            shaped(model_width + LANES),
            shaped(width),
            shaped(width),
            shaped(width),
        ],
        compiler_params=pltpu.CompilerParams(vmem_limit_bytes=28 * 1024 * 1024),
        cost_estimate=pl.CostEstimate(
            flops=12 * rows * model_width * width,
            bytes_accessed=6 * model_width * width + 14 * rows * model_width,
            transcendentals=rows * width,
        ),
        name="experts",
    )(names, normed, grad, router, *weights)


def half_turn(field, cosine, sine):
    width = field.shape[1]
    half = HEAD_DIMENSION // 2
    lane = lax.broadcasted_iota(jnp.int32, field.shape, 1)
    partner = jnp.where(
        lane % HEAD_DIMENSION < half,
        pltpu.roll(field, width - half, 1),
        pltpu.roll(field, half, 1),
    )
    repeats = width // cosine.shape[1]
    cosine = jnp.concatenate([cosine] * repeats, axis=1)
    sine = jnp.concatenate([sine] * repeats, axis=1)
    return field * cosine + partner * sine


def forward_kernel(
    tokens_ref, gain_ref, query_ref, key_ref, value_ref, cosine_ref, sine_ref, normed_ref, out_ref
):
    size = HEAD_DIMENSION
    tokens = tokens_ref[...].astype(F32)
    normed = (tokens * norm_scale(tokens) * gain_ref[...]).astype(BF16)
    normed_ref[...] = normed
    cosine, sine = cosine_ref[...], sine_ref[...]
    queries = half_turn(mm(normed, query_ref[...]), cosine, sine).astype(BF16)
    keys = half_turn(mm(normed, key_ref[...]), cosine, sine).astype(BF16)
    values = mm(normed, value_ref[...]).astype(BF16)
    group = queries.shape[1] // keys.shape[1]
    tile = tokens.shape[0] // 2
    for t in range(2):
        heads = []
        seen = (t + 1) * tile
        for h in range(queries.shape[1] // size):
            g = h // group
            query = queries[t * tile : seen, h * size : (h + 1) * size]
            scores = mm_cols(query, keys[:seen, g * size : (g + 1) * size]) * SCALE
            place = lax.broadcasted_iota(jnp.int32, scores.shape, 0) + t * tile
            other = lax.broadcasted_iota(jnp.int32, scores.shape, 1)
            scores = jnp.where(place >= other, scores, NEGATIVE)
            expanded = jnp.exp(scores - jnp.max(scores, axis=-1, keepdims=True))
            probability = expanded * (1.0 / jnp.sum(expanded, axis=-1, keepdims=True))
            heads.append(mm(probability.astype(BF16), values[:seen, g * size : (g + 1) * size]))
        out_ref[t * tile : seen, :] = jnp.concatenate(heads, axis=1).astype(BF16)


def attention_forward(tokens, gain, query_w, key_w, value_w, cosine, sine):
    rows, model_width = tokens.shape
    return pl.pallas_call(
        forward_kernel,
        out_shape=[
            jax.ShapeDtypeStruct((rows, model_width), BF16),
            jax.ShapeDtypeStruct((rows, query_w.shape[1]), BF16),
        ],
        compiler_params=pltpu.CompilerParams(vmem_limit_bytes=20 * 1024 * 1024),
        cost_estimate=pl.CostEstimate(
            flops=4 * rows * model_width * query_w.shape[1],
            bytes_accessed=4 * rows * model_width,
            transcendentals=rows * rows * 4,
        ),
        name="forward",
    )(tokens, gain[None], query_w, key_w, value_w, cosine, sine)


def attention_kernel(
    q_width,
    k_width,
    normed_ref,
    weight_ref,
    output_ref,
    grad_ref,
    cosine_ref,
    sine_ref,
    raw_ref,
    first_ref,
):
    size = HEAD_DIMENSION
    rows = normed_ref.shape[0]
    turned = q_width + k_width
    group = q_width // k_width
    weight = weight_ref[0]
    cosine, sine = cosine_ref[...], sine_ref[...]
    projected = mm(normed_ref[...], weight)
    rotated = half_turn(projected[:, :turned], cosine, sine).astype(BF16)
    values = projected[:, turned:].astype(BF16)
    grad_heads = mm_cols(grad_ref[...], output_ref[0]).astype(BF16)
    tile = rows // 2
    grad_queries, grad_keys, grad_values = [], [], []
    for g in range(k_width // size):
        key = rotated[:, q_width + g * size : q_width + (g + 1) * size]
        value = values[:, g * size : (g + 1) * size]
        key_parts, value_parts = [0.0, 0.0], [0.0, 0.0]
        for h in range(g * group, (g + 1) * group):
            query = rotated[:, h * size : (h + 1) * size]
            grad_head = grad_heads[:, h * size : (h + 1) * size]
            query_parts = []
            for t in range(2):
                here = slice(t * tile, (t + 1) * tile)
                seen = (t + 1) * tile
                scores = mm_cols(query[here], key[:seen]) * SCALE
                place = lax.broadcasted_iota(jnp.int32, scores.shape, 0) + t * tile
                other = lax.broadcasted_iota(jnp.int32, scores.shape, 1)
                scores = jnp.where(place >= other, scores, NEGATIVE)
                expanded = jnp.exp(scores - jnp.max(scores, axis=-1, keepdims=True))
                probability = expanded * (1.0 / jnp.sum(expanded, axis=-1, keepdims=True))
                grad_prob = mm_cols(grad_head[here], value[:seen])
                delta = jnp.sum(probability * grad_prob, axis=-1, keepdims=True)
                grad_scores = (probability * (grad_prob - delta)).astype(BF16)
                query_parts.append(mm(grad_scores, key[:seen]) * SCALE)
                from_keys = mm_rows(grad_scores, query[here])
                from_values = mm_rows(probability.astype(BF16), grad_head[here])
                for u in range(t + 1):
                    block = slice(u * tile, (u + 1) * tile)
                    key_parts[u] = key_parts[u] + from_keys[block]
                    value_parts[u] = value_parts[u] + from_values[block]
            grad_queries.append(jnp.concatenate(query_parts, axis=0))
        grad_keys.append(jnp.concatenate(key_parts, axis=0) * SCALE)
        grad_values.append(jnp.concatenate(value_parts, axis=0))
    grad_turned = jnp.concatenate(grad_queries + grad_keys, axis=1)
    raw_ref[0, :, :turned] = half_turn(grad_turned, cosine, -sine).astype(BF16)
    raw_ref[0, :, turned:] = jnp.concatenate(grad_values, axis=1).astype(BF16)
    total = mm_cols(raw_ref[0], weight)

    @pl.when(pl.program_id(0) == 0)
    def _():
        first_ref[...] = total

    @pl.when(pl.program_id(0) > 0)
    def _():
        first_ref[...] += total


def attention_back(normed, weights, outputs, grad, cosine, sine, q_width, k_width):
    parts, model_width, width = weights.shape
    rows = normed.shape[0]

    def fixed(array):
        return pl.BlockSpec(array.shape, lambda i: (0, 0))

    def stacked(array):
        return pl.BlockSpec((1,) + array.shape[1:], lambda i: (i, 0, 0))

    raw = jax.ShapeDtypeStruct((parts, rows, width), BF16)
    return pl.pallas_call(
        functools.partial(attention_kernel, q_width, k_width),
        grid=(parts,),
        in_specs=[
            fixed(normed),
            stacked(weights),
            stacked(outputs),
            fixed(grad),
            fixed(cosine),
            fixed(sine),
        ],
        out_specs=[stacked(raw), pl.BlockSpec((rows, model_width), lambda i: (0, 0))],
        out_shape=[raw, jax.ShapeDtypeStruct((rows, model_width), F32)],
        compiler_params=pltpu.CompilerParams(vmem_limit_bytes=24 * 1024 * 1024),
        cost_estimate=pl.CostEstimate(
            flops=parts * 6 * rows * model_width * width,
            bytes_accessed=parts * 2 * model_width * width + 8 * rows * model_width,
            transcendentals=parts * rows * rows * 4,
        ),
        name="attention",
    )(normed, weights, outputs, grad, cosine, sine)


def tied(*arrays):
    return lax.optimization_barrier(arrays)


def norm_scale(field):
    return lax.rsqrt(jnp.mean(field * field, axis=-1, keepdims=True) + EPS)


def route(normed, router, chosen):
    logits = mm(normed, router)
    masked = jnp.where(chosen, logits, NEGATIVE)
    highest = jnp.max(masked, axis=-1, keepdims=True)
    expanded = jnp.where(chosen, jnp.exp(masked - highest), 0.0)
    return expanded / jnp.sum(expanded, axis=-1, keepdims=True)


def local(
    tokens,
    norm1_gain,
    w_query,
    key_projection_weight,
    value_projection_weight,
    w_output,
    norm2_gain,
    w_router,
    expert_gate_weight,
    expert_up_weight,
    expert_down_weight,
    expert_ids,
    cotangent,
):
    tok_count = tokens.shape[0]
    model_width = tokens.shape[1]
    experts, top_count = w_router.shape[1], expert_ids.shape[1]
    here, units = expert_gate_weight.shape[0], expert_gate_weight.shape[2]
    heads_query = w_query.shape[1] // HEAD_DIMENSION
    heads_kv = key_projection_weight.shape[1] // HEAD_DIMENSION
    group_size = heads_query // heads_kv
    cosine, sine_table = tables(tok_count)
    expert_count = lax.axis_size("expert")
    tensor_count = lax.axis_size("tensor")
    expert_place = lax.axis_index("expert")
    tensor_place = lax.axis_index("tensor")
    core = expert_place % 2
    own_rows = tok_count // tensor_count
    col_width = model_width // tensor_count

    names_wide = jnp.pad(expert_ids.astype(BF16), ((0, 0), (0, LANES - top_count)))
    grad_blocks = plane_gather(jnp.concatenate([cotangent, names_wide], axis=1))
    if expert_count == 8:
        grad_blocks, grad_far = grad_blocks[:3], grad_blocks[3:]

    half = w_output.shape[0] // 2
    w_halves = [z_shift(piece(w_output, core, half), step) for step in range(1, tensor_count)]
    expert_weights = [expert_gate_weight, expert_up_weight, expert_down_weight]
    w_halves = jnp.stack(w_halves)
    w_others = swap(w_halves, 1)
    w_parts = jnp.where(
        core == 0,
        jnp.concatenate([w_halves, w_others], axis=1),
        jnp.concatenate([w_others, w_halves], axis=1),
    )

    q_width, k_width = w_query.shape[1], key_projection_weight.shape[1]
    replicated = expert_count == 8 and k_width % LANES == 0
    resid_in = tokens.astype(F32)
    first_scale = norm_scale(resid_in)
    if replicated:
        wide_cosine = jnp.concatenate([cosine[:, 0]] * (LANES // 32), axis=1)
        signed = jnp.concatenate([-sine_table[:, 0], sine_table[:, 0]], axis=1)
        wide_sine = jnp.concatenate([signed] * (LANES // HEAD_DIMENSION), axis=1)
        first_norm, attended = attention_forward(
            tokens,
            norm1_gain,
            w_query,
            key_projection_weight,
            value_projection_weight,
            wide_cosine,
            wide_sine,
        )
    else:
        first_norm = (resid_in * first_scale * norm1_gain).astype(BF16)
        query_raw = mm(first_norm, w_query).reshape(tok_count, heads_query, HEAD_DIMENSION)
        key_raw = mm(first_norm, key_projection_weight).reshape(tok_count, heads_kv, HEAD_DIMENSION)
        query_rows = (
            rotate(query_raw, cosine, sine_table, 1.0)
            .astype(BF16)
            .reshape(tok_count, heads_kv, group_size, HEAD_DIMENSION)
        )
        rotated_keys = rotate(key_raw, cosine, sine_table, 1.0).astype(BF16)
        value_rows = (
            mm(first_norm, value_projection_weight)
            .astype(BF16)
            .reshape(tok_count, heads_kv, HEAD_DIMENSION)
        )
        attended, log_total = attend_forward(query_rows, rotated_keys, value_rows)
        attended = attended.reshape(tok_count, heads_query * HEAD_DIMENSION)

    attended_parts = z_received(attended)

    if expert_count == 8:
        attended_parts, grad_far = tied(attended_parts, grad_far)
    tokens, attended_parts, expert_weights, w_parts, w_router, qkv_weights = tied(
        tokens,
        attended_parts,
        expert_weights,
        w_parts,
        w_router,
        (w_query, key_projection_weight, value_projection_weight),
    )
    other_weights = [swap(weight, 1) for weight in expert_weights]
    resid_in = tokens.astype(F32)
    first_scale = norm_scale(resid_in)
    attended = attended_parts[0]

    hidden = resid_in + mm(attended, w_output)
    for step in range(1, tensor_count):
        hidden = hidden + mm(attended_parts[step], w_parts[step - 1])
    second_scale = norm_scale(hidden)
    second_norm = (hidden * second_scale * norm2_gain).astype(BF16)

    local_names = jnp.concatenate(
        [
            expert_place * here + jnp.arange(here, dtype=jnp.int32),
            (expert_place ^ 1) * here + jnp.arange(here, dtype=jnp.int32),
        ]
    )
    router_wide = jnp.pad(w_router, ((0, 0), (0, LANES - experts)))
    if expert_count == 8:
        grad_blocks = grad_blocks + grad_far

    def through_experts(normed, grad):
        return expert_block(
            local_names,
            normed,
            grad,
            router_wide,
            expert_weights + other_weights,
            experts,
            top_count,
        )

    if replicated:
        own_weight = jnp.concatenate(qkv_weights, axis=1)
        qkv_half = piece(own_weight, core, model_width // 2)
        other_weights, qkv_half = tied(other_weights, qkv_half)
        qkv_halves = [z_shift(qkv_half, step) for step in range(1, tensor_count)]
    if expert_count == 8:
        half = tok_count // 2
        from_x, from_y = swap(second_norm, 2), swap(second_norm, 4)
        own_done = through_experts(second_norm, grad_blocks[0])
        from_x, from_y, own_done = tied(from_x, from_y, own_done)
        normed_blocks = [
            second_norm, from_x, from_y, swap(from_x[:half], 4), swap(from_y[half:], 2)
        ]
        if replicated:
            own_done, qkv_halves = tied(own_done, qkv_halves)
            qkv_halves = jnp.stack(qkv_halves)
            qkv_others = swap(qkv_halves, 1)
            qkv_parts = jnp.where(
                core == 0,
                jnp.concatenate([qkv_halves, qkv_others], axis=1),
                jnp.concatenate([qkv_others, qkv_halves], axis=1),
            )
        done = [own_done]
    else:
        normed_blocks = plane_gather(second_norm)
        done = []
    if expert_count == 8:
        done.append(through_experts(normed_blocks[1], grad_blocks[1]))
        far_done = [through_experts(normed_blocks[i], grad_blocks[i]) for i in (3, 4)]
        normed_blocks[2], far_done = tied(normed_blocks[2], far_done)
        done.append(through_experts(normed_blocks[2], grad_blocks[2]))
        done += far_done
    else:
        done = [through_experts(normed, grad) for normed, grad in zip(normed_blocks, grad_blocks)]
    plane_rows = plane_scatter([block[1] for block in done])
    plane_rows, *out_blocks = tied(plane_rows, *[block[0] for block in done])
    gate_grads, up_grads, plane_rows = tied(
        [block[2] for block in done], [block[3] for block in done], plane_rows
    )
    inners = [block[4] for block in done]
    row_sum = z_scatter(plane_rows)
    out_far = plane_scatter_far(out_blocks)
    row_sum, out_far, inners = tied(row_sum, out_far, inners)
    gate_total = up_total = down_total = 0.0
    for normed, grad, gate_grad, up_grad, inner in zip(
        normed_blocks, grad_blocks, gate_grads, up_grads, inners
    ):
        gate_total = gate_total + mm_rows(normed, gate_grad)
        up_total = up_total + mm_rows(normed, up_grad)
        down_total = down_total + mm_rows(inner, grad[:, :model_width])
    plane_out = plane_scatter(out_blocks, out_far)

    my_routing_grad = (
        row_sum[:, model_width : model_width + experts]
        + row_sum[:, model_width + experts : model_width + 2 * experts]
    )
    row_sum = row_sum[:, :model_width]

    def mine(array):
        return piece(array, tensor_place, own_rows)

    my_hidden, my_scale = mine(hidden), mine(second_scale)
    my_normed = mine(second_norm)
    names = jnp.arange(experts, dtype=jnp.int32)
    my_chosen = jnp.any(mine(expert_ids)[:, :, None] == names[None, None, :], axis=1)
    my_routing = route(my_normed, w_router, my_chosen)
    my_normed = my_normed.astype(F32)
    my_logits = my_routing * (
        my_routing_grad - jnp.sum(my_routing * my_routing_grad, axis=-1, keepdims=True)
    )
    router_float = w_router.astype(F32)
    grad_second = row_sum + jnp.dot(my_logits, router_float.T, precision=EXACT)
    grad_router = lax.dot_general(
        my_logits, my_normed, (((0,), (0,)), ((), ())), precision=EXACT
    )
    grad_norm2 = jnp.sum(grad_second * my_hidden * my_scale, axis=0)
    gained_two = grad_second * norm2_gain
    my_grad_hidden = (
        mine(cotangent).astype(F32)
        + my_scale * gained_two
        - my_hidden * my_scale**3 * jnp.mean(gained_two * my_hidden, axis=-1, keepdims=True)
    )
    small = jnp.concatenate([grad_router, grad_norm2[None]])
    extra = -small.shape[0] % 16
    small = jnp.pad(small, ((0, extra), (0, 0))).astype(BF16)
    parts = z_received(jnp.concatenate([my_grad_hidden.astype(BF16), small]))
    plane_out, down_total, *parts = tied(plane_out, down_total, *parts)
    routed = piece(hidden, tensor_place, col_width, 1) + piece(
        plane_out, tensor_place, col_width, 1
    )
    out_pieces = [
        piece(plane_out, (tensor_place + step) % tensor_count, col_width, 1).astype(BF16)
        for step in range(1, tensor_count)
    ]
    grad_branch = z_place([part[:own_rows] for part in parts])
    small = sum(part[own_rows:].astype(F32) for part in parts)
    grad_output = mm_rows(attended, grad_branch)

    if replicated:
        grad_raw, grad_first = attention_back(
            first_norm,
            own_weight[None],
            w_output[None],
            grad_branch,
            wide_cosine,
            wide_sine,
            q_width,
            k_width,
        )
        grad_raw = grad_raw[0]
        norm1_part = jnp.sum(grad_first * resid_in * first_scale, axis=0)[None]
    else:
        grad_heads = mm_cols(grad_branch, w_output).astype(BF16)
        grad_heads = grad_heads.reshape(tok_count, heads_kv, group_size, HEAD_DIMENSION)
        grad_queries, grad_keys, grad_values = attend_backward(
            query_rows, rotated_keys, value_rows, grad_heads, log_total
        )
        grad_query_raw = rotate(
            grad_queries.reshape(tok_count, heads_query, HEAD_DIMENSION), cosine, sine_table, -1.0
        )
        grad_query_raw = grad_query_raw.reshape(tok_count, -1).astype(BF16)
        grad_key_raw = rotate(grad_keys, cosine, sine_table, -1.0)
        grad_key_raw = grad_key_raw.reshape(tok_count, -1).astype(BF16)
        grad_value_raw = grad_values.reshape(tok_count, -1).astype(BF16)
        grad_raw = jnp.concatenate([grad_query_raw, grad_key_raw, grad_value_raw], axis=1)
        grad_first = (
            mm_cols(grad_query_raw, w_query)
            + mm_cols(grad_key_raw, key_projection_weight)
            + mm_cols(grad_value_raw, value_projection_weight)
        )
        norm1_part = jnp.sum(grad_first * resid_in * first_scale, axis=0)[None]

    grad_raw = mm_rows(first_norm, grad_raw)
    raw_width = grad_raw.shape[1]

    def folded(array):
        array = jnp.pad(array.astype(BF16), ((0, -array.shape[0] % 16), (0, 0)))
        return [array[:, i : i + raw_width] for i in range(0, model_width, raw_width)]

    pile = [grad_raw.astype(BF16)] + folded(grad_output) + folded(small)
    norm1_part = jnp.pad(norm1_part.reshape(-1, raw_width), ((0, 16 - model_width // raw_width), (0, 0)))
    norm1_part = sum(z_received(norm1_part))
    places = [0]
    for part in pile:
        places.append(places[-1] + part.shape[0])
    extra = -places[-1] % 128
    pile = jnp.concatenate(pile + [jnp.zeros((extra, raw_width), BF16)])
    pile, branch_zero = tied(pile, grad_branch)
    out_received = [z_shift(out_pieces[0], 1)]
    pile, late, (branch_first, out_first, up_total), (branch_second, out_second, down_total) = (
        expert_sum(
            pile,
            norm1_part,
            (grad_branch, out_pieces[1:2], up_total),
            (grad_branch, out_pieces[2:], down_total),
        )
    )
    branch_first, norm1_part = tied(branch_first, norm1_part)
    out_received += [z_shift(sent, step + 2) for step, sent in enumerate(out_first + out_second)]
    for part in out_received:
        routed = routed + part.astype(F32)
    mixed = routed.astype(BF16)

    width = here * units

    def from_chip(total):
        return total[:, :width] + swap(total[:, width:].astype(BF16), 1).astype(F32)

    def as_experts(total):
        return total.reshape(model_width, here, units).transpose(1, 0, 2)

    grad_gate = as_experts(from_chip(gate_total))
    up_weight_gradient = as_experts(from_chip(up_total))
    grad_down = down_total[:width] + swap(down_total[width:].astype(BF16), 1).astype(F32)
    grad_down = grad_down.reshape(here, units, model_width)
    grad_weights = pile[: places[1]]
    folds = model_width // raw_width

    def unfolded(first, rows):
        return jnp.concatenate(
            [pile[places[i] : places[i] + rows] for i in range(first, first + folds)], axis=1
        )

    grad_output = unfolded(1, grad_output.shape[0])
    small = unfolded(1 + folds, experts + 1)
    grad_norm1 = late[:folds].reshape(-1)

    def first_norm_back(grad_first, grad_hidden, resid, scale):
        gained = grad_first * norm1_gain
        return (
            grad_hidden
            + scale * gained
            - resid * scale**3 * jnp.mean(gained * resid, axis=-1, keepdims=True)
        )

    if replicated:
        branches = [branch_zero, branch_first] + [branch_second] * (tensor_count - 3)
        for step, branch in enumerate(branches[: tensor_count - 1]):
            _, part_first = attention_back(
                first_norm,
                qkv_parts[step][None],
                w_parts[step][None],
                branch,
                wide_cosine,
                wide_sine,
                q_width,
                k_width,
            )
            grad_first = grad_first + part_first
        grad_input = first_norm_back(
            grad_first, grad_branch.astype(F32), resid_in, first_scale
        )
    else:
        my_grad_input = first_norm_back(
            z_scatter(grad_first), my_grad_hidden, mine(resid_in), mine(first_scale)
        )
        grad_input = z_place(z_received(my_grad_input.astype(BF16))).astype(F32)

    return (
        mixed,
        grad_input,
        grad_norm1,
        grad_weights[:, :q_width],
        grad_weights[:, q_width : q_width + k_width],
        grad_weights[:, q_width + k_width :],
        grad_output,
        small[experts],
        small[:experts].T,
        grad_gate,
        up_weight_gradient,
        grad_down,
    )


def solution(mesh):
    placed = (
        P("expert", None),
        P(),
        P(None, "tensor"),
        P(None, "tensor"),
        P(None, "tensor"),
        P("tensor", None),
        P(),
        P(),
        P("expert", None, "tensor"),
        P("expert", None, "tensor"),
        P("expert", "tensor", None),
        P("expert", None),
        P("expert", None),
    )
    return jax.shard_map(
        local,
        mesh=mesh,
        in_specs=placed,
        out_specs=(
            P("expert", "tensor"),
            P("expert", None),
            P(),
            P(None, "tensor"),
            P(None, "tensor"),
            P(None, "tensor"),
            P("tensor", None),
            P(),
            P(),
            P("expert", None, "tensor"),
            P("expert", None, "tensor"),
            P("expert", "tensor", None),
        ),
        check_vma=False,
    )
```

```python
import functools
import math

import jax
import jax.numpy as jnp
from jax import lax
from jax.experimental import pallas as pl
from jax.experimental.pallas import tpu as pltpu
from jax.sharding import PartitionSpec as P

HEAD_DIMENSION = 64
SEQ_LEN = 512

EPS = 1e-06
SCALE = 0.125
NEGATIVE = -1e30
THETA = 10000.0
F32 = jnp.float32
BF16 = jnp.bfloat16
EXACT = lax.Precision.HIGHEST
LANES = 128
TILE = 256


def tables(tok_count):
    half = HEAD_DIMENSION // 2
    freq = jnp.exp(-math.log(THETA) * jnp.arange(half, dtype=F32) / half)
    places = (jnp.arange(tok_count) % SEQ_LEN).astype(F32)
    angle = places[:, None] * freq[None, :]
    return (jnp.cos(angle)[:, None, :], jnp.sin(angle)[:, None, :])


def rotate(field, cosine, sine_table, factor):
    half = HEAD_DIMENSION // 2
    first = field[..., :half]
    second = field[..., half:]
    return jnp.concatenate(
        [
            first * cosine - factor * second * sine_table,
            second * cosine + factor * first * sine_table,
        ],
        axis=-1,
    )


def causal_mask():
    places = jnp.arange(SEQ_LEN)
    return places[:, None] >= places[None, :]


def attend_forward(query_rows, rotated_keys, value_rows):
    scores = (
        jnp.einsum("lkgd,mkd->kglm", query_rows, rotated_keys, preferred_element_type=F32) * SCALE
    )
    scores = jnp.where(causal_mask(), scores, NEGATIVE)
    highest = jnp.max(scores, axis=-1, keepdims=True)
    expanded = jnp.exp(scores - highest)
    summed = jnp.sum(expanded, axis=-1, keepdims=True)
    probability = (expanded / summed).astype(BF16)
    heads_out = jnp.einsum("kglm,mkd->lkgd", probability, value_rows, preferred_element_type=F32)
    return (heads_out.astype(BF16), (highest + jnp.log(summed))[..., 0])


def attend_backward(query_rows, rotated_keys, value_rows, grad_heads, log_total):
    scores = (
        jnp.einsum("lkgd,mkd->kglm", query_rows, rotated_keys, preferred_element_type=F32) * SCALE
    )
    probability = jnp.where(causal_mask(), jnp.exp(scores - log_total[..., None]), 0.0)
    prob_low = probability.astype(BF16)
    grad_values = jnp.einsum("kglm,lkgd->mkd", prob_low, grad_heads, preferred_element_type=F32)
    grad_prob = jnp.einsum("lkgd,mkd->kglm", grad_heads, value_rows, preferred_element_type=F32)
    row_delta = jnp.sum(probability * grad_prob, axis=-1, keepdims=True)
    grad_scores = (probability * (grad_prob - row_delta)).astype(BF16)
    grad_queries = (
        jnp.einsum("kglm,mkd->lkgd", grad_scores, rotated_keys, preferred_element_type=F32) * SCALE
    )
    grad_keys = (
        jnp.einsum("kglm,lkgd->mkd", grad_scores, query_rows, preferred_element_type=F32) * SCALE
    )
    return (grad_queries, grad_keys, grad_values)


def mm(left, right):
    return jnp.dot(left, right, preferred_element_type=F32)


def mm_rows(left, right):
    return lax.dot_general(left, right, (((0,), (0,)), ((), ())), preferred_element_type=F32)


def mm_cols(left, right):
    return lax.dot_general(left, right, (((1,), (1,)), ((), ())), preferred_element_type=F32)


def piece(array, index, size, axis=0):
    return lax.dynamic_slice_in_dim(array, index * size, size, axis)


def swap(array, mask):
    size = lax.axis_size("expert")
    return lax.ppermute(array, "expert", [(i, i ^ mask) for i in range(size)])


def z_shift(array, step):
    size = lax.axis_size("tensor")
    return lax.ppermute(array, "tensor", [(i, (i + step) % size) for i in range(size)])


def z_received(array):
    return [array] + [z_shift(array, step) for step in range(1, lax.axis_size("tensor"))]


def z_place(parts):
    size, mine = lax.axis_size("tensor"), lax.axis_index("tensor")
    rows = parts[0].shape[0]
    whole = jnp.zeros((rows * size,) + parts[0].shape[1:], parts[0].dtype)
    for step, part in enumerate(parts):
        whole = lax.dynamic_update_slice_in_dim(whole, part, (mine + size - step) % size * rows, 0)
    return whole


def z_scatter(array, axis=0):
    size, mine = lax.axis_size("tensor"), lax.axis_index("tensor")
    width = array.shape[axis] // size
    total = piece(array, mine, width, axis).astype(F32)
    for step in range(1, size):
        sent = piece(array, (mine + step) % size, width, axis).astype(BF16)
        total = total + z_shift(sent, step).astype(F32)
    return total


def same_core_groups():
    size = lax.axis_size("expert")
    return [list(range(0, size, 2)), list(range(1, size, 2))]


def plane_gather(array):
    if lax.axis_size("expert") != 8:
        return [
            lax.all_gather(
                array, "expert", axis=0, tiled=True, axis_index_groups=same_core_groups()
            )
        ]
    half = array.shape[0] // 2
    from_x = swap(array, 2)
    from_y = swap(array, 4)
    return [array, from_x, from_y, swap(from_x[:half], 4), swap(from_y[half:], 2)]


def plane_scatter_far(blocks):
    return [swap(blocks[3], 2), swap(blocks[4], 4)] if len(blocks) == 5 else []


def plane_scatter(blocks, far=()):
    if lax.axis_size("expert") != 8:
        return lax.psum_scatter(
            blocks[0].astype(BF16),
            "expert",
            scatter_dimension=0,
            tiled=True,
            axis_index_groups=same_core_groups(),
        ).astype(F32), ()
    own, for_x, for_y, far_x, far_y = blocks
    half = own.shape[0] // 2
    via_x, via_y = far if far else plane_scatter_far(blocks)
    via_x, via_y = via_x.astype(F32), via_y.astype(F32)
    for_y = for_y.at[:half].set((for_y[:half].astype(F32) + via_x).astype(BF16))
    for_x = for_x.at[half:].set((for_x[half:].astype(F32) + via_y).astype(BF16))
    total = own.astype(F32) + swap(for_x, 2).astype(F32) + swap(for_y, 4).astype(F32)
    return total, (for_x, for_y)


def expert_sum(array, late, first=(), second=()):
    if lax.axis_size("expert") != 8:
        array, late = lax.psum((array.astype(BF16), late.astype(BF16)), "expert")
        return array.astype(F32), late.astype(F32), first, second
    place = lax.axis_index("expert")
    core, chip = place % 2, place // 2
    half = array.shape[0] // 2
    rows = half // 4
    array = array.astype(BF16)
    mine = piece(array, core, half).astype(F32)
    mine = mine + swap(piece(array, 1 - core, half), 1).astype(F32)
    mine, first = tied(mine, first)
    total = piece(mine, chip, rows)
    for mask in (1, 2, 3):
        total = total + swap(piece(mine, chip ^ mask, rows).astype(BF16), 2 * mask).astype(F32)
    total, second = tied(total.astype(BF16), second)
    late_rows = late.shape[0]
    total = jnp.concatenate([total, late.astype(BF16)])
    gathered = jnp.zeros((half + late_rows,) + array.shape[1:], BF16)
    late = 0.0
    for mask in (0, 1, 2, 3):
        part = swap(total, 2 * mask) if mask else total
        late = late + part[rows:].astype(F32)
        gathered = lax.dynamic_update_slice_in_dim(gathered, part[:rows], (chip ^ mask) * rows, 0)
    gathered = lax.dynamic_update_slice_in_dim(gathered, late.astype(BF16), half, 0)
    other = swap(gathered, 1)
    late = late + other[half:].astype(F32)
    both = jnp.concatenate([gathered[:half], gathered[:half]])
    both = lax.dynamic_update_slice_in_dim(both, other[:half], (1 - core) * half, 0)
    return both.astype(F32), late, first, second


def expert_kernel(
    experts,
    top_count,
    units,
    names_ref,
    normed_ref,
    grad_ref,
    router_ref,
    gate_ref,
    up_ref,
    down_ref,
    other_gate_ref,
    other_up_ref,
    other_down_ref,
    out_ref,
    rows_ref,
    gate_grad_ref,
    up_grad_ref,
    inner_ref,
):
    tile, model_width = normed_ref.shape
    here = gate_ref.shape[0]
    width = 2 * here * units

    def joined(own_ref, other_ref, chosen_units, axis):
        parts = [own_ref[e] if e < here else other_ref[e - here] for e in chosen_units]
        return jnp.concatenate(parts, axis=axis) if len(parts) > 1 else parts[0]

    normed = normed_ref[...]
    grad = grad_ref[:, :model_width]
    chosen_names = grad_ref[:, model_width:].astype(F32)
    lane = lax.broadcasted_iota(jnp.int32, (tile, LANES), 1)
    lane_float = lane.astype(F32)
    chosen = lane_float == chosen_names[:, 0:1]
    for k in range(1, top_count):
        chosen = chosen | (lane_float == chosen_names[:, k : k + 1])
    logits = jnp.where(chosen, mm(normed, router_ref[...]), NEGATIVE)
    expanded = jnp.exp(logits - jnp.max(logits, axis=-1, keepdims=True))
    expanded = jnp.where(chosen, expanded, 0.0)
    routing = expanded / jnp.sum(expanded, axis=-1, keepdims=True)
    grad_routing = jnp.zeros((tile, LANES), F32)
    columns = min(TILE, width)
    for start in range(0, width, columns):
        part = slice(start, start + columns)
        held = range(start // units, (start + columns) // units)
        gate_act = mm(normed, joined(gate_ref, other_gate_ref, held, 1))
        up_act = mm(normed, joined(up_ref, other_up_ref, held, 1))
        grad_plain = mm_cols(grad, joined(down_ref, other_down_ref, held, 0))
        weights = []
        for e in range(start // units, (start + columns) // units):
            weight = jnp.sum(
                jnp.where(lane == names_ref[e], routing, 0.0), axis=-1, keepdims=True
            )
            weights.append(jnp.broadcast_to(weight, (tile, units)))
        wide = jnp.concatenate(weights, axis=1) if len(weights) > 1 else weights[0]
        sigmoid_gate = jax.nn.sigmoid(gate_act)
        swish = gate_act * sigmoid_gate
        inner = swish * up_act
        inner_grad = inner * grad_plain
        for i, e in enumerate(range(start // units, (start + columns) // units)):
            total = jnp.sum(inner_grad[:, i * units : (i + 1) * units], axis=-1, keepdims=True)
            grad_routing = jnp.where(lane == names_ref[e], total, grad_routing)
        grad_inner = grad_plain * wide
        inner_ref[:, part] = (inner * wide).astype(BF16)
        up_grad_ref[:, part] = (grad_inner * swish).astype(BF16)
        gate_grad_ref[:, part] = (
            grad_inner * up_act * (sigmoid_gate + swish * (1.0 - sigmoid_gate))
        ).astype(BF16)
    rounded = grad_routing.astype(BF16).astype(F32)
    left = pltpu.roll(grad_routing - rounded, experts, 1)
    rows_ref[:, model_width:] = (rounded + left).astype(BF16)
    held = range(2 * here)
    rows_ref[:, :model_width] = (
        mm_cols(gate_grad_ref[...], joined(gate_ref, other_gate_ref, held, 1))
        + mm_cols(up_grad_ref[...], joined(up_ref, other_up_ref, held, 1))
    ).astype(BF16)
    out_ref[...] = mm(inner_ref[...], joined(down_ref, other_down_ref, held, 0)).astype(BF16)


def expert_block(names, normed, grad, router, weights, experts, top_count):
    rows, model_width = normed.shape
    units = weights[0].shape[2]
    width = 2 * weights[0].shape[0] * units
    tile = min(TILE, rows)

    def tiled(columns):
        return pl.BlockSpec((tile, columns), lambda i, names: (i, 0))

    def fixed(array):
        return pl.BlockSpec(array.shape, lambda i, names: (0,) * array.ndim)

    def shaped(columns):
        return jax.ShapeDtypeStruct((rows, columns), BF16)

    return pl.pallas_call(
        functools.partial(expert_kernel, experts, top_count, units),
        grid_spec=pltpu.PrefetchScalarGridSpec(
            num_scalar_prefetch=1,
            grid=(rows // tile,),
            in_specs=[
                tiled(model_width),
                tiled(model_width + LANES),
                fixed(router),
            ]
            + [fixed(weight) for weight in weights],
            out_specs=[
                tiled(model_width),
                tiled(model_width + LANES),
                tiled(width),
                tiled(width),
                tiled(width),
            ],
        ),
        out_shape=[
            shaped(model_width),
            shaped(model_width + LANES),
            shaped(width),
            shaped(width),
            shaped(width),
        ],
        compiler_params=pltpu.CompilerParams(vmem_limit_bytes=28 * 1024 * 1024),
        cost_estimate=pl.CostEstimate(
            flops=12 * rows * model_width * width,
            bytes_accessed=6 * model_width * width + 14 * rows * model_width,
            transcendentals=rows * width,
        ),
        name="experts",
    )(names, normed, grad, router, *weights)


def half_turn(field, cosine, sine):
    width = field.shape[1]
    half = HEAD_DIMENSION // 2
    lane = lax.broadcasted_iota(jnp.int32, field.shape, 1)
    partner = jnp.where(
        lane % HEAD_DIMENSION < half,
        pltpu.roll(field, width - half, 1),
        pltpu.roll(field, half, 1),
    )
    repeats = width // cosine.shape[1]
    cosine = jnp.concatenate([cosine] * repeats, axis=1)
    sine = jnp.concatenate([sine] * repeats, axis=1)
    return field * cosine + partner * sine


def forward_kernel(
    tokens_ref, gain_ref, query_ref, key_ref, value_ref, cosine_ref, sine_ref, normed_ref, out_ref
):
    size = HEAD_DIMENSION
    tokens = tokens_ref[...].astype(F32)
    normed = (tokens * norm_scale(tokens) * gain_ref[...]).astype(BF16)
    normed_ref[...] = normed
    cosine, sine = cosine_ref[...], sine_ref[...]
    queries = half_turn(mm(normed, query_ref[...]), cosine, sine).astype(BF16)
    keys = half_turn(mm(normed, key_ref[...]), cosine, sine).astype(BF16)
    values = mm(normed, value_ref[...]).astype(BF16)
    group = queries.shape[1] // keys.shape[1]
    tile = tokens.shape[0] // 2
    for t in range(2):
        heads = []
        seen = (t + 1) * tile
        for h in range(queries.shape[1] // size):
            g = h // group
            query = queries[t * tile : seen, h * size : (h + 1) * size]
            scores = mm_cols(query, keys[:seen, g * size : (g + 1) * size]) * SCALE
            place = lax.broadcasted_iota(jnp.int32, scores.shape, 0) + t * tile
            other = lax.broadcasted_iota(jnp.int32, scores.shape, 1)
            scores = jnp.where(place >= other, scores, NEGATIVE)
            expanded = jnp.exp(scores - jnp.max(scores, axis=-1, keepdims=True))
            probability = expanded * (1.0 / jnp.sum(expanded, axis=-1, keepdims=True))
            heads.append(mm(probability.astype(BF16), values[:seen, g * size : (g + 1) * size]))
        out_ref[t * tile : seen, :] = jnp.concatenate(heads, axis=1).astype(BF16)


def attention_forward(tokens, gain, query_w, key_w, value_w, cosine, sine):
    rows, model_width = tokens.shape
    return pl.pallas_call(
        forward_kernel,
        out_shape=[
            jax.ShapeDtypeStruct((rows, model_width), BF16),
            jax.ShapeDtypeStruct((rows, query_w.shape[1]), BF16),
        ],
        compiler_params=pltpu.CompilerParams(vmem_limit_bytes=20 * 1024 * 1024),
        cost_estimate=pl.CostEstimate(
            flops=4 * rows * model_width * query_w.shape[1],
            bytes_accessed=4 * rows * model_width,
            transcendentals=rows * rows * 4,
        ),
        name="forward",
    )(tokens, gain[None], query_w, key_w, value_w, cosine, sine)


def attention_kernel(
    q_width,
    k_width,
    normed_ref,
    weight_ref,
    output_ref,
    grad_ref,
    cosine_ref,
    sine_ref,
    raw_ref,
    first_ref,
):
    size = HEAD_DIMENSION
    rows = normed_ref.shape[0]
    turned = q_width + k_width
    group = q_width // k_width
    weight = weight_ref[0]
    cosine, sine = cosine_ref[...], sine_ref[...]
    projected = mm(normed_ref[...], weight)
    rotated = half_turn(projected[:, :turned], cosine, sine).astype(BF16)
    values = projected[:, turned:].astype(BF16)
    grad_heads = mm_cols(grad_ref[...], output_ref[0]).astype(BF16)
    tile = rows // 2
    grad_queries, grad_keys, grad_values = [], [], []
    for g in range(k_width // size):
        key = rotated[:, q_width + g * size : q_width + (g + 1) * size]
        value = values[:, g * size : (g + 1) * size]
        key_parts, value_parts = [0.0, 0.0], [0.0, 0.0]
        for h in range(g * group, (g + 1) * group):
            query = rotated[:, h * size : (h + 1) * size]
            grad_head = grad_heads[:, h * size : (h + 1) * size]
            query_parts = []
            for t in range(2):
                here = slice(t * tile, (t + 1) * tile)
                seen = (t + 1) * tile
                scores = mm_cols(query[here], key[:seen]) * SCALE
                place = lax.broadcasted_iota(jnp.int32, scores.shape, 0) + t * tile
                other = lax.broadcasted_iota(jnp.int32, scores.shape, 1)
                scores = jnp.where(place >= other, scores, NEGATIVE)
                expanded = jnp.exp(scores - jnp.max(scores, axis=-1, keepdims=True))
                probability = expanded * (1.0 / jnp.sum(expanded, axis=-1, keepdims=True))
                grad_prob = mm_cols(grad_head[here], value[:seen])
                delta = jnp.sum(probability * grad_prob, axis=-1, keepdims=True)
                grad_scores = (probability * (grad_prob - delta)).astype(BF16)
                query_parts.append(mm(grad_scores, key[:seen]) * SCALE)
                from_keys = mm_rows(grad_scores, query[here])
                from_values = mm_rows(probability.astype(BF16), grad_head[here])
                for u in range(t + 1):
                    block = slice(u * tile, (u + 1) * tile)
                    key_parts[u] = key_parts[u] + from_keys[block]
                    value_parts[u] = value_parts[u] + from_values[block]
            grad_queries.append(jnp.concatenate(query_parts, axis=0))
        grad_keys.append(jnp.concatenate(key_parts, axis=0) * SCALE)
        grad_values.append(jnp.concatenate(value_parts, axis=0))
    grad_turned = jnp.concatenate(grad_queries + grad_keys, axis=1)
    raw_ref[0, :, :turned] = half_turn(grad_turned, cosine, -sine).astype(BF16)
    raw_ref[0, :, turned:] = jnp.concatenate(grad_values, axis=1).astype(BF16)
    total = mm_cols(raw_ref[0], weight)

    @pl.when(pl.program_id(0) == 0)
    def _():
        first_ref[...] = total

    @pl.when(pl.program_id(0) > 0)
    def _():
        first_ref[...] += total


def attention_back(normed, weights, outputs, grad, cosine, sine, q_width, k_width):
    parts, model_width, width = weights.shape
    rows = normed.shape[0]

    def fixed(array):
        return pl.BlockSpec(array.shape, lambda i: (0, 0))

    def stacked(array):
        return pl.BlockSpec((1,) + array.shape[1:], lambda i: (i, 0, 0))

    raw = jax.ShapeDtypeStruct((parts, rows, width), BF16)
    return pl.pallas_call(
        functools.partial(attention_kernel, q_width, k_width),
        grid=(parts,),
        in_specs=[
            fixed(normed),
            stacked(weights),
            stacked(outputs),
            fixed(grad),
            fixed(cosine),
            fixed(sine),
        ],
        out_specs=[stacked(raw), pl.BlockSpec((rows, model_width), lambda i: (0, 0))],
        out_shape=[raw, jax.ShapeDtypeStruct((rows, model_width), F32)],
        compiler_params=pltpu.CompilerParams(vmem_limit_bytes=24 * 1024 * 1024),
        cost_estimate=pl.CostEstimate(
            flops=parts * 6 * rows * model_width * width,
            bytes_accessed=parts * 2 * model_width * width + 8 * rows * model_width,
            transcendentals=parts * rows * rows * 4,
        ),
        name="attention",
    )(normed, weights, outputs, grad, cosine, sine)


def tied(*arrays):
    return lax.optimization_barrier(arrays)


def norm_scale(field):
    return lax.rsqrt(jnp.mean(field * field, axis=-1, keepdims=True) + EPS)


def route(normed, router, chosen):
    logits = mm(normed, router)
    masked = jnp.where(chosen, logits, NEGATIVE)
    highest = jnp.max(masked, axis=-1, keepdims=True)
    expanded = jnp.where(chosen, jnp.exp(masked - highest), 0.0)
    return expanded / jnp.sum(expanded, axis=-1, keepdims=True)


def local(
    tokens,
    norm1_gain,
    w_query,
    key_projection_weight,
    value_projection_weight,
    w_output,
    norm2_gain,
    w_router,
    expert_gate_weight,
    expert_up_weight,
    expert_down_weight,
    expert_ids,
    cotangent,
):
    tok_count = tokens.shape[0]
    model_width = tokens.shape[1]
    experts, top_count = w_router.shape[1], expert_ids.shape[1]
    here, units = expert_gate_weight.shape[0], expert_gate_weight.shape[2]
    heads_query = w_query.shape[1] // HEAD_DIMENSION
    heads_kv = key_projection_weight.shape[1] // HEAD_DIMENSION
    group_size = heads_query // heads_kv
    cosine, sine_table = tables(tok_count)
    expert_count = lax.axis_size("expert")
    tensor_count = lax.axis_size("tensor")
    expert_place = lax.axis_index("expert")
    tensor_place = lax.axis_index("tensor")
    core = expert_place % 2
    own_rows = tok_count // tensor_count
    col_width = model_width // tensor_count

    names_wide = jnp.pad(expert_ids.astype(BF16), ((0, 0), (0, LANES - top_count)))
    grad_blocks = plane_gather(jnp.concatenate([cotangent, names_wide], axis=1))
    if expert_count == 8:
        grad_blocks, grad_far = grad_blocks[:3], grad_blocks[3:]

    half = w_output.shape[0] // 2
    w_halves = [z_shift(piece(w_output, core, half), step) for step in range(1, tensor_count)]
    expert_weights = [expert_gate_weight, expert_up_weight, expert_down_weight]
    w_halves = jnp.stack(w_halves)
    w_others = swap(w_halves, 1)
    w_parts = jnp.where(
        core == 0,
        jnp.concatenate([w_halves, w_others], axis=1),
        jnp.concatenate([w_others, w_halves], axis=1),
    )

    q_width, k_width = w_query.shape[1], key_projection_weight.shape[1]
    replicated = expert_count == 8 and k_width % LANES == 0
    resid_in = tokens.astype(F32)
    first_scale = norm_scale(resid_in)
    if replicated:
        wide_cosine = jnp.concatenate([cosine[:, 0]] * (LANES // 32), axis=1)
        signed = jnp.concatenate([-sine_table[:, 0], sine_table[:, 0]], axis=1)
        wide_sine = jnp.concatenate([signed] * (LANES // HEAD_DIMENSION), axis=1)
        first_norm, attended = attention_forward(
            tokens,
            norm1_gain,
            w_query,
            key_projection_weight,
            value_projection_weight,
            wide_cosine,
            wide_sine,
        )
    else:
        first_norm = (resid_in * first_scale * norm1_gain).astype(BF16)
        query_raw = mm(first_norm, w_query).reshape(tok_count, heads_query, HEAD_DIMENSION)
        key_raw = mm(first_norm, key_projection_weight).reshape(tok_count, heads_kv, HEAD_DIMENSION)
        query_rows = (
            rotate(query_raw, cosine, sine_table, 1.0)
            .astype(BF16)
            .reshape(tok_count, heads_kv, group_size, HEAD_DIMENSION)
        )
        rotated_keys = rotate(key_raw, cosine, sine_table, 1.0).astype(BF16)
        value_rows = (
            mm(first_norm, value_projection_weight)
            .astype(BF16)
            .reshape(tok_count, heads_kv, HEAD_DIMENSION)
        )
        attended, log_total = attend_forward(query_rows, rotated_keys, value_rows)
        attended = attended.reshape(tok_count, heads_query * HEAD_DIMENSION)

    attended_parts = z_received(attended)

    if expert_count == 8:
        attended_parts, grad_far = tied(attended_parts, grad_far)
    tokens, attended_parts, expert_weights, w_parts, w_router, qkv_weights = tied(
        tokens,
        attended_parts,
        expert_weights,
        w_parts,
        w_router,
        (w_query, key_projection_weight, value_projection_weight),
    )
    other_weights = [swap(weight, 1) for weight in expert_weights]
    resid_in = tokens.astype(F32)
    first_scale = norm_scale(resid_in)
    attended = attended_parts[0]

    hidden = resid_in + mm(attended, w_output)
    for step in range(1, tensor_count):
        hidden = hidden + mm(attended_parts[step], w_parts[step - 1])
    second_scale = norm_scale(hidden)
    second_norm = (hidden * second_scale * norm2_gain).astype(BF16)

    local_names = jnp.concatenate(
        [
            expert_place * here + jnp.arange(here, dtype=jnp.int32),
            (expert_place ^ 1) * here + jnp.arange(here, dtype=jnp.int32),
        ]
    )
    router_wide = jnp.pad(w_router, ((0, 0), (0, LANES - experts)))
    if expert_count == 8:
        grad_blocks = grad_blocks + grad_far

    def through_experts(normed, grad):
        return expert_block(
            local_names,
            normed,
            grad,
            router_wide,
            expert_weights + other_weights,
            experts,
            top_count,
        )

    if replicated:
        own_weight = jnp.concatenate(qkv_weights, axis=1)
        qkv_half = piece(own_weight, core, model_width // 2)
        other_weights, qkv_half = tied(other_weights, qkv_half)
        qkv_halves = [z_shift(qkv_half, step) for step in range(1, tensor_count)]
    if expert_count == 8:
        half = tok_count // 2
        from_x, from_y = swap(second_norm, 2), swap(second_norm, 4)
        own_done = through_experts(second_norm, grad_blocks[0])
        from_x, from_y, own_done = tied(from_x, from_y, own_done)
        normed_blocks = [
            second_norm, from_x, from_y, swap(from_x[:half], 4), swap(from_y[half:], 2)
        ]
        if replicated:
            own_done, qkv_halves = tied(own_done, qkv_halves)
            qkv_halves = jnp.stack(qkv_halves)
            qkv_others = swap(qkv_halves, 1)
            qkv_parts = jnp.where(
                core == 0,
                jnp.concatenate([qkv_halves, qkv_others], axis=1),
                jnp.concatenate([qkv_others, qkv_halves], axis=1),
            )
        done = [own_done]
    else:
        normed_blocks = plane_gather(second_norm)
        done = []
    if expert_count == 8:
        done.append(through_experts(normed_blocks[1], grad_blocks[1]))
        far_done = [through_experts(normed_blocks[i], grad_blocks[i]) for i in (3, 4)]
        normed_blocks[2], far_done = tied(normed_blocks[2], far_done)
        done.append(through_experts(normed_blocks[2], grad_blocks[2]))
        done += far_done
    else:
        done = [through_experts(normed, grad) for normed, grad in zip(normed_blocks, grad_blocks)]
    plane_rows, merged = plane_scatter([block[1] for block in done])
    plane_rows, *out_blocks = tied(plane_rows, *[block[0] for block in done])
    gate_grads, merged = tied([block[2] for block in done], merged)
    up_grads, plane_rows = tied([block[3] for block in done], plane_rows)
    inners = [block[4] for block in done]
    row_sum = z_scatter(plane_rows)
    out_far = plane_scatter_far(out_blocks)
    row_sum, out_far, inners = tied(row_sum, out_far, inners)
    gate_total = up_total = down_total = 0.0
    for normed, grad, gate_grad, up_grad, inner in zip(
        normed_blocks, grad_blocks, gate_grads, up_grads, inners
    ):
        gate_total = gate_total + mm_rows(normed, gate_grad)
        up_total = up_total + mm_rows(normed, up_grad)
        down_total = down_total + mm_rows(inner, grad[:, :model_width])
    plane_out, _ = plane_scatter(out_blocks, out_far)

    my_routing_grad = (
        row_sum[:, model_width : model_width + experts]
        + row_sum[:, model_width + experts : model_width + 2 * experts]
    )
    row_sum = row_sum[:, :model_width]

    def mine(array):
        return piece(array, tensor_place, own_rows)

    my_hidden, my_scale = mine(hidden), mine(second_scale)
    my_normed = mine(second_norm)
    names = jnp.arange(experts, dtype=jnp.int32)
    my_chosen = jnp.any(mine(expert_ids)[:, :, None] == names[None, None, :], axis=1)
    my_routing = route(my_normed, w_router, my_chosen)
    my_normed = my_normed.astype(F32)
    my_logits = my_routing * (
        my_routing_grad - jnp.sum(my_routing * my_routing_grad, axis=-1, keepdims=True)
    )
    router_float = w_router.astype(F32)
    grad_second = row_sum + jnp.dot(my_logits, router_float.T, precision=EXACT)
    grad_router = lax.dot_general(
        my_logits, my_normed, (((0,), (0,)), ((), ())), precision=EXACT
    )
    grad_norm2 = jnp.sum(grad_second * my_hidden * my_scale, axis=0)
    gained_two = grad_second * norm2_gain
    my_grad_hidden = (
        mine(cotangent).astype(F32)
        + my_scale * gained_two
        - my_hidden * my_scale**3 * jnp.mean(gained_two * my_hidden, axis=-1, keepdims=True)
    )
    small = jnp.concatenate([grad_router, grad_norm2[None]])
    extra = -small.shape[0] % 16
    small = jnp.pad(small, ((0, extra), (0, 0))).astype(BF16)
    parts = z_received(jnp.concatenate([my_grad_hidden.astype(BF16), small]))
    plane_out, down_total, gate_total, *parts = tied(plane_out, down_total, gate_total, *parts)
    routed = piece(hidden, tensor_place, col_width, 1) + piece(
        plane_out, tensor_place, col_width, 1
    )
    out_pieces = [
        piece(plane_out, (tensor_place + step) % tensor_count, col_width, 1).astype(BF16)
        for step in range(1, tensor_count)
    ]
    grad_branch = z_place([part[:own_rows] for part in parts])
    small = sum(part[own_rows:].astype(F32) for part in parts)
    grad_output = mm_rows(attended, grad_branch)

    if replicated:
        grad_raw, grad_first = attention_back(
            first_norm,
            own_weight[None],
            w_output[None],
            grad_branch,
            wide_cosine,
            wide_sine,
            q_width,
            k_width,
        )
        grad_raw = grad_raw[0]
        norm1_part = jnp.sum(grad_first * resid_in * first_scale, axis=0)[None]
    else:
        grad_heads = mm_cols(grad_branch, w_output).astype(BF16)
        grad_heads = grad_heads.reshape(tok_count, heads_kv, group_size, HEAD_DIMENSION)
        grad_queries, grad_keys, grad_values = attend_backward(
            query_rows, rotated_keys, value_rows, grad_heads, log_total
        )
        grad_query_raw = rotate(
            grad_queries.reshape(tok_count, heads_query, HEAD_DIMENSION), cosine, sine_table, -1.0
        )
        grad_query_raw = grad_query_raw.reshape(tok_count, -1).astype(BF16)
        grad_key_raw = rotate(grad_keys, cosine, sine_table, -1.0)
        grad_key_raw = grad_key_raw.reshape(tok_count, -1).astype(BF16)
        grad_value_raw = grad_values.reshape(tok_count, -1).astype(BF16)
        grad_raw = jnp.concatenate([grad_query_raw, grad_key_raw, grad_value_raw], axis=1)
        grad_first = (
            mm_cols(grad_query_raw, w_query)
            + mm_cols(grad_key_raw, key_projection_weight)
            + mm_cols(grad_value_raw, value_projection_weight)
        )
        norm1_part = jnp.sum(grad_first * resid_in * first_scale, axis=0)[None]

    grad_raw = mm_rows(first_norm, grad_raw)
    raw_width = grad_raw.shape[1]

    def folded(array):
        array = jnp.pad(array.astype(BF16), ((0, -array.shape[0] % 16), (0, 0)))
        return [array[:, i : i + raw_width] for i in range(0, model_width, raw_width)]

    pile = [grad_raw.astype(BF16)] + folded(grad_output) + folded(small)
    norm1_part = jnp.pad(norm1_part.reshape(-1, raw_width), ((0, 16 - model_width // raw_width), (0, 0)))
    norm1_part = sum(z_received(norm1_part))
    places = [0]
    for part in pile:
        places.append(places[-1] + part.shape[0])
    extra = -places[-1] % 128
    pile = jnp.concatenate(pile + [jnp.zeros((extra, raw_width), BF16)])
    pile, branch_zero = tied(pile, grad_branch)
    out_received = [z_shift(out_pieces[0], 1)]
    pile, late, after_first, after_second = expert_sum(
        pile,
        norm1_part,
        (grad_branch, out_pieces[1:2], up_total),
        (grad_branch, out_pieces[2:], down_total),
    )
    branch_first, out_first, up_total = after_first
    branch_second, out_second, down_total = after_second
    branch_first, norm1_part = tied(branch_first, norm1_part)
    out_received += [z_shift(sent, step + 2) for step, sent in enumerate(out_first + out_second)]
    for part in out_received:
        routed = routed + part.astype(F32)
    mixed = routed.astype(BF16)

    width = here * units

    def from_chip(total):
        return total[:, :width] + swap(total[:, width:].astype(BF16), 1).astype(F32)

    def as_experts(total):
        return total.reshape(model_width, here, units).transpose(1, 0, 2)

    grad_gate = as_experts(from_chip(gate_total))
    up_weight_gradient = as_experts(from_chip(up_total))
    grad_down = down_total[:width] + swap(down_total[width:].astype(BF16), 1).astype(F32)
    grad_down = grad_down.reshape(here, units, model_width)
    grad_weights = pile[: places[1]]
    folds = model_width // raw_width

    def unfolded(first, rows):
        return jnp.concatenate(
            [pile[places[i] : places[i] + rows] for i in range(first, first + folds)], axis=1
        )

    grad_output = unfolded(1, grad_output.shape[0])
    small = unfolded(1 + folds, experts + 1)
    grad_norm1 = late[:folds].reshape(-1)

    def first_norm_back(grad_first, grad_hidden, resid, scale):
        gained = grad_first * norm1_gain
        return (
            grad_hidden
            + scale * gained
            - resid * scale**3 * jnp.mean(gained * resid, axis=-1, keepdims=True)
        )

    if replicated:
        branches = [branch_zero, branch_first] + [branch_second] * (tensor_count - 3)
        for step, branch in enumerate(branches[: tensor_count - 1]):
            _, part_first = attention_back(
                first_norm,
                qkv_parts[step][None],
                w_parts[step][None],
                branch,
                wide_cosine,
                wide_sine,
                q_width,
                k_width,
            )
            grad_first = grad_first + part_first
        grad_input = first_norm_back(
            grad_first, grad_branch.astype(F32), resid_in, first_scale
        )
    else:
        my_grad_input = first_norm_back(
            z_scatter(grad_first), my_grad_hidden, mine(resid_in), mine(first_scale)
        )
        grad_input = z_place(z_received(my_grad_input.astype(BF16))).astype(F32)

    return (
        mixed,
        grad_input,
        grad_norm1,
        grad_weights[:, :q_width],
        grad_weights[:, q_width : q_width + k_width],
        grad_weights[:, q_width + k_width :],
        grad_output,
        small[experts],
        small[:experts].T,
        grad_gate,
        up_weight_gradient,
        grad_down,
    )


def solution(mesh):
    placed = (
        P("expert", None),
        P(),
        P(None, "tensor"),
        P(None, "tensor"),
        P(None, "tensor"),
        P("tensor", None),
        P(),
        P(),
        P("expert", None, "tensor"),
        P("expert", None, "tensor"),
        P("expert", "tensor", None),
        P("expert", None),
        P("expert", None),
    )
    return jax.shard_map(
        local,
        mesh=mesh,
        in_specs=placed,
        out_specs=(
            P("expert", "tensor"),
            P("expert", None),
            P(),
            P(None, "tensor"),
            P(None, "tensor"),
            P(None, "tensor"),
            P("tensor", None),
            P(),
            P(),
            P("expert", None, "tensor"),
            P("expert", None, "tensor"),
            P("expert", "tensor", None),
        ),
        check_vma=False,
    )
```
